32 devices in a mesh: dp: 2 (over y), seq: 16 (over z, x, core).
Axes of the slice: x: 2, y: 2, z: 4, core: 2. Of those that a mesh axis runs over, the one named last changes fastest.
Arguments:
- queries: bfloat16 [4096, 3072], P('seq', 'dp'), may hold values from -6 to 6
- keys: bfloat16 [4096, 3072], P('seq', 'dp'), may hold values from -6 to 6
- values: bfloat16 [4096, 3072], P('seq', 'dp'), may hold values from -6 to 6
- out_grad: bfloat16 [4096, 3072], P('seq', 'dp'), may hold values from -6 to 6
- log_decay: float32 [4096, 24], P('seq', 'dp'), may hold values from -0.61 to 0
- norm_gain: float32 [3072], P('dp'), may hold values from 0.1 to 1.9
- doc_ids: int32 [32], P('seq'), may hold values from 0 to 3, never falling along the last dimension, each value on 1 to 16 neighbouring positions
Outputs:
- key_grad: bfloat16 [4096, 3072], P('seq', 'dp')
- value_grad: bfloat16 [4096, 3072], P('seq', 'dp')
- gain_grad: float32 [3072], P('dp')
The draws below stay inside these ranges and needn't reach their ends.
Inputs may be any that keep to these rules, and one draw needn't show every extreme that they name: `doc_ids`: document numbers never fall along the sequence; every number from 0 to 3 occurs.
All inputs are finite; a program needn't handle non-finite values.
Results may differ from the reference program's by a relative error of at most 0.0052.
Values sent between devices are 32-bit elements; how exact they have to be, the bound alone decides.
No kernel may reach another device: no remote copies, remote signals or barrier semaphores. Data moves between devices by JAX's collectives and lax.ppermute only.
A program may use at most 64 MiB of HBM per device.

```python
import math
import jax
import jax.numpy as jnp
import numpy as np
from jax import lax

H = 24
C = 128
DOCS = 4
SEQUENCE_LENGTH = 4096
NBLK = 32
F = 3072


def draw_log_decay(key, part):
    sequence_rows = jax.random.split(jax.random.fold_in(key, 71), 7)
    order = jax.random.permutation(sequence_rows[0], H)
    fast_count = H // 2
    fast_heads = order < fast_count
    slow_total = jnp.exp(jax.random.uniform(sequence_rows[1], (1, 1, H), jnp.float32, jnp.log(0.05), jnp.log(0.5)))
    slow_rate = slow_total / SEQUENCE_LENGTH
    fast_rate = jnp.exp(jax.random.uniform(sequence_rows[2], (1, 1, H), jnp.float32, jnp.log(1.0 / 50.0), jnp.log(1.0 / 30.0)))
    base_rate = jnp.where(fast_heads[None, None, :], fast_rate, slow_rate)
    block_count = SEQUENCE_LENGTH // C
    block_factor = jnp.exp(jax.random.uniform(sequence_rows[3], (1, block_count, 1, H), jnp.float32, jnp.log(0.5), jnp.log(2.0)))
    block_factor = jnp.broadcast_to(block_factor, (1, block_count, C, H)).reshape(1, SEQUENCE_LENGTH, H)
    roughness = jnp.exp(jax.random.uniform(sequence_rows[4], (1, SEQUENCE_LENGTH, H), jnp.float32, jnp.log(0.7), jnp.log(1.4)))
    reset_probability = base_rate * block_factor * roughness
    reset_positions = jax.random.randint(sequence_rows[5], (1, 3), 0, SEQUENCE_LENGTH)
    token_positions = jnp.arange(SEQUENCE_LENGTH)
    reset_hits = jnp.any(token_positions[None, :, None] == reset_positions[:, None, :], axis=2)
    keep_fraction = jax.random.uniform(sequence_rows[6], (1, SEQUENCE_LENGTH, 1), jnp.float32, 0.6, 0.8)
    reset_flags = jnp.where(reset_hits[:, :, None], jnp.log(keep_fraction), 0.0)
    return (reset_flags - reset_probability).astype(jnp.float32)[0]


def block_levels(own_key, shape, cuts, smallest, top_value):
    def one(position, shards_of):
        heights = jax.random.uniform(jax.random.fold_in(jax.random.fold_in(own_key, 6), position), (shards_of,), jnp.float32, smallest / len(cuts), top_value / len(cuts))
        return jnp.repeat(jnp.exp(heights), shape[position] // shards_of).reshape((-1,) + (1,) * (len(shape) - position - 1))

    factor_of = one(*cuts[0])
    for cut in cuts[1:]:
        factor_of = factor_of * one(*cut)
    return factor_of


def length_profile(amount, total, bound, lean):
    weights = [(1 << 20) // math.isqrt(standing ** lean) + 1 for standing in range(2, amount + 1)]
    rest, counts = total - bound - (amount - 1), [1] * (amount - 1)
    while rest > 0:
        candidates = [i for i in range(amount - 1) if counts[i] < bound]
        pool, left = sum([weights[i] for i in candidates]), rest
        for i in candidates:
            more = min(bound - counts[i], max(1, left * weights[i] // pool), rest)
            counts[i] = counts[i] + more
            rest = rest - more
    return np.array([bound] + counts)


def uneven_parts(stream_key, number_of, total, limit, lean):
    if number_of == 2:
        one = jax.random.randint(stream_key, (), max(1, total - limit), min(limit, total - 1) + 1)
        return jnp.stack([one, total - one])
    sizes = jnp.asarray(length_profile(number_of, total, limit, lean), jnp.int32)
    pairs = (number_of - 1) // 2
    giver, receiver = sizes[1:1 + 2 * pairs:2], sizes[2:2 + 2 * pairs:2]
    slack = jnp.minimum(giver - 1, limit - receiver)
    passed = jax.random.randint(jax.random.fold_in(stream_key, 1), (pairs,), 0, 1 << 20) % (slack + 1)
    sizes = sizes.at[1:1 + 2 * pairs:2].set(giver - passed).at[2:2 + 2 * pairs:2].set(receiver + passed)
    return sizes[jax.random.permutation(jax.random.fold_in(stream_key, 2), number_of)]


def normal_values(rng, extent, spread, reach, cuts=(), kind=jnp.bfloat16):
    values = spread * jax.random.normal(rng, extent, jnp.float32)
    if cuts:
        values = values * block_levels(rng, extent, cuts, -0.22, 0.18)
    return jnp.clip(values, -reach, reach).astype(kind)


def setup_inputs(seed: int = 0) -> dict:
    arg_keys = jax.random.split(jax.random.key(seed), 8)
    queries = normal_values(arg_keys[0], (SEQUENCE_LENGTH, F), 1.0, 6.0, ((0, 16), (1, 2)))
    keys = normal_values(arg_keys[1], (SEQUENCE_LENGTH, F), 1.0, 6.0, ((0, 16), (1, 2)))
    values = normal_values(arg_keys[2], (SEQUENCE_LENGTH, F), 1.0, 6.0, ((0, 16), (1, 2)))
    out_grad = normal_values(arg_keys[3], (SEQUENCE_LENGTH, F), 1.0, 6.0, ((0, 16), (1, 2)))
    log_decay = draw_log_decay(jax.random.fold_in(arg_keys[7], 71), 0)
    norm_gain = jnp.clip(1.0 + 0.18 * jax.random.normal(arg_keys[5], (F,), jnp.float32), 0.1, 1.9)
    doc_ids = jnp.searchsorted(jnp.cumsum(uneven_parts(arg_keys[6], DOCS, NBLK, NBLK // 2, 0)), jnp.arange(NBLK), side="right").astype(jnp.int32)
    return {"queries": queries, "keys": keys, "values": values, "out_grad": out_grad, "log_decay": log_decay, "norm_gain": norm_gain, "doc_ids": doc_ids}


EPSILON = 1e-06

def block_setup(log_block, length):
    cumulative = jnp.cumsum(log_block, axis=1)
    block_total = cumulative[:, -1, :]
    causal = (jnp.arange(length)[:, None] >= jnp.arange(length)[None, :]).astype(jnp.float32)
    log_gap = jnp.swapaxes(cumulative, 1, 2)
    decay_mask = jnp.exp(jnp.minimum(log_gap[..., :, None] - log_gap[..., None, :], 0.0)) * causal
    end_decay = jnp.exp(block_total[:, None, :] - cumulative)
    return (cumulative, block_total, decay_mask, end_decay)

def block_weights(query_blk, key_blk, decay_mask):
    scores = jnp.einsum('bthd,bshd->bhts', query_blk.astype(jnp.float32), key_blk.astype(jnp.float32))
    return (scores * decay_mask).astype(jnp.bfloat16)

def reference(queries, keys, values, out_grad, log_decay, norm_gain, doc_ids):
    queries = queries[None]
    keys = keys[None]
    values = values[None]
    out_grad = out_grad[None]
    log_decay = log_decay[None]
    doc_ids = doc_ids[None]
    batch, length, features = queries.shape
    head_count = log_decay.shape[2]
    head_width = features // head_count
    block_count = length // C

    def to_blocks(array):
        shaped = array.reshape((batch, block_count, C) + array.shape[2:])
        return jnp.swapaxes(shaped, 0, 1)

    def split_heads(array):
        return to_blocks(array.reshape(batch, length, head_count, head_width))
    query_all = split_heads(queries)
    key_all = split_heads(keys)
    value_all = split_heads(values)
    cot_all = split_heads(out_grad)
    decay_all = to_blocks(log_decay)
    previous = jnp.concatenate([jnp.full((batch, 1), -1, jnp.int32), doc_ids[:, :-1].astype(jnp.int32)], axis=1)
    carried_all = (previous == doc_ids.astype(jnp.int32)).astype(jnp.float32).T

    def forward_step(carry_pair, block_item):
        state, gain_acc = carry_pair
        query_blk, key_blk, value_blk, cot_blk, log_block, carried = block_item
        cumulative, block_total, decay_mask, end_decay = block_setup(log_block, query_blk.shape[1])
        weights = block_weights(query_blk, key_blk, decay_mask)
        local_out = jnp.einsum('bhts,bshd->bthd', weights.astype(jnp.float32), value_blk.astype(jnp.float32))
        query_scaled = query_blk.astype(jnp.float32) * (jnp.exp(cumulative) * carried[:, None, None])[..., None]
        far_out = jnp.einsum('bthd,bhde->bthe', query_scaled, state, precision=lax.Precision.HIGHEST)
        attention = (local_out + far_out).reshape(query_blk.shape[0], query_blk.shape[1], -1)
        inverse = lax.rsqrt(lax.optimization_barrier(jnp.mean(attention * attention, axis=2, keepdims=True)) + EPSILON)
        out_cot = cot_blk.astype(jnp.float32).reshape(attention.shape)
        weighted = out_cot * norm_gain
        inner = lax.optimization_barrier(jnp.mean(weighted * attention, axis=2, keepdims=True))
        attn_grad = ((weighted - attention * inner * inverse * inverse) * inverse).astype(jnp.bfloat16)
        gain_acc = gain_acc + lax.optimization_barrier(jnp.sum(out_cot * attention * inverse, axis=(0, 1)))
        key_scaled = (key_blk.astype(jnp.float32) * end_decay[..., None]).astype(jnp.bfloat16)
        update = jnp.einsum('bshd,bshe->bhde', key_scaled.astype(jnp.float32), value_blk.astype(jnp.float32))
        factor = carried[:, None] * jnp.exp(block_total)
        state = factor[..., None, None] * state + update
        return ((state, gain_acc), attn_grad.reshape(query_blk.shape))
    start_state = jnp.zeros((batch, head_count, head_width, head_width), jnp.float32)
    start_gain = jnp.zeros((features,), jnp.float32)
    (final_state, gain_grad), grad_all = lax.scan(forward_step, (start_state, start_gain), (query_all, key_all, value_all, cot_all, decay_all, carried_all))

    def backward_step(later_grad, block_item):
        query_blk, key_blk, value_blk, grad_blk, log_block, carried = block_item
        cumulative, block_total, decay_mask, end_decay = block_setup(log_block, query_blk.shape[1])
        weights = block_weights(query_blk, key_blk, decay_mask)
        value_local = jnp.einsum('bhts,bthd->bshd', weights.astype(jnp.float32), grad_blk.astype(jnp.float32))
        grad_dot = jnp.einsum('bthd,bshd->bhts', grad_blk.astype(jnp.float32), value_blk.astype(jnp.float32))
        grad_weights = (grad_dot * decay_mask).astype(jnp.bfloat16)
        key_local = jnp.einsum('bhts,bthd->bshd', grad_weights.astype(jnp.float32), query_blk.astype(jnp.float32))
        key_far = jnp.einsum('bshe,bhde->bshd', value_blk.astype(jnp.float32) * end_decay[..., None], later_grad, precision=lax.Precision.HIGHEST)
        value_far = jnp.einsum('bshd,bhde->bshe', key_blk.astype(jnp.float32) * end_decay[..., None], later_grad, precision=lax.Precision.HIGHEST)
        query_weighted = (query_blk.astype(jnp.float32) * jnp.exp(cumulative)[..., None]).astype(jnp.bfloat16)
        back_term = jnp.einsum('bthd,bthe->bhde', query_weighted.astype(jnp.float32), grad_blk.astype(jnp.float32))
        back_term = back_term * carried[:, None, None, None]
        factor = carried[:, None] * jnp.exp(block_total)
        later_grad = back_term + factor[..., None, None] * later_grad
        return (later_grad, ((key_local + key_far).astype(jnp.bfloat16), (value_local + value_far).astype(jnp.bfloat16)))
    final_grad, (key_blocks, value_blocks) = lax.scan(backward_step, start_state, (query_all, key_all, value_all, grad_all, decay_all, carried_all), reverse=True)

    def from_blocks(array):
        return jnp.swapaxes(array, 0, 1).reshape(batch, length, features)
    return (from_blocks(key_blocks)[0], from_blocks(value_blocks)[0], gain_grad)
```

```python
import functools

import jax
import jax.numpy as jnp
from jax import lax
from jax.experimental import pallas as pl
from jax.experimental.pallas import tpu as pltpu
from jax.sharding import PartitionSpec as P

C = 128
EPSILON = 1e-06
PLANE = 4
F32 = jnp.float32
BF16 = jnp.bfloat16
HIGHEST = lax.Precision.HIGHEST


def dot(a, b, contract_a, contract_b, precision=None):
    return lax.dot_general(
        a,
        b,
        (((contract_a,), (contract_b,)), ((), ())),
        precision=precision,
        preferred_element_type=F32,
    )


def two_parts(a):
    high = a.astype(BF16)
    return high, (a - high.astype(F32)).astype(BF16)


def far_dot(a, state, contract_state):
    high, low = two_parts(state)
    return dot(a, high, 1, contract_state) + dot(a, low, 1, contract_state)


def equal(a, b):
    return (a == b).astype(F32)


def place_bits(count, reverse):
    place = lax.axis_index("seq")
    place = count - 1 - place if reverse else place
    return lax.rem(place, 2), lax.rem(place // 2, 2), place // PLANE


def triangle():
    row = lax.broadcasted_iota(jnp.int32, (C, C), 0)
    column = lax.broadcasted_iota(jnp.int32, (C, C), 1)
    return row, column


def decay_columns(log_block):
    row, column = triangle()
    return dot((row >= column).astype(F32), log_block, 1, 0, HIGHEST)


def decay_rows(log_block):
    row, column = triangle()
    return dot(log_block, (row <= column).astype(F32), 0, 0, HIGHEST)


def total_rows(log_block):
    return dot(log_block, jnp.ones((C, C), F32), 0, 0, HIGHEST)


class Sizes:
    def __init__(self, tokens, features, heads, count):
        self.tokens, self.features, self.heads, self.count = tokens, features, heads, count
        self.blocks = tokens // C
        self.width = features // heads
        self.half = self.width // 2
        self.quarter = self.width // 4
        self.planes = count // PLANE
        longest = self.blocks * count // 2
        per_plane = self.blocks * PLANE
        self.window = max(1, min(self.planes - 1, 1 + (longest - 2) // per_plane))
        self.tail = -(-(2 * heads + 2) // 8) * 8
        self.start, self.end, self.gain = heads, heads + 1, heads + 2

    def head(self, h):
        return slice(h * self.width, (h + 1) * self.width)

    def block(self, j):
        return slice(j * C, (j + 1) * C)

    def rows(self, h, size):
        return slice(h * size, (h + 1) * size)

    def carry(self, j):
        return 2 * self.heads + 2 + j


def call(kernel, outs, *args, flops=0, name=None):
    moved = sum(a.size * a.dtype.itemsize for a in args) + sum(
        o.size * o.dtype.itemsize for o in outs
    )
    return pl.pallas_call(
        kernel,
        out_shape=outs,
        in_specs=[pl.BlockSpec(memory_space=pltpu.VMEM)] * len(args),
        out_specs=[pl.BlockSpec(memory_space=pltpu.VMEM)] * len(outs),
        compiler_params=pltpu.CompilerParams(vmem_limit_bytes=20 * 1024 * 1024),
        cost_estimate=pl.CostEstimate(flops=flops, bytes_accessed=moved, transcendentals=0),
        name=name,
    )(*args)


def shape(rows, columns, dtype=F32):
    return jax.ShapeDtypeStruct((rows, columns), dtype)


def put_tail(s, tail_ref, base, factors, start, end):
    tail_ref[base : base + s.heads, :] = factors
    tail_ref[base + s.start : base + s.start + 1, :] = start
    tail_ref[base + s.end : base + s.end + 1, :] = end


def put_parts(first, own, size, h, whole, keep_ref, send_ref):
    low, high = whole[:size], whole[size:]
    rows = slice(h * size, (h + 1) * size)
    keep_ref[rows, :] = lax.select(first, low, high)
    send_ref[rows, :] = lax.select(first, high, low)


def state_kernel(s, keys, values, log_decay, doc_rows, keep, send, tail, first_update):
    core, _, _ = place_bits(s.count, False)
    lower = core == 0
    docs = [doc_rows[j : j + 1, :] for j in range(s.blocks)]
    carries = [None] + [equal(docs[j - 1], docs[j]) for j in range(1, s.blocks)]
    logs = [log_decay[s.block(j), :] for j in range(s.blocks)]
    totals = [total_rows(a) for a in logs]
    factors = [jnp.exp(t) for t in totals]
    whole_factor = factors[0]
    for j in range(1, s.blocks):
        whole_factor = whole_factor * factors[j] * carries[j]
    base = s.heads * s.half
    send[base:, :] = jnp.zeros((s.tail, s.width), F32)
    put_tail(s, send, base, whole_factor, docs[0], docs[-1])
    tail[...] = jnp.zeros(tail.shape, F32)
    put_tail(s, tail, 0, whole_factor, docs[0], docs[-1])
    for j in range(1, s.blocks):
        tail[s.carry(j) : s.carry(j) + 1, :] = carries[j]
    columns = [decay_columns(a) for a in logs]
    ends = [jnp.exp(a[C - 1 : C, :] - a) for a in columns]
    for h in range(s.heads):
        state = None
        for j in range(s.blocks):
            scaled = keys[s.block(j), s.head(h)].astype(F32) * ends[j][:, h : h + 1]
            update = dot(scaled.astype(BF16), values[s.block(j), s.head(h)], 0, 0)
            if j < s.blocks - 1:
                first_update[s.rows(j * s.heads + h, s.width), :] = update
            if state is None:
                state = update
            else:
                state = (carries[j] * factors[j][h : h + 1, :]) * state + update
        put_parts(lower, None, s.half, h, state, keep, send)


def chip_kernel(s, reverse, keep, received, tail, out_keep, out_send):
    core, chip, _ = place_bits(s.count, reverse)
    lower, left = core == 0, chip == 0
    base = s.heads * s.half
    other = received[base:, :]
    own = tail[: s.tail, :]
    far, near = lax.select(lower, own, other), lax.select(lower, other, own)
    link = equal(far[s.end : s.end + 1, :], near[s.start : s.start + 1, :])
    factor = near[: s.heads, :] * link
    top = s.heads * s.quarter
    out_send[top:, :] = far + near
    put_tail(
        s,
        out_send,
        top,
        far[: s.heads, :] * factor,
        far[s.start : s.start + 1, :],
        near[s.end : s.end + 1, :],
    )
    for h in range(s.heads):
        rows = s.rows(h, s.half)
        a, b = keep[rows, :], received[rows, :]
        far_state, near_state = lax.select(lower, a, b), lax.select(lower, b, a)
        total = near_state + factor[h : h + 1, :] * far_state
        put_parts(left, None, s.quarter, h, total, out_keep, out_send)


def plane_kernel(s, reverse, keep, sent, received, out):
    _, chip, _ = place_bits(s.count, reverse)
    left = chip == 0
    top = s.heads * s.quarter
    own, other = sent[top:, :], received[top:, :]
    far, near = lax.select(left, own, other), lax.select(left, other, own)
    link = equal(far[s.end : s.end + 1, :], near[s.start : s.start + 1, :])
    factor = near[: s.heads, :] * link
    out[top:, :] = far + near
    put_tail(
        s,
        out,
        top,
        far[: s.heads, :] * factor,
        far[s.start : s.start + 1, :],
        near[s.end : s.end + 1, :],
    )
    for h in range(s.heads):
        rows = s.rows(h, s.quarter)
        a, b = keep[rows, :], received[rows, :]
        far_state, near_state = lax.select(left, a, b), lax.select(left, b, a)
        out[rows, :] = near_state + factor[h : h + 1, :] * far_state


def spread_kernel(s, reverse, keep, sent, received, *rest):
    earlier, (out_keep, out_send) = rest[:-2], rest[-2:]
    _, chip, plane = place_bits(s.count, reverse)
    left = chip == 0
    top = s.heads * s.quarter
    own, other = sent[top:, :], received[top:, :]
    far, near = lax.select(left, own, other), lax.select(left, other, own)
    start, end = slice(s.start, s.start + 1), slice(s.end, s.end + 1)
    tails = [ref[top:, :] for ref in earlier]
    reach = [(plane >= w + 1).astype(F32) for w in range(len(earlier))]
    entry = equal(tails[0][end], far[start]) * reach[0]
    inner = [
        equal(tails[w + 1][end], tails[w][start]) * reach[w + 1] * tails[w][: s.heads, :]
        for w in range(len(earlier) - 1)
    ]
    link = equal(far[end], near[start])
    far_factor = far[: s.heads, :]
    for h in range(s.heads):
        rows, one = s.rows(h, s.quarter), slice(h, h + 1)
        state = earlier[-1][rows, :]
        for w in reversed(range(len(earlier) - 1)):
            state = earlier[w][rows, :] + inner[w][one] * state
        into_far = entry * state
        far_state = lax.select(left, keep[rows, :], received[rows, :])
        into_near = link * (far_state + far_factor[one] * into_far)
        out_keep[rows, :] = lax.select(left, into_far, into_near)
        out_send[rows, :] = lax.select(left, into_near, into_far)


def entry_kernel(s, reverse, chip_keep, chip_received, keep, received, tail, out_keep, out_send):
    core, chip, _ = place_bits(s.count, reverse)
    lower, left = core == 0, chip == 0
    base = s.heads * s.half
    other = received[base:, :]
    own = tail[: s.tail, :]
    far, near = lax.select(lower, own, other), lax.select(lower, other, own)
    link = equal(far[s.end : s.end + 1, :], near[s.start : s.start + 1, :])
    far_factor = far[: s.heads, :]
    for h in range(s.heads):
        rows, quarter = s.rows(h, s.half), s.rows(h, s.quarter)
        a, b = chip_keep[quarter, :], chip_received[quarter, :]
        into_far = jnp.concatenate([lax.select(left, a, b), lax.select(left, b, a)], axis=0)
        far_state = lax.select(lower, keep[rows, :], received[rows, :])
        into_near = link * (far_state + far_factor[h : h + 1, :] * into_far)
        out_keep[rows, :] = lax.select(lower, into_far, into_near)
        out_send[rows, :] = lax.select(lower, into_near, into_far)


def joined(s, lower, keep, received, h):
    rows = s.rows(h, s.half)
    a, b = keep[rows, :], received[rows, :]
    return jnp.concatenate([lax.select(lower, a, b), lax.select(lower, b, a)], axis=0)


def decay_mask(column, row):
    at, other = triangle()
    gap = jnp.minimum(column - row, 0.0)
    return jnp.where(at >= other, jnp.exp(gap), 0.0)


def local_kernel(s, queries, keys, values, log_decay, out, weights):
    for j in range(s.blocks):
        logs = log_decay[s.block(j), :]
        columns, rows = decay_columns(logs), decay_rows(logs)
        for h in range(s.heads):
            mask = decay_mask(columns[:, h : h + 1], rows[h : h + 1, :])
            part = (s.block(j), s.head(h))
            scores = dot(queries[part], keys[part], 1, 1)
            weight = (scores * mask).astype(BF16)
            weights[s.rows(j * s.heads + h, C), :] = weight
            out[part] = dot(weight, values[part], 1, 0)


def attention_kernel(
    s, queries, out_grad, gain, log_decay, tail, local, first_update, keep, received, out, sums
):
    core, _, _ = place_bits(s.count, False)
    lower = core == 0
    logs = [log_decay[s.block(j), :] for j in range(s.blocks)]
    factors = [jnp.exp(total_rows(a)) for a in logs]
    decays = [jnp.exp(decay_columns(a)) for a in logs]
    squares = [jnp.zeros((C, s.width), F32) for _ in logs]
    inners = [jnp.zeros((C, s.width), F32) for _ in logs]
    for h in range(s.heads):
        state = joined(s, lower, keep, received, h)
        for j in range(s.blocks):
            part = (s.block(j), s.head(h))
            far = far_dot(queries[part], state, 0)
            attention = local[part] + decays[j][:, h : h + 1] * far
            out[part] = attention
            squares[j] = squares[j] + attention * attention
            inners[j] = inners[j] + out_grad[part].astype(F32) * gain[:, s.head(h)] * attention
            if j < s.blocks - 1:
                update = first_update[s.rows(j * s.heads + h, s.width), :]
                carried = tail[s.carry(j + 1) : s.carry(j + 1) + 1, :]
                state = carried * (factors[j][h : h + 1, :] * state + update)
    sums[...] = jnp.zeros(sums.shape, F32)
    for j in range(s.blocks):
        sums[0:1, s.block(j)] = jnp.sum(squares[j].T, axis=0, keepdims=True)
        sums[1:2, s.block(j)] = jnp.sum(inners[j].T, axis=0, keepdims=True)


def grad_kernel(
    s, all_features, queries, out_grad, gain, log_decay, tail, attention, sums,
    attn_grad, keep, send, out_tail, back_terms,
):
    core, _, _ = place_bits(s.count, True)
    lower = core == 0
    logs = [log_decay[s.block(j), :] for j in range(s.blocks)]
    factors = [jnp.exp(total_rows(a)) for a in logs]
    decays = [jnp.exp(decay_columns(a)) for a in logs]
    totals = sums[...] / all_features
    spread = lambda row: jnp.broadcast_to(row, (C, C)).T
    inverses, slopes = [], []
    for j in range(s.blocks):
        inverse = lax.rsqrt(totals[0:1, s.block(j)] + EPSILON)
        inverses.append(spread(inverse))
        slopes.append(spread(totals[1:2, s.block(j)] * inverse * inverse))
    base = s.heads * s.half
    out_tail[...] = jnp.zeros(out_tail.shape, F32)
    own = tail[...]
    put_tail(
        s, out_tail, 0, own[: s.heads], own[s.end : s.end + 1], own[s.start : s.start + 1]
    )
    for h in range(s.heads):
        gain_row = gain[:, s.head(h)]
        gain_part = jnp.zeros((1, s.width), F32)
        terms = []
        for j in range(s.blocks):
            part = (s.block(j), s.head(h))
            cot = out_grad[part].astype(F32)
            att = attention[part]
            grad = ((cot * gain_row - att * slopes[j]) * inverses[j]).astype(BF16)
            attn_grad[part] = grad
            gain_part = gain_part + jnp.sum(cot * att * inverses[j], axis=0, keepdims=True)
            weighted = (queries[part].astype(F32) * decays[j][:, h : h + 1]).astype(BF16)
            term = dot(weighted, grad, 0, 0)
            terms.append(term)
            if j > 0:
                back_terms[s.rows((j - 1) * s.heads + h, s.width), :] = term
        state = terms[-1]
        for j in reversed(range(s.blocks - 1)):
            carried = tail[s.carry(j + 1) : s.carry(j + 1) + 1, :]
            state = terms[j] + (carried * factors[j][h : h + 1, :]) * state
        put_parts(lower, None, s.half, h, state, keep, send)
        out_tail[s.gain + h : s.gain + h + 1, :] = gain_part
    send[base:, :] = out_tail[...]


def local_grad_kernel(s, queries, values, log_decay, weights, attn_grad, key_out, value_out):
    for j in range(s.blocks):
        logs = log_decay[s.block(j), :]
        columns, rows = decay_columns(logs), decay_rows(logs)
        for h in range(s.heads):
            mask = decay_mask(columns[:, h : h + 1], rows[h : h + 1, :])
            part = (s.block(j), s.head(h))
            grad = attn_grad[part]
            grad_weight = (dot(grad, values[part], 1, 1) * mask).astype(BF16)
            key_out[part] = dot(grad_weight, queries[part], 0, 0)
            value_out[part] = dot(weights[s.rows(j * s.heads + h, C), :], grad, 0, 0)


def final_kernel(
    s, keys, values, log_decay, tail, key_local, value_local, back_terms, keep, received,
    key_out, value_out,
):
    core, _, _ = place_bits(s.count, True)
    lower = core == 0
    logs = [log_decay[s.block(j), :] for j in range(s.blocks)]
    factors = [jnp.exp(total_rows(a)) for a in logs]
    columns = [decay_columns(a) for a in logs]
    ends = [jnp.exp(a[C - 1 : C, :] - a) for a in columns]
    for h in range(s.heads):
        state = joined(s, lower, keep, received, h)
        for j in reversed(range(s.blocks)):
            part = (s.block(j), s.head(h))
            end = ends[j][:, h : h + 1]
            key_far = end * far_dot(values[part], state, 1)
            value_far = end * far_dot(keys[part], state, 0)
            key_out[part] = (key_local[part] + key_far).astype(BF16)
            value_out[part] = (value_local[part] + value_far).astype(BF16)
            if j > 0:
                carried = tail[s.carry(j) : s.carry(j) + 1, :]
                term = back_terms[s.rows((j - 1) * s.heads + h, s.width), :]
                state = carried * (term + factors[j][h : h + 1, :] * state)


def swap(value, axis, bit):
    count = lax.axis_size(axis)
    return lax.ppermute(value, axis, [(i, i ^ bit) for i in range(count)])


def next_plane(value, count, reverse):
    step = -PLANE if reverse else PLANE
    return lax.ppermute(value, "seq", [(i, (i + step) % count) for i in range(count)])


def scan_in(s, keep, send, tail, reverse, beside):
    quarter = shape(s.heads * s.quarter, s.width)
    quarter_tail = shape(s.heads * s.quarter + s.tail, s.width)
    half = shape(s.heads * s.half, s.width)
    with_args = functools.partial
    received = swap(send, "seq", 1)
    chip_keep, chip_sent = call(
        with_args(chip_kernel, s, reverse), [quarter, quarter_tail], keep, received, tail
    )
    chip_received = swap(chip_sent, "seq", 2)
    (plane,) = call(
        with_args(plane_kernel, s, reverse), [quarter_tail], chip_keep, chip_sent, chip_received
    )
    earlier = []
    passed = plane
    for _ in range(s.window):
        passed = next_plane(passed, s.count, reverse)
        earlier.append(passed)
    plane, local = beside(plane)
    into_keep, into_sent = call(
        with_args(spread_kernel, s, reverse),
        [quarter, quarter],
        chip_keep,
        chip_sent,
        chip_received,
        *earlier,
    )
    into_received = swap(into_sent, "seq", 2)
    out_keep, out_sent = call(
        with_args(entry_kernel, s, reverse),
        [half, half],
        into_keep,
        into_received,
        keep,
        received,
        tail,
    )
    out_received = swap(out_sent, "seq", 1)
    return out_keep, out_received, local, [plane] + earlier


def per_device(queries, keys, values, out_grad, log_decay, norm_gain, doc_ids):
    tokens, features = queries.shape
    heads = log_decay.shape[1]
    s = Sizes(tokens, features, heads, lax.axis_size("seq"))
    dp = lax.axis_size("dp")
    bind = functools.partial
    unit = 2 * C * C * C * s.blocks * heads
    doc_rows = jnp.broadcast_to(doc_ids.astype(F32)[:, None], (s.blocks, s.width))
    gain = norm_gain.reshape(1, features)
    half = shape(heads * s.half, s.width)
    half_tail = shape(heads * s.half + s.tail, s.width)
    rest = shape(max(1, s.blocks - 1) * heads * s.width, s.width)
    tail_rows = -(-s.carry(s.blocks) // 8) * 8
    keep, send, tail, first_update = call(
        bind(state_kernel, s),
        [half, half_tail, shape(tail_rows, s.width), rest],
        keys,
        values,
        log_decay,
        doc_rows,
        flops=unit,
    )

    def beside_forward(plane):
        local = call(
            bind(local_kernel, s),
            [shape(tokens, features), shape(s.blocks * heads * C, C, BF16)],
            queries,
            keys,
            values,
            log_decay,
            flops=2 * unit,
        )
        return plane, local

    state_keep, state_received, (local_out, weights), _ = scan_in(
        s, keep, send, tail, False, beside_forward
    )
    attention, sums = call(
        bind(attention_kernel, s),
        [shape(tokens, features), shape(8, tokens)],
        queries,
        out_grad,
        gain,
        log_decay,
        tail,
        local_out,
        first_update,
        state_keep,
        state_received,
        flops=2 * unit,
    )
    if dp & (dp - 1):
        sums = lax.psum(sums, "dp")
    else:
        bit = 1
        while bit < dp:
            sums = sums + swap(sums, "dp", bit)
            bit *= 2
    attn_grad, keep, send, back_tail, back_terms = call(
        bind(grad_kernel, s, features * dp),
        [shape(tokens, features, BF16), half, half_tail, shape(s.tail, s.width), rest],
        queries,
        out_grad,
        gain,
        log_decay,
        tail,
        attention,
        sums,
        flops=unit,
    )

    def beside_backward(plane):
        local = call(
            bind(local_grad_kernel, s),
            [shape(tokens, features), shape(tokens, features)],
            queries,
            values,
            log_decay,
            weights,
            attn_grad,
            flops=3 * unit,
        )
        return plane, local

    grad_keep, grad_received, (key_local, value_local), parts = scan_in(
        s, keep, send, back_tail, True, beside_backward
    )
    top = heads * s.quarter
    gains = [a[top + s.gain : top + s.gain + heads] for a in parts]
    while len(gains) < s.planes:
        gains.append(next_plane(gains[-1], s.count, True))
    gain_grad = sum(gains[1:], gains[0]).reshape(features)
    key_grad, value_grad = call(
        bind(final_kernel, s),
        [shape(tokens, features, BF16), shape(tokens, features, BF16)],
        keys,
        values,
        log_decay,
        tail,
        key_local,
        value_local,
        back_terms,
        grad_keep,
        grad_received,
        flops=4 * unit,
    )
    return (key_grad, value_grad, gain_grad)


def solution(mesh):
    placed = (
        P("seq", "dp"),
        P("seq", "dp"),
        P("seq", "dp"),
        P("seq", "dp"),
        P("seq", "dp"),
        P("dp"),
        P("seq"),
    )
    return jax.shard_map(
        per_device,
        mesh=mesh,
        in_specs=placed,
        out_specs=(P("seq", "dp"), P("seq", "dp"), P("dp")),
        check_vma=False,
    )
```

```python
import functools

import jax
import jax.numpy as jnp
from jax import lax
from jax.experimental import pallas as pl
from jax.experimental.pallas import tpu as pltpu
from jax.sharding import PartitionSpec as P

C = 128
EPSILON = 1e-06
PLANE = 4
WAVES = (1,)
F32 = jnp.float32
BF16 = jnp.bfloat16
HIGHEST = lax.Precision.HIGHEST


def dot(a, b, contract_a, contract_b, precision=None):
    return lax.dot_general(
        a,
        b,
        (((contract_a,), (contract_b,)), ((), ())),
        precision=precision,
        preferred_element_type=F32,
    )


def two_parts(a):
    high = a.astype(BF16)
    return high, (a - high.astype(F32)).astype(BF16)


def far_dot(a, state, contract_state):
    high, low = two_parts(state)
    return dot(a, high, 1, contract_state) + dot(a, low, 1, contract_state)


def equal(a, b):
    return (a == b).astype(F32)


def place_bits(count, reverse):
    place = lax.axis_index("seq")
    place = count - 1 - place if reverse else place
    return lax.rem(place, 2), lax.rem(place // 2, 2), place // PLANE


def triangle():
    row = lax.broadcasted_iota(jnp.int32, (C, C), 0)
    column = lax.broadcasted_iota(jnp.int32, (C, C), 1)
    return row, column


def decay_columns(log_block):
    row, column = triangle()
    return dot((row >= column).astype(F32), log_block, 1, 1, HIGHEST)


def decay_rows(log_block):
    row, column = triangle()
    return dot(log_block, (row <= column).astype(F32), 1, 0, HIGHEST)


def total_rows(log_block):
    return dot(log_block, jnp.ones((C, C), F32), 1, 0, HIGHEST)


class Sizes:
    def __init__(self, tokens, features, all_heads, count, wave, waves):
        self.tokens, self.features, self.count = tokens, features, count
        self.heads = all_heads // waves
        self.first = wave * self.heads
        self.wave = wave
        self.blocks = tokens // C
        self.width = features // all_heads
        self.half = self.width // 2
        self.quarter = self.width // 4
        self.columns = self.heads * self.width
        self.planes = count // PLANE
        longest = self.blocks * count // 2
        per_plane = self.blocks * PLANE
        self.window = max(1, min(self.planes - 1, 1 + (longest - 2) // per_plane))
        self.gains = -(-self.heads // 8) * 8
        self.tail = -(-(self.heads + 2) // 8) * 8
        self.start, self.end = self.heads, self.heads + 1
        self.notes = -(-(self.heads + 2 + self.blocks) // 8) * 8

    def own(self, h):
        return slice(h * self.width, (h + 1) * self.width)

    def head(self, h):
        return self.own(self.first + h)

    def block(self, j):
        return slice(j * C, (j + 1) * C)

    def rows(self, h, size):
        return slice(h * size, (h + 1) * size)

    def carry(self, j):
        return slice(self.heads + 2 + j, self.heads + 3 + j)

    def logs(self, log_decay):
        return [
            log_decay[self.first : self.first + self.heads, self.block(j)]
            for j in range(self.blocks)
        ]


def call(kernel, outs, *args, flops=0, spaces=None, out_spaces=None, scratch=()):
    moved = sum(a.size * a.dtype.itemsize for a in args) + sum(
        o.size * o.dtype.itemsize for o in outs
    )
    spaces = spaces or [pltpu.VMEM] * len(args)
    out_spaces = out_spaces or [pltpu.VMEM] * len(outs)
    return pl.pallas_call(
        kernel,
        out_shape=outs,
        in_specs=[pl.BlockSpec(memory_space=p) for p in spaces],
        out_specs=[pl.BlockSpec(memory_space=p) for p in out_spaces],
        compiler_params=pltpu.CompilerParams(vmem_limit_bytes=2 * moved + (3 << 20)),
        cost_estimate=pl.CostEstimate(flops=flops, bytes_accessed=moved, transcendentals=0),
        scratch_shapes=scratch,
    )(*args)


def after(token, *values):
    return lax.optimization_barrier((token,) + values)[1:]


def shape(rows, columns, dtype=F32):
    return jax.ShapeDtypeStruct((rows, columns), dtype)


def put_tail(s, tail_ref, base, factors, start, end):
    tail_ref[base : base + s.heads, :] = factors
    tail_ref[base + s.start : base + s.start + 1, :] = start
    tail_ref[base + s.end : base + s.end + 1, :] = end


def put_parts(first, size, h, whole, keep_ref, send_ref):
    low, high = whole[:size], whole[size:]
    rows = slice(h * size, (h + 1) * size)
    keep_ref[rows, :] = lax.select(first, low, high)
    send_ref[rows, :] = lax.select(first, high, low)


def state_kernel(s, keys, values, log_decay, doc_ids, keep, send, notes, first_update, *near):
    each, waits, first = s.heads, [], s.first
    if near:
        near_keys, near_values, near_logs, near_ids, arrived, small = near
        few = [
            pltpu.make_async_copy(doc_ids, near_ids, small.at[0]),
            pltpu.make_async_copy(log_decay, near_logs, small.at[1]),
        ]
        each = s.heads // arrived.shape[1]
        for g in range(arrived.shape[1]):
            far_part = pl.ds((s.first + g * each) * s.width, each * s.width)
            part = pl.ds(g * each * s.width, each * s.width)
            waits.append(
                [
                    pltpu.make_async_copy(keys.at[:, far_part], near_keys.at[:, part], arrived.at[0, g]),
                    pltpu.make_async_copy(
                        values.at[:, far_part], near_values.at[:, part], arrived.at[1, g]
                    ),
                ]
            )
        for copy in few + sum(waits, []):
            copy.start()
        for copy in few:
            copy.wait()
        keys, values, log_decay, doc_ids, first = near_keys, near_values, near_logs, near_ids, 0
    core, _, _ = place_bits(s.count, False)
    lower = core == 0
    docs = [jnp.full((1, s.width), doc_ids[j].astype(F32)) for j in range(s.blocks)]
    carries = [None] + [equal(docs[j - 1], docs[j]) for j in range(1, s.blocks)]
    logs = s.logs(log_decay)
    totals = [total_rows(a) for a in logs]
    factors = [jnp.exp(t) for t in totals]
    whole_factor = factors[0]
    for j in range(1, s.blocks):
        whole_factor = whole_factor * factors[j] * carries[j]
    base = s.heads * s.half
    send[base:, :] = jnp.zeros((s.tail, s.width), F32)
    put_tail(s, send, base, whole_factor, docs[0], docs[-1])
    notes[...] = jnp.zeros(notes.shape, F32)
    put_tail(s, notes, 0, whole_factor, docs[0], docs[-1])
    for j in range(1, s.blocks):
        notes[s.carry(j), :] = carries[j]
    columns = [decay_columns(a) for a in logs]
    ends = [jnp.exp(a[C - 1 : C, :] - a) for a in columns]
    for h in range(s.heads):
        if waits and h % each == 0:
            for copy in waits[h // each]:
                copy.wait()
        place = slice((first + h) * s.width, (first + h + 1) * s.width)
        state = None
        for j in range(s.blocks):
            scaled = keys[s.block(j), place].astype(F32) * ends[j][:, h : h + 1]
            update = dot(scaled.astype(BF16), values[s.block(j), place], 0, 0)
            if j < s.blocks - 1:
                first_update[s.rows(j * s.heads + h, s.width), :] = update
            if state is None:
                state = update
            else:
                state = (carries[j] * factors[j][h : h + 1, :]) * state + update
        put_parts(lower, s.half, h, state, keep, send)


def sides(first, own, other):
    return lax.select(first, own, other), lax.select(first, other, own)


def linked(s, far, near):
    return equal(far[s.end : s.end + 1, :], near[s.start : s.start + 1, :])


def join_tail(s, out, base, far, near, factor):
    out[base : base + s.tail, :] = jnp.zeros((s.tail, s.width), F32)
    put_tail(
        s,
        out,
        base,
        far[: s.heads, :] * factor,
        far[s.start : s.start + 1, :],
        near[s.end : s.end + 1, :],
    )


def chip_kernel(s, reverse, keep, received, own_tail, *rest):
    out_keep, out_send = rest[-2:]
    core, chip, _ = place_bits(s.count, reverse)
    lower, left = core == 0, chip == 0
    base, top = s.heads * s.half, s.heads * s.quarter
    far, near = sides(lower, own_tail[: s.tail, :], received[base : base + s.tail, :])
    factor = near[: s.heads, :] * linked(s, far, near)
    join_tail(s, out_send, top, far, near, factor)
    if reverse:
        out_send[top + s.tail :, :] = rest[0][...] + received[base + s.tail :, :]
    for h in range(s.heads):
        rows = s.rows(h, s.half)
        far_state, near_state = sides(lower, keep[rows, :], received[rows, :])
        total = near_state + factor[h : h + 1, :] * far_state
        put_parts(left, s.quarter, h, total, out_keep, out_send)


def plane_kernel(s, reverse, keep, sent, received, *rest):
    out = rest[-2] if reverse else rest[0]
    _, chip, _ = place_bits(s.count, reverse)
    left = chip == 0
    top = s.heads * s.quarter
    far, near = sides(left, sent[top:, :], received[top:, :])
    factor = near[: s.heads, :] * linked(s, far, near)
    join_tail(s, out, top, far, near, factor)
    if reverse:
        gain = sent[top + s.tail :, :] + received[top + s.tail :, :]
        out[top + s.tail :, :] = gain
        every = rest[-1]
        if len(rest) > 2:
            every[: -s.gains, :] = rest[0][...]
        every[every.shape[0] - s.gains :, :] = gain
    for h in range(s.heads):
        rows = s.rows(h, s.quarter)
        far_state, near_state = sides(left, keep[rows, :], received[rows, :])
        out[rows, :] = near_state + factor[h : h + 1, :] * far_state


def spread_kernel(s, reverse, keep, sent, received, *rest):
    out_keep, out_send = rest[-3:-1] if reverse else rest[-2:]
    earlier = rest[: s.window]
    _, chip, plane = place_bits(s.count, reverse)
    left = chip == 0
    top = s.heads * s.quarter
    far, near = sides(left, sent[top:, :], received[top:, :])
    tails = [ref[top : top + s.tail, :] for ref in earlier]
    reach = [(plane >= w + 1).astype(F32) for w in range(s.window)]
    entry = linked(s, tails[0], far) * reach[0]
    inner = [
        linked(s, tails[w + 1], tails[w]) * reach[w + 1] * tails[w][: s.heads, :]
        for w in range(s.window - 1)
    ]
    link = linked(s, far, near)
    far_factor = far[: s.heads, :]
    if reverse:
        gain = rest[s.window][top + s.tail :, :]
        for other in earlier[: s.planes - 1]:
            gain = gain + other[top + s.tail :, :]
        rest[-1][...] = gain
    for h in range(s.heads):
        rows, one = s.rows(h, s.quarter), slice(h, h + 1)
        state = earlier[-1][rows, :]
        for w in reversed(range(s.window - 1)):
            state = earlier[w][rows, :] + inner[w][one] * state
        into_far = entry * state
        far_state = lax.select(left, keep[rows, :], received[rows, :])
        into_near = link * (far_state + far_factor[one] * into_far)
        out_keep[rows, :] = lax.select(left, into_far, into_near)
        out_send[rows, :] = lax.select(left, into_near, into_far)


def entry_kernel(
    s, reverse, chip_keep, chip_received, keep, received, own_tail, out_keep, out_send
):
    core, chip, _ = place_bits(s.count, reverse)
    lower, left = core == 0, chip == 0
    base = s.heads * s.half
    far, near = sides(lower, own_tail[: s.tail, :], received[base : base + s.tail, :])
    link = linked(s, far, near)
    far_factor = far[: s.heads, :]
    for h in range(s.heads):
        rows, quarter = s.rows(h, s.half), s.rows(h, s.quarter)
        into_far = jnp.concatenate(
            sides(left, chip_keep[quarter, :], chip_received[quarter, :]), axis=0
        )
        far_state = lax.select(lower, keep[rows, :], received[rows, :])
        into_near = link * (far_state + far_factor[h : h + 1, :] * into_far)
        out_keep[rows, :] = lax.select(lower, into_far, into_near)
        out_send[rows, :] = lax.select(lower, into_near, into_far)


def joined(s, lower, keep, received, h):
    rows = s.rows(h, s.half)
    return jnp.concatenate(sides(lower, keep[rows, :], received[rows, :]), axis=0)


def decay_mask(column, row):
    at, other = triangle()
    gap = jnp.minimum(column - row, 0.0)
    return jnp.where(at >= other, jnp.exp(gap), 0.0)


def local_kernel(s, queries, keys, values, log_decay, out, weights):
    for j, logs in enumerate(s.logs(log_decay)):
        columns, rows = decay_columns(logs), decay_rows(logs)
        for h in range(s.heads):
            mask = decay_mask(columns[:, h : h + 1], rows[h : h + 1, :])
            part = (s.block(j), s.head(h))
            scores = dot(queries[part], keys[part], 1, 1)
            weight = (scores * mask).astype(BF16)
            weights[s.rows(j * s.heads + h, C), :] = weight
            out[s.block(j), s.own(h)] = dot(weight, values[part], 1, 0)


def attention_kernel(
    s, queries, out_grad, gain, log_decay, notes, local, first_update, keep, received, *rest
):
    earlier_sums, (out, sums) = rest[:-2], rest[-2:]
    core, _, _ = place_bits(s.count, False)
    lower = core == 0
    logs = s.logs(log_decay)
    factors = [jnp.exp(total_rows(a)) for a in logs]
    decays = [jnp.exp(decay_columns(a)) for a in logs]
    squares = [jnp.zeros((C, s.width), F32) for _ in logs]
    inners = [jnp.zeros((C, s.width), F32) for _ in logs]
    for h in range(s.heads):
        state = joined(s, lower, keep, received, h)
        for j in range(s.blocks):
            part, own = (s.block(j), s.head(h)), (s.block(j), s.own(h))
            far = far_dot(queries[part], state, 0)
            attention = local[own] + decays[j][:, h : h + 1] * far
            out[own] = attention
            squares[j] = squares[j] + attention * attention
            inners[j] = inners[j] + out_grad[part].astype(F32) * gain[:, s.head(h)] * attention
            if j < s.blocks - 1:
                update = first_update[s.rows(j * s.heads + h, s.width), :]
                state = notes[s.carry(j + 1), :] * (factors[j][h : h + 1, :] * state + update)
    if earlier_sums:
        sums[...] = earlier_sums[0][...]
    else:
        sums[...] = jnp.zeros(sums.shape, F32)
    for j in range(s.blocks):
        for i, part in enumerate([squares[j], inners[j]]):
            row = (slice(i, i + 1), s.block(j))
            sums[row] = sums[row] + jnp.sum(part.T, axis=0, keepdims=True)


def grad_kernel(
    s, all_features, queries, out_grad, gain, log_decay, notes, attention, sums,
    attn_grad, keep, send, out_tail, out_gain, back_terms,
):
    core, _, _ = place_bits(s.count, True)
    lower = core == 0
    logs = s.logs(log_decay)
    factors = [jnp.exp(total_rows(a)) for a in logs]
    decays = [jnp.exp(decay_columns(a)) for a in logs]
    totals = sums[...] / all_features
    spread = lambda row: jnp.broadcast_to(row, (C, C)).T
    inverses, slopes = [], []
    for j in range(s.blocks):
        inverse = lax.rsqrt(totals[0:1, s.block(j)] + EPSILON)
        inverses.append(spread(inverse))
        slopes.append(spread(totals[1:2, s.block(j)] * inverse * inverse))
    base = s.heads * s.half
    out_tail[...] = jnp.zeros(out_tail.shape, F32)
    own = notes[: s.tail, :]
    put_tail(
        s, out_tail, 0, own[: s.heads], own[s.end : s.end + 1], own[s.start : s.start + 1]
    )
    out_gain[...] = jnp.zeros(out_gain.shape, F32)
    for h in range(s.heads):
        gain_row = gain[:, s.head(h)]
        gain_part = jnp.zeros((1, s.width), F32)
        terms = []
        for j in range(s.blocks):
            part, own = (s.block(j), s.head(h)), (s.block(j), s.own(h))
            cot = out_grad[part].astype(F32)
            att = attention[own]
            grad = ((cot * gain_row - att * slopes[j]) * inverses[j]).astype(BF16)
            attn_grad[own] = grad
            gain_part = gain_part + jnp.sum(cot * att * inverses[j], axis=0, keepdims=True)
            weighted = (queries[part].astype(F32) * decays[j][:, h : h + 1]).astype(BF16)
            term = dot(weighted, grad, 0, 0)
            terms.append(term)
            if j > 0:
                back_terms[s.rows((j - 1) * s.heads + h, s.width), :] = term
        state = terms[-1]
        for j in reversed(range(s.blocks - 1)):
            state = terms[j] + (notes[s.carry(j + 1), :] * factors[j][h : h + 1, :]) * state
        put_parts(lower, s.half, h, state, keep, send)
        out_gain[h : h + 1, :] = gain_part
    send[base : base + s.tail, :] = out_tail[...]
    send[base + s.tail :, :] = out_gain[...]


def local_grad_kernel(s, queries, values, log_decay, weights, attn_grad, key_out, value_out):
    for j, logs in enumerate(s.logs(log_decay)):
        columns, rows = decay_columns(logs), decay_rows(logs)
        for h in range(s.heads):
            mask = decay_mask(columns[:, h : h + 1], rows[h : h + 1, :])
            part, own = (s.block(j), s.head(h)), (s.block(j), s.own(h))
            grad = attn_grad[own]
            grad_weight = (dot(grad, values[part], 1, 1) * mask).astype(BF16)
            key_out[own] = dot(grad_weight, queries[part], 0, 0)
            value_out[own] = dot(weights[s.rows(j * s.heads + h, C), :], grad, 0, 0)


def final_kernel(
    s, last, keys, values, log_decay, notes, key_local, value_local, back_terms, keep, received,
    *rest,
):
    earlier, (key_out, value_out) = rest[:-2], rest[-2:]
    core, _, _ = place_bits(s.count, True)
    lower = core == 0
    logs = s.logs(log_decay)
    factors = [jnp.exp(total_rows(a)) for a in logs]
    columns = [decay_columns(a) for a in logs]
    ends = [jnp.exp(a[C - 1 : C, :] - a) for a in columns]
    for i in range(0, len(earlier), 2):
        place = slice(i // 2 * s.columns, (i // 2 + 1) * s.columns)
        key_out[:, place] = earlier[i][...]
        value_out[:, place] = earlier[i + 1][...]
    for h in range(s.heads):
        state = joined(s, lower, keep, received, h)
        for j in reversed(range(s.blocks)):
            part, own = (s.block(j), s.head(h)), (s.block(j), s.own(h))
            out = part if last else own
            end = ends[j][:, h : h + 1]
            key_far = end * far_dot(values[part], state, 1)
            value_far = end * far_dot(keys[part], state, 0)
            key_out[out] = (key_local[own] + key_far).astype(BF16)
            value_out[out] = (value_local[own] + value_far).astype(BF16)
            if j > 0:
                term = back_terms[s.rows((j - 1) * s.heads + h, s.width), :]
                state = notes[s.carry(j), :] * (term + factors[j][h : h + 1, :] * state)


def swap(value, axis, bit):
    count = lax.axis_size(axis)
    return lax.ppermute(value, axis, [(i, i ^ bit) for i in range(count)])


def next_plane(value, count, reverse):
    step = -PLANE if reverse else PLANE
    return lax.ppermute(value, "seq", [(i, (i + step) % count) for i in range(count)])


def scan_in(waves, parts, reverse, token, beside):
    bind = functools.partial
    gain_rows = lambda s: s.gains if reverse else 0
    received, chips, chip_received, local = [], [], [], []
    for s, (keep, send, tail, gain) in zip(waves, parts):
        received.append(swap(send, "seq", 1))
    for i, (s, (keep, send, tail, gain)) in enumerate(zip(waves, parts)):
        outs = [
            shape(s.heads * s.quarter, s.width),
            shape(s.heads * s.quarter + s.tail + gain_rows(s), s.width),
        ]
        (keep,) = after(token, keep)
        extra = [gain] if reverse else []
        chip = call(bind(chip_kernel, s, reverse), outs, keep, received[i], tail, *extra)
        token = chip[0]
        chips.append(chip)
        sent = chip[1]
        if chip_received:
            (sent,) = after(chip_received[-1], sent)
        chip_received.append(swap(sent, "seq", 2))
    planes, passed, gains, others = [], [], [], []
    for i, s in enumerate(waves):
        (keep,) = after(token, chips[i][0])
        outs = [shape(s.heads * s.quarter + s.tail + gain_rows(s), s.width)]
        if reverse:
            outs.append(shape((i + 1) * s.gains, s.width))
        plane, *gains = call(
            bind(plane_kernel, s, reverse), outs, keep, chips[i][1], chip_received[i], *gains
        )
        token = plane
        planes.append(plane)
        into = next_plane(plane, s.count, reverse)
        token, one = beside(token, i)
        local.append(one)
        if reverse and i == len(waves) - 1:
            others = list(after(token, *gains))
            for _ in range(s.planes - 1 - s.window):
                others.append(next_plane(others[-1], s.count, not reverse))
            (token,) = after(others[-1], token)
        passed.append(list(after(token, into)))
    for _ in range(waves[0].window - 1):
        for i, s in enumerate(waves):
            passed[i].append(next_plane(passed[i][-1], s.count, reverse))
    spreads, spread_received = [], []
    for i, s in enumerate(waves):
        (keep,) = after(token, chips[i][0])
        outs = [shape(s.heads * s.quarter, s.width)] * 2
        extra = []
        if reverse:
            outs.append(shape(s.gains, s.width))
            extra = [planes[i]]
        spread = call(
            bind(spread_kernel, s, reverse),
            outs,
            keep,
            chips[i][1],
            chip_received[i],
            *passed[i],
            *extra,
        )
        token = spread[0]
        spreads.append(spread)
        spread_received.append(swap(spread[1], "seq", 2))
    entries = []
    for i, s in enumerate(waves):
        (keep,) = after(token, spreads[i][0])
        entry = call(
            bind(entry_kernel, s, reverse),
            [shape(s.heads * s.half, s.width)] * 2,
            keep,
            spread_received[i],
            parts[i][0],
            received[i],
            parts[i][2],
        )
        token = entry[0]
        entries.append((entry[0], swap(entry[1], "seq", 1)))
    gain = None
    if reverse:
        pad = lambda a, s: a.reshape(-1, s.gains, s.width)[:, : s.heads].reshape(-1, s.width)
        gain = jnp.concatenate([pad(spread[2], s) for spread in spreads])
        for other in others[1:]:
            gain = gain + pad(other, s)
        gain = gain.reshape(-1)
    return entries, local, token, gain


def per_device(queries, keys, values, out_grad, log_decay, norm_gain, doc_ids):
    tokens, features = queries.shape
    heads = log_decay.shape[1]
    count, dp = lax.axis_size("seq"), lax.axis_size("dp")
    wave_count = max(w for w in WAVES if heads % w == 0)
    waves = [Sizes(tokens, features, heads, count, w, wave_count) for w in range(wave_count)]
    bind = functools.partial
    unit = 2 * C * C * C * waves[0].blocks * waves[0].heads
    gain = norm_gain.reshape(1, features)
    log_decay = log_decay.T
    states = []
    far = [pltpu.with_memory_space_constraint(a, pltpu.HBM) for a in (keys, values, log_decay, doc_ids)]
    for s in waves:
        groups = max(g for g in (2, 1) if s.heads % g == 0)
        given, options = (keys, values, log_decay, doc_ids), {}
        spaces = [pltpu.VMEM, pltpu.VMEM, pltpu.VMEM, pltpu.SMEM]
        scratch = []
        if not states:
            given, spaces = far, [pltpu.HBM] * 4
            scratch = [
                pltpu.VMEM((tokens, s.columns), BF16),
                pltpu.VMEM((tokens, s.columns), BF16),
                pltpu.VMEM(log_decay.shape, F32),
                pltpu.SMEM(doc_ids.shape, jnp.int32),
                pltpu.SemaphoreType.DMA((2, groups)),
                pltpu.SemaphoreType.DMA((2,)),
            ]
        else:
            given = given[:2] + after(token, log_decay) + given[3:]
        state = call(
            bind(state_kernel, s),
            [
                shape(s.heads * s.half, s.width),
                shape(s.heads * s.half + s.tail, s.width),
                shape(s.notes, s.width),
                shape(max(1, s.blocks - 1) * s.heads * s.width, s.width),
            ],
            *given,
            flops=unit,
            spaces=spaces,
            scratch=scratch,
        )
        token = state[0]
        states.append(state)
    queries, keys, values, out_grad, gain, log_decay = after(
        token, queries, keys, values, out_grad, gain, log_decay
    )

    def beside_forward(token, i):
        s = waves[i]
        (held,) = after(token, log_decay)
        local = call(
            bind(local_kernel, s),
            [shape(tokens, s.columns), shape(s.blocks * s.heads * C, C, BF16)],
            queries,
            keys,
            values,
            held,
            flops=2 * unit,
        )
        return local[0], local

    parts = [(state[0], state[1], state[2], None) for state in states]
    entries, local, token, _ = scan_in(waves, parts, False, token, beside_forward)
    attentions, sums = [], []
    for i, s in enumerate(waves):
        (held,) = after(token, log_decay)
        attention, total = call(
            bind(attention_kernel, s),
            [shape(tokens, s.columns), shape(8, tokens)],
            queries,
            out_grad,
            gain,
            held,
            states[i][2],
            local[i][0],
            states[i][3],
            *entries[i],
            *sums,
            flops=2 * unit,
        )
        token = attention
        attentions.append(attention)
        sums = [total]
    sums = sums[0]
    if dp & (dp - 1):
        sums = lax.psum(sums, "dp")
    else:
        bit = 1
        while bit < dp:
            sums = sums + swap(sums, "dp", bit)
            bit *= 2
    grads = []
    for i, s in enumerate(waves):
        (held,) = after(token, log_decay)
        grad = call(
            bind(grad_kernel, s, features * dp),
            [
                shape(tokens, s.columns, BF16),
                shape(s.heads * s.half, s.width),
                shape(s.heads * s.half + s.tail + s.gains, s.width),
                shape(s.tail, s.width),
                shape(s.gains, s.width),
                shape(max(1, s.blocks - 1) * s.heads * s.width, s.width),
            ],
            queries,
            out_grad,
            gain,
            held,
            states[i][2],
            attentions[i],
            sums,
            flops=unit,
        )
        token = grad[0]
        grads.append(grad)

    def beside_backward(token, i):
        s = waves[i]
        (held,) = after(token, log_decay)
        local_grad = call(
            bind(local_grad_kernel, s),
            [shape(tokens, s.columns), shape(tokens, s.columns)],
            queries,
            values,
            held,
            local[i][1],
            grads[i][0],
            flops=3 * unit,
        )
        return local_grad[0], local_grad

    parts = [(grad[1], grad[2], grad[3], grad[4]) for grad in grads]
    entries, local_grads, token, gain_grad = scan_in(waves, parts, True, token, beside_backward)
    (token,) = after(gain_grad, token)
    done = []
    for i, s in enumerate(waves):
        last = i == wave_count - 1
        (held,) = after(token, log_decay)
        done.extend(
            call(
                bind(final_kernel, s, last),
                [shape(tokens, features if last else s.columns, BF16)] * 2,
                keys,
                values,
                held,
                states[i][2],
                *local_grads[i],
                grads[i][5],
                *entries[i][:2],
                *(done if last else ()),
                flops=4 * unit,
            )
        )
        token = done[-1]
    return (done[-2], done[-1], gain_grad)


def solution(mesh):
    placed = (
        P("seq", "dp"),
        P("seq", "dp"),
        P("seq", "dp"),
        P("seq", "dp"),
        P("seq", "dp"),
        P("dp"),
        P("seq"),
    )
    return jax.shard_map(
        per_device,
        mesh=mesh,
        in_specs=placed,
        out_specs=(P("seq", "dp"), P("seq", "dp"), P("dp")),
        check_vma=False,
    )
```

```python
import functools
import math

import jax
import jax.numpy as jnp
from jax import lax
from jax.experimental import pallas as pl
from jax.experimental.pallas import tpu as pltpu
from jax.sharding import PartitionSpec as P

C = 128
EPSILON = 1e-06
PLANE = 4
WAVES = (2, 1)
F32 = jnp.float32
BF16 = jnp.bfloat16
HIGHEST = lax.Precision.HIGHEST


def dot(a, b, contract_a, contract_b, precision=None):
    return lax.dot_general(
        a,
        b,
        (((contract_a,), (contract_b,)), ((), ())),
        precision=precision,
        preferred_element_type=F32,
    )


def two_parts(a):
    high = a.astype(BF16)
    return high, (a - high.astype(F32)).astype(BF16)


def far_dot(a, state, contract_state):
    high, low = two_parts(state)
    return dot(a, high, 1, contract_state) + dot(a, low, 1, contract_state)


def equal(a, b):
    return (a == b).astype(F32)


def place_bits(count, reverse):
    place = lax.axis_index("seq")
    place = count - 1 - place if reverse else place
    return lax.rem(place, 2), lax.rem(place // 2, 2), place // PLANE


def triangle():
    row = lax.broadcasted_iota(jnp.int32, (C, C), 0)
    column = lax.broadcasted_iota(jnp.int32, (C, C), 1)
    return row, column


def decay_columns(log_block):
    row, column = triangle()
    return dot((row >= column).astype(F32), log_block, 1, 1, HIGHEST)


def decay_rows(log_block):
    row, column = triangle()
    return dot(log_block, (row <= column).astype(F32), 1, 0, HIGHEST)


def total_rows(log_block):
    return dot(log_block, jnp.ones((C, C), F32), 1, 0, HIGHEST)


class Sizes:
    def __init__(self, tokens, features, all_heads, count, wave, waves):
        self.tokens, self.features, self.count = tokens, features, count
        self.heads = all_heads // waves
        self.first = wave * self.heads
        self.wave = wave
        self.blocks = tokens // C
        self.width = features // all_heads
        self.half = self.width // 2
        self.quarter = self.width // 4
        self.columns = self.heads * self.width
        self.planes = count // PLANE
        longest = self.blocks * count // 2
        per_plane = self.blocks * PLANE
        self.window = max(1, min(self.planes - 1, 1 + (longest - 2) // per_plane))
        self.gains = -(-self.heads // 8) * 8
        self.tail = -(-(self.heads + 2) // 8) * 8
        self.start, self.end = self.heads, self.heads + 1
        self.notes = -(-(self.heads + 2 + self.blocks) // 8) * 8

    def own(self, h):
        return slice(h * self.width, (h + 1) * self.width)

    def head(self, h):
        return self.own(self.first + h)

    def block(self, j):
        return slice(j * C, (j + 1) * C)

    def rows(self, h, size):
        return slice(h * size, (h + 1) * size)

    def carry(self, j):
        return slice(self.heads + 2 + j, self.heads + 3 + j)

    def logs(self, log_decay):
        return [
            log_decay[self.first : self.first + self.heads, self.block(j)]
            for j in range(self.blocks)
        ]


def call(kernel, outs, *args, flops=0, spaces=None, out_spaces=None, scratch=(), deps=()):
    moved = sum(math.prod(a.shape) * a.dtype.itemsize for a in (*args, *outs))
    spaces = spaces or [pltpu.VMEM] * len(args)
    out_spaces = out_spaces or [pltpu.VMEM] * len(outs)
    given = len(args)
    return pl.pallas_call(
        lambda *refs: kernel(*refs[:given], *refs[given + len(deps) :]),
        out_shape=outs,
        in_specs=[pl.BlockSpec(memory_space=p) for p in spaces + [pl.ANY] * len(deps)],
        out_specs=[pl.BlockSpec(memory_space=p) for p in out_spaces],
        compiler_params=pltpu.CompilerParams(vmem_limit_bytes=moved + (4 << 20)),
        cost_estimate=pl.CostEstimate(flops=flops, bytes_accessed=moved, transcendentals=0),
        scratch_shapes=scratch,
    )(*args, *deps)


def after(token, *values):
    return lax.optimization_barrier((token,) + values)[1:]


def shape(rows, columns, dtype=F32):
    return jax.ShapeDtypeStruct((rows, columns), dtype)


def put_tail(s, tail_ref, base, factors, start, end):
    tail_ref[base : base + s.heads, :] = factors
    tail_ref[base + s.start : base + s.start + 1, :] = start
    tail_ref[base + s.end : base + s.end + 1, :] = end


def put_parts(first, size, h, whole, keep_ref, send_ref):
    low, high = whole[:size], whole[size:]
    rows = slice(h * size, (h + 1) * size)
    keep_ref[rows, :] = lax.select(first, low, high)
    send_ref[rows, :] = lax.select(first, high, low)


def state_kernel(s, keys, values, log_decay, doc_ids, keep, send, notes, first_update, *near):
    each, waits, first = s.heads, [], s.first
    if near:
        near_keys, near_values, near_logs, near_ids, arrived, small = near
        few = [
            pltpu.make_async_copy(doc_ids, near_ids, small.at[0]),
            pltpu.make_async_copy(log_decay, near_logs, small.at[1]),
        ]
        each = s.heads // arrived.shape[1]
        for g in range(arrived.shape[1]):
            far_part = pl.ds((s.first + g * each) * s.width, each * s.width)
            part = pl.ds(g * each * s.width, each * s.width)
            waits.append(
                [
                    pltpu.make_async_copy(keys.at[:, far_part], near_keys.at[:, part], arrived.at[0, g]),
                    pltpu.make_async_copy(
                        values.at[:, far_part], near_values.at[:, part], arrived.at[1, g]
                    ),
                ]
            )
        for copy in few + sum(waits, []):
            copy.start()
        for copy in few:
            copy.wait()
        keys, values, log_decay, doc_ids, first = near_keys, near_values, near_logs, near_ids, 0
    core, _, _ = place_bits(s.count, False)
    lower = core == 0
    docs = [jnp.full((1, s.width), doc_ids[j].astype(F32)) for j in range(s.blocks)]
    carries = [None] + [equal(docs[j - 1], docs[j]) for j in range(1, s.blocks)]
    logs = s.logs(log_decay)
    totals = [total_rows(a) for a in logs]
    factors = [jnp.exp(t) for t in totals]
    whole_factor = factors[0]
    for j in range(1, s.blocks):
        whole_factor = whole_factor * factors[j] * carries[j]
    base = s.heads * s.half
    send[base:, :] = jnp.zeros((s.tail, s.width), F32)
    put_tail(s, send, base, whole_factor, docs[0], docs[-1])
    notes[...] = jnp.zeros(notes.shape, F32)
    put_tail(s, notes, 0, whole_factor, docs[0], docs[-1])
    for j in range(1, s.blocks):
        notes[s.carry(j), :] = carries[j]
    columns = [decay_columns(a) for a in logs]
    ends = [jnp.exp(a[C - 1 : C, :] - a) for a in columns]
    for h in range(s.heads):
        if waits and h % each == 0:
            for copy in waits[h // each]:
                copy.wait()
        place = slice((first + h) * s.width, (first + h + 1) * s.width)
        state = None
        for j in range(s.blocks):
            scaled = keys[s.block(j), place].astype(F32) * ends[j][:, h : h + 1]
            update = dot(scaled.astype(BF16), values[s.block(j), place], 0, 0)
            if j < s.blocks - 1:
                first_update[s.rows(j * s.heads + h, s.width), :] = update
            if state is None:
                state = update
            else:
                state = (carries[j] * factors[j][h : h + 1, :]) * state + update
        put_parts(lower, s.half, h, state, keep, send)


def sides(first, own, other):
    return lax.select(first, own, other), lax.select(first, other, own)


def linked(s, far, near):
    return equal(far[s.end : s.end + 1, :], near[s.start : s.start + 1, :])


def join_tail(s, out, base, far, near, factor):
    out[base : base + s.tail, :] = jnp.zeros((s.tail, s.width), F32)
    put_tail(
        s,
        out,
        base,
        far[: s.heads, :] * factor,
        far[s.start : s.start + 1, :],
        near[s.end : s.end + 1, :],
    )


def chip_kernel(s, reverse, keep, received, own_tail, *rest):
    out_keep, out_send = rest[-3:-1] if reverse else rest
    core, chip, _ = place_bits(s.count, reverse)
    lower, left = core == 0, chip == 0
    base, top = s.heads * s.half, s.heads * s.quarter
    far, near = sides(lower, own_tail[: s.tail, :], received[base : base + s.tail, :])
    factor = near[: s.heads, :] * linked(s, far, near)
    join_tail(s, out_send, top, far, near, factor)
    if reverse:
        gain = rest[0][...] + received[base + s.tail :, :]
        every = rest[-1]
        if s.wave:
            every[: -s.gains, :] = rest[1][...]
        every[every.shape[0] - s.gains :, :] = gain
    for h in range(s.heads):
        rows = s.rows(h, s.half)
        far_state, near_state = sides(lower, keep[rows, :], received[rows, :])
        total = near_state + factor[h : h + 1, :] * far_state
        put_parts(left, s.quarter, h, total, out_keep, out_send)


def plane_kernel(s, reverse, keep, sent, received, *rest):
    columns, out = rest[:-1], rest[-1]
    _, chip, _ = place_bits(s.count, reverse)
    left = chip == 0
    top = s.heads * s.quarter
    far, near = sides(left, sent[top:, :], received[top:, :])
    factor = near[: s.heads, :] * linked(s, far, near)
    join_tail(s, out, top, far, near, factor)
    if columns:
        out[top + s.tail :, :] = sum([a[...] for a in columns[1:]], columns[0][...])
    for h in range(s.heads):
        rows = s.rows(h, s.quarter)
        far_state, near_state = sides(left, keep[rows, :], received[rows, :])
        out[rows, :] = near_state + factor[h : h + 1, :] * far_state


def spread_kernel(s, reverse, keep, sent, received, *rest):
    earlier, rest = rest[: s.window], rest[s.window :]
    out_keep, out_send = rest[1:3] if rest[2:] else rest
    _, chip, plane = place_bits(s.count, reverse)
    left = chip == 0
    top = s.heads * s.quarter
    far, near = sides(left, sent[top:, :], received[top:, :])
    tails = [ref[top : top + s.tail, :] for ref in earlier]
    reach = [(plane >= w + 1).astype(F32) for w in range(s.window)]
    entry = linked(s, tails[0], far) * reach[0]
    inner = [
        linked(s, tails[w + 1], tails[w]) * reach[w + 1] * tails[w][: s.heads, :]
        for w in range(s.window - 1)
    ]
    link = linked(s, far, near)
    far_factor = far[: s.heads, :]
    if rest[2:]:
        gain = rest[0][top + s.tail :, :]
        if s.planes > 1:
            gain = gain + earlier[0][top + s.tail :, :]
        rest[3][...] = gain
        out_send[top:, :] = gain
    for h in range(s.heads):
        rows, one = s.rows(h, s.quarter), slice(h, h + 1)
        state = earlier[-1][rows, :]
        for w in reversed(range(s.window - 1)):
            state = earlier[w][rows, :] + inner[w][one] * state
        into_far = entry * state
        far_state = lax.select(left, keep[rows, :], received[rows, :])
        into_near = link * (far_state + far_factor[one] * into_far)
        out_keep[rows, :] = lax.select(left, into_far, into_near)
        out_send[rows, :] = lax.select(left, into_near, into_far)


def entry_kernel(
    s, reverse, chip_keep, chip_received, keep, received, own_tail, out_keep, out_send
):
    core, chip, _ = place_bits(s.count, reverse)
    lower, left = core == 0, chip == 0
    base = s.heads * s.half
    far, near = sides(lower, own_tail[: s.tail, :], received[base : base + s.tail, :])
    link = linked(s, far, near)
    far_factor = far[: s.heads, :]
    for h in range(s.heads):
        rows, quarter = s.rows(h, s.half), s.rows(h, s.quarter)
        into_far = jnp.concatenate(
            sides(left, chip_keep[quarter, :], chip_received[quarter, :]), axis=0
        )
        far_state = lax.select(lower, keep[rows, :], received[rows, :])
        into_near = link * (far_state + far_factor[h : h + 1, :] * into_far)
        out_keep[rows, :] = lax.select(lower, into_far, into_near)
        out_send[rows, :] = lax.select(lower, into_near, into_far)


def joined(s, lower, keep, received, h):
    rows = s.rows(h, s.half)
    return jnp.concatenate(sides(lower, keep[rows, :], received[rows, :]), axis=0)


def decay_mask(column, row):
    at, other = triangle()
    gap = jnp.minimum(column - row, 0.0)
    return jnp.where(at >= other, jnp.exp(gap), 0.0)


def local_kernel(s, queries, keys, values, log_decay, out, weights):
    for j, logs in enumerate(s.logs(log_decay)):
        columns, rows = decay_columns(logs), decay_rows(logs)
        for h in range(s.heads):
            mask = decay_mask(columns[:, h : h + 1], rows[h : h + 1, :])
            part = (s.block(j), s.head(h))
            scores = dot(queries[part], keys[part], 1, 1)
            weight = (scores * mask).astype(BF16)
            weights[s.rows(j * s.heads + h, C), :] = weight
            out[s.block(j), s.own(h)] = dot(weight, values[part], 1, 0)


def attention_kernel(
    s, queries, out_grad, gain, log_decay, notes, local, first_update, keep, received, *rest
):
    earlier_sums, (out, sums) = rest[:-2], rest[-2:]
    core, _, _ = place_bits(s.count, False)
    lower = core == 0
    logs = s.logs(log_decay)
    factors = [jnp.exp(total_rows(a)) for a in logs]
    decays = [jnp.exp(decay_columns(a)) for a in logs]
    squares = [jnp.zeros((C, s.width), F32) for _ in logs]
    inners = [jnp.zeros((C, s.width), F32) for _ in logs]
    for h in range(s.heads):
        state = joined(s, lower, keep, received, h)
        for j in range(s.blocks):
            part, own = (s.block(j), s.head(h)), (s.block(j), s.own(h))
            far = far_dot(queries[part], state, 0)
            attention = local[own] + decays[j][:, h : h + 1] * far
            out[own] = attention
            squares[j] = squares[j] + attention * attention
            inners[j] = inners[j] + out_grad[part].astype(F32) * gain[s.head(h)].reshape(1, s.width) * attention
            if j < s.blocks - 1:
                update = first_update[s.rows(j * s.heads + h, s.width), :]
                state = notes[s.carry(j + 1), :] * (factors[j][h : h + 1, :] * state + update)
    if earlier_sums:
        sums[...] = earlier_sums[0][...]
    else:
        sums[...] = jnp.zeros(sums.shape, F32)
    for j in range(s.blocks):
        for i, part in enumerate([squares[j], inners[j]]):
            row = (slice(i, i + 1), s.block(j))
            sums[row] = sums[row] + jnp.sum(part.T, axis=0, keepdims=True)


def grad_kernel(
    s, all_features, queries, out_grad, gain, log_decay, notes, attention, sums,
    attn_grad, keep, send, out_tail, out_gain, back_terms,
):
    core, _, _ = place_bits(s.count, True)
    lower = core == 0
    logs = s.logs(log_decay)
    factors = [jnp.exp(total_rows(a)) for a in logs]
    decays = [jnp.exp(decay_columns(a)) for a in logs]
    totals = sums[...] / all_features
    spread = lambda row: jnp.broadcast_to(row, (C, C)).T
    inverses, slopes = [], []
    for j in range(s.blocks):
        inverse = lax.rsqrt(totals[0:1, s.block(j)] + EPSILON)
        inverses.append(spread(inverse))
        slopes.append(spread(totals[1:2, s.block(j)] * inverse * inverse))
    base = s.heads * s.half
    out_tail[...] = jnp.zeros(out_tail.shape, F32)
    own = notes[: s.tail, :]
    put_tail(
        s, out_tail, 0, own[: s.heads], own[s.end : s.end + 1], own[s.start : s.start + 1]
    )
    out_gain[...] = jnp.zeros(out_gain.shape, F32)
    for h in range(s.heads):
        gain_row = gain[s.head(h)].reshape(1, s.width)
        gain_part = jnp.zeros((1, s.width), F32)
        terms = []
        for j in range(s.blocks):
            part, own = (s.block(j), s.head(h)), (s.block(j), s.own(h))
            cot = out_grad[part].astype(F32)
            att = attention[own]
            grad = ((cot * gain_row - att * slopes[j]) * inverses[j]).astype(BF16)
            attn_grad[own] = grad
            gain_part = gain_part + jnp.sum(cot * att * inverses[j], axis=0, keepdims=True)
            weighted = (queries[part].astype(F32) * decays[j][:, h : h + 1]).astype(BF16)
            term = dot(weighted, grad, 0, 0)
            terms.append(term)
            if j > 0:
                back_terms[s.rows((j - 1) * s.heads + h, s.width), :] = term
        state = terms[-1]
        for j in reversed(range(s.blocks - 1)):
            state = terms[j] + (notes[s.carry(j + 1), :] * factors[j][h : h + 1, :]) * state
        put_parts(lower, s.half, h, state, keep, send)
        out_gain[h : h + 1, :] = gain_part
    send[base : base + s.tail, :] = out_tail[...]
    send[base + s.tail :, :] = out_gain[...]


def local_grad_kernel(s, queries, values, log_decay, weights, attn_grad, key_out, value_out):
    for j, logs in enumerate(s.logs(log_decay)):
        columns, rows = decay_columns(logs), decay_rows(logs)
        for h in range(s.heads):
            mask = decay_mask(columns[:, h : h + 1], rows[h : h + 1, :])
            part, own = (s.block(j), s.head(h)), (s.block(j), s.own(h))
            grad = attn_grad[own]
            grad_weight = (dot(grad, values[part], 1, 1) * mask).astype(BF16)
            key_out[own] = dot(grad_weight, queries[part], 0, 0)
            value_out[own] = dot(weights[s.rows(j * s.heads + h, C), :], grad, 0, 0)


def final_kernel(s, waves, keys, values, log_decay, notes, key_local, value_local, back_terms, *rest):
    keep, received = rest[:2]
    last = s.wave == waves - 1
    near_outs = rest[-2:]
    copies = []
    if last:
        *far_outs, far_gain, near_gain, sent = rest[-7:-2]
        groups = sent.shape[1] - s.wave
        own, other = rest[2 + 2 * s.wave : 4 + 2 * s.wave]
        base = s.heads * s.quarter
        for w in range(waves):
            for h in range(s.heads):
                row = w * s.gains + h
                total = own[row : row + 1, :] + other[base + row : base + row + 1, :]
                place = (w * s.heads + h) * s.width
                near_gain[place : place + s.width] = total.reshape(s.width)
        copies.append(pltpu.make_async_copy(near_gain, far_gain, sent.at[2, 0]))
        copies[-1].start()
        for w in range(s.wave):
            place = pl.ds(w * s.columns, s.columns)
            for i, far in enumerate(far_outs):
                near = rest[2 + 2 * w + i]
                copies.append(
                    pltpu.make_async_copy(near, far.at[:, place], sent.at[i, groups + w])
                )
                copies[-1].start()
    core, _, _ = place_bits(s.count, True)
    lower = core == 0
    logs = s.logs(log_decay)
    factors = [jnp.exp(total_rows(a)) for a in logs]
    columns = [decay_columns(a) for a in logs]
    ends = [jnp.exp(a[C - 1 : C, :] - a) for a in columns]
    for h in range(s.heads):
        state = joined(s, lower, keep, received, h)
        for j in reversed(range(s.blocks)):
            part, own = (s.block(j), s.head(h)), (s.block(j), s.own(h))
            end = ends[j][:, h : h + 1]
            key_far = end * far_dot(values[part], state, 1)
            value_far = end * far_dot(keys[part], state, 0)
            near_outs[0][own] = (key_local[own] + key_far).astype(BF16)
            near_outs[1][own] = (value_local[own] + value_far).astype(BF16)
            if j > 0:
                term = back_terms[s.rows((j - 1) * s.heads + h, s.width), :]
                state = notes[s.carry(j), :] * (term + factors[j][h : h + 1, :] * state)
        if last and (h + 1) * groups % s.heads == 0:
            each, g = s.heads // groups, h * groups // s.heads
            part = pl.ds(g * each * s.width, each * s.width)
            far_part = pl.ds((s.first + g * each) * s.width, each * s.width)
            for i, (near, far) in enumerate(zip(near_outs, far_outs)):
                copies.append(
                    pltpu.make_async_copy(near.at[:, part], far.at[:, far_part], sent.at[i, g])
                )
                copies[-1].start()
    for copy in copies:
        copy.wait()


def swap(value, axis, bit):
    count = lax.axis_size(axis)
    return lax.ppermute(value, axis, [(i, i ^ bit) for i in range(count)])


def next_plane(value, count, reverse):
    step = -PLANE if reverse else PLANE
    return lax.ppermute(value, "seq", [(i, (i + step) % count) for i in range(count)])


def scan_in(waves, parts, reverse, token, beside):
    bind = functools.partial
    last = waves[-1]
    gain_rows = lambda s: len(waves) * s.gains if reverse and s is last else 0
    received, chips, chip_received, local, gains, others = [], [], [], [], [], []
    for s, (keep, send, tail, gain) in zip(waves, parts):
        received.append(swap(send, "seq", 1))
    for i, (s, (keep, send, tail, gain)) in enumerate(zip(waves, parts)):
        outs = [
            shape(s.heads * s.quarter, s.width),
            shape(s.heads * s.quarter + s.tail, s.width),
        ]
        (keep,) = after(token, keep)
        extra = []
        if reverse:
            extra = [gain, *gains]
            outs.append(shape((i + 1) * s.gains, s.width))
        *chip, = call(bind(chip_kernel, s, reverse), outs, keep, received[i], tail, *extra)
        gains = chip[2:]
        token = chip[0]
        chips.append(chip)
        chip_received.append(swap(chip[1], "seq", 2))
    if reverse:
        bit = last.count // 2
        while bit > PLANE:
            if others:
                gains, others = [gains[0] + others[0]], []
            others = [swap(gains[0], "seq", bit)]
            bit //= 2
    planes, passed = [], []
    for i in range(len(waves) - 1):
        token, one = beside(token, i)
        local.append(one)
    for i, s in enumerate(waves):
        (keep,) = after(token, chips[i][0])
        outs = [shape(s.heads * s.quarter + s.tail + gain_rows(s), s.width)]
        columns = gains + others if gain_rows(s) else []
        (plane,) = call(
            bind(plane_kernel, s, reverse),
            outs,
            keep,
            chips[i][1],
            chip_received[i],
            *columns,
            deps=planes[-1:],
        )
        token = plane
        planes.append(plane)
        passed.append([next_plane(plane, s.count, reverse)])
    for i in range(len(local), len(waves)):
        token, one = beside(token, i)
        local.append(one)
    passed = [list(after(token, one[0])) for one in passed]
    for _ in range(waves[0].window - 1):
        for i, s in enumerate(waves):
            passed[i].append(next_plane(passed[i][-1], s.count, reverse))
    spreads, spread_received = [], []
    for i, s in enumerate(waves):
        (keep,) = after(token, chips[i][0])
        outs = [
            shape(s.heads * s.quarter, s.width),
            shape(s.heads * s.quarter + gain_rows(s), s.width),
        ]
        extra = []
        if gain_rows(s):
            outs.append(shape(gain_rows(s), s.width))
            extra = [planes[i]]
        spread = call(
            bind(spread_kernel, s, reverse),
            outs,
            keep,
            chips[i][1],
            chip_received[i],
            *passed[i],
            *extra,
        )
        token = spread[0]
        spreads.append(spread)
        spread_received.append(swap(spread[1], "seq", 2))
    entries = []
    for i, s in enumerate(waves):
        (keep,) = after(token, spreads[i][0])
        entry = call(
            bind(entry_kernel, s, reverse),
            [shape(s.heads * s.half, s.width)] * 2,
            keep,
            spread_received[i],
            parts[i][0],
            received[i],
            parts[i][2],
        )
        token = entry[0]
        entries.append((entry[0], swap(entry[1], "seq", 1)))
    return entries, local, token, [spreads[-1][-1], spread_received[-1]]


def per_device(queries, keys, values, out_grad, log_decay, norm_gain, doc_ids):
    tokens, features = queries.shape
    heads = log_decay.shape[1]
    count, dp = lax.axis_size("seq"), lax.axis_size("dp")
    wave_count = max(w for w in WAVES if heads % w == 0)
    waves = [Sizes(tokens, features, heads, count, w, wave_count) for w in range(wave_count)]
    bind = functools.partial
    unit = 2 * C * C * C * waves[0].blocks * waves[0].heads
    gain = norm_gain
    log_decay = log_decay.T
    states = []
    far = [pltpu.with_memory_space_constraint(a, pltpu.HBM) for a in (keys, values, log_decay, doc_ids)]
    for s in waves:
        groups = max(g for g in (2, 1) if s.heads % g == 0)
        given, options = (keys, values, log_decay, doc_ids), {}
        spaces = [pltpu.VMEM, pltpu.VMEM, pltpu.VMEM, pltpu.SMEM]
        scratch = []
        if not states:
            given, spaces = far, [pltpu.HBM] * 4
            scratch = [
                pltpu.VMEM((tokens, s.columns), BF16),
                pltpu.VMEM((tokens, s.columns), BF16),
                pltpu.VMEM(log_decay.shape, F32),
                pltpu.SMEM(doc_ids.shape, jnp.int32),
                pltpu.SemaphoreType.DMA((2, groups)),
                pltpu.SemaphoreType.DMA((2,)),
            ]
        else:
            given = given[:2] + after(token, log_decay) + given[3:]
        state = call(
            bind(state_kernel, s),
            [
                shape(s.heads * s.half, s.width),
                shape(s.heads * s.half + s.tail, s.width),
                shape(s.notes, s.width),
                shape(max(1, s.blocks - 1) * s.heads * s.width, s.width),
            ],
            *given,
            flops=unit,
            spaces=spaces,
            scratch=scratch,
        )
        token = state[0]
        states.append(state)
    queries, keys, values, out_grad, gain, log_decay = after(
        token, queries, keys, values, out_grad, gain, log_decay
    )

    def beside_forward(token, i):
        s = waves[i]
        (held,) = after(token, log_decay)
        local = call(
            bind(local_kernel, s),
            [shape(tokens, s.columns), shape(s.blocks * s.heads * C, C, BF16)],
            queries,
            keys,
            values,
            held,
            flops=2 * unit,
        )
        return local[0], local

    parts = [(state[0], state[1], state[2], None) for state in states]
    entries, local, token, _ = scan_in(waves, parts, False, token, beside_forward)
    attentions, sums = [], []
    for i, s in enumerate(waves):
        (held,) = after(token, log_decay)
        attention, total = call(
            bind(attention_kernel, s),
            [shape(tokens, s.columns), shape(8, tokens)],
            queries,
            out_grad,
            gain,
            held,
            states[i][2],
            local[i][0],
            states[i][3],
            *entries[i],
            *sums,
            flops=2 * unit,
        )
        token = attention
        attentions.append(attention)
        sums = [total]
    sums = sums[0]
    if dp & (dp - 1):
        sums = lax.psum(sums, "dp")
    else:
        bit = 1
        while bit < dp:
            sums = sums + swap(sums, "dp", bit)
            bit *= 2
    grads = []
    for i, s in enumerate(waves):
        (held,) = after(token, log_decay)
        grad = call(
            bind(grad_kernel, s, features * dp),
            [
                shape(tokens, s.columns, BF16),
                shape(s.heads * s.half, s.width),
                shape(s.heads * s.half + s.tail + s.gains, s.width),
                shape(s.tail, s.width),
                shape(s.gains, s.width),
                shape(max(1, s.blocks - 1) * s.heads * s.width, s.width),
            ],
            queries,
            out_grad,
            gain,
            held,
            states[i][2],
            attentions[i],
            sums,
            flops=unit,
        )
        token = grad[0]
        grads.append(grad)

    def beside_backward(token, i):
        s = waves[i]
        (held,) = after(token, log_decay)
        local_grad = call(
            bind(local_grad_kernel, s),
            [shape(tokens, s.columns), shape(tokens, s.columns)],
            queries,
            values,
            held,
            local[i][1],
            grads[i][0],
            flops=3 * unit,
        )
        return local_grad[0], local_grad

    parts = [(grad[1], grad[2], grad[3], grad[4]) for grad in grads]
    entries, local_grads, token, gains = scan_in(waves, parts, True, token, beside_backward)
    done = []
    for i, s in enumerate(waves):
        last = i == wave_count - 1
        (held,) = after(token, log_decay)
        groups = max(g for g in (3, 2, 1) if s.heads % g == 0)
        given = [
            keys, values, held, states[i][2], *local_grads[i], grads[i][5], *entries[i], *done,
        ]
        scratch = []
        if last:
            given += gains
            outs = [pltpu.HBM((tokens, features), BF16)] * 2 + [pltpu.HBM((features,), F32)]
            out_spaces = [pltpu.HBM] * 3
            scratch = [
                pltpu.VMEM((features,), F32),
                pltpu.SemaphoreType.DMA((3, groups + i)),
                pltpu.VMEM((tokens, s.columns), BF16),
                pltpu.VMEM((tokens, s.columns), BF16),
            ]
        else:
            outs = [shape(tokens, s.columns, BF16)] * 2
            out_spaces = [pltpu.VMEM] * 2
        made = call(
            bind(final_kernel, s, wave_count),
            outs,
            *given,
            flops=4 * unit,
            out_spaces=out_spaces,
            scratch=scratch,
        )
        token = made[0]
        done += made
    return tuple(done[-3:])


def solution(mesh):
    placed = (
        P("seq", "dp"),
        P("seq", "dp"),
        P("seq", "dp"),
        P("seq", "dp"),
        P("seq", "dp"),
        P("dp"),
        P("seq"),
    )
    return jax.shard_map(
        per_device,
        mesh=mesh,
        in_specs=placed,
        out_specs=(P("seq", "dp"), P("seq", "dp"), P("dp")),
        check_vma=False,
    )
```

```python
import functools
import math

import jax
import jax.numpy as jnp
from jax import lax
from jax.experimental import pallas as pl
from jax.experimental.pallas import tpu as pltpu
from jax.sharding import PartitionSpec as P

C = 128
EPSILON = 1e-06
PLANE = 4
WAVES = (2, 1)
F32 = jnp.float32
BF16 = jnp.bfloat16
HIGHEST = lax.Precision.HIGHEST


def dot(a, b, contract_a, contract_b, precision=None):
    return lax.dot_general(
        a,
        b,
        (((contract_a,), (contract_b,)), ((), ())),
        precision=precision,
        preferred_element_type=F32,
    )


def two_parts(a):
    high = a.astype(BF16)
    return high, (a - high.astype(F32)).astype(BF16)


def far_dot(a, state, contract_state):
    parts = jnp.concatenate(two_parts(state), axis=contract_state)
    return dot(jnp.concatenate([a, a], axis=1), parts, 1, contract_state)


def equal(a, b):
    return (a == b).astype(F32)


def place_bits(count, reverse):
    place = lax.axis_index("seq")
    place = count - 1 - place if reverse else place
    return lax.rem(place, 2), lax.rem(place // 2, 2), place // PLANE


def triangle():
    row = lax.broadcasted_iota(jnp.int32, (C, C), 0)
    column = lax.broadcasted_iota(jnp.int32, (C, C), 1)
    return row, column


def decay_columns(log_block):
    row, column = triangle()
    return dot((row >= column).astype(F32), log_block, 1, 1, HIGHEST)


def decay_rows(log_block):
    row, column = triangle()
    return dot(log_block, (row <= column).astype(F32), 1, 0, HIGHEST)


def total_rows(log_block):
    return dot(log_block, jnp.ones((C, C), F32), 1, 0, HIGHEST)


class Sizes:
    def __init__(self, tokens, features, all_heads, count, wave, waves):
        self.tokens, self.features, self.count = tokens, features, count
        self.heads = all_heads // waves
        self.first = wave * self.heads
        self.wave = wave
        self.blocks = tokens // C
        self.width = features // all_heads
        self.half = self.width // 2
        self.quarter = self.width // 4
        self.columns = self.heads * self.width
        self.planes = count // PLANE
        longest = self.blocks * count // 2
        per_plane = self.blocks * PLANE
        self.window = max(1, min(self.planes - 1, 1 + (longest - 2) // per_plane))
        self.gains = -(-self.heads // 8) * 8
        self.tail = -(-(self.heads + 2) // 8) * 8
        self.start, self.end = self.heads, self.heads + 1
        self.notes = -(-(self.heads + 2 + self.blocks) // 8) * 8

    def own(self, h):
        return slice(h * self.width, (h + 1) * self.width)

    def head(self, h):
        return self.own(self.first + h)

    def block(self, j):
        return slice(j * C, (j + 1) * C)

    def rows(self, h, size):
        return slice(h * size, (h + 1) * size)

    def carry(self, j):
        return slice(self.heads + 2 + j, self.heads + 3 + j)

    def logs(self, log_decay):
        return [
            log_decay[self.first : self.first + self.heads, self.block(j)]
            for j in range(self.blocks)
        ]


def call(kernel, outs, *args, flops=0, spaces=None, out_spaces=None, scratch=(), deps=()):
    moved = sum(math.prod(a.shape) * a.dtype.itemsize for a in (*args, *outs))
    spaces = spaces or [pltpu.VMEM] * len(args)
    out_spaces = out_spaces or [pltpu.VMEM] * len(outs)
    given = len(args)
    return pl.pallas_call(
        lambda *refs: kernel(*refs[:given], *refs[given + len(deps) :]),
        out_shape=outs,
        in_specs=[pl.BlockSpec(memory_space=p) for p in spaces + [pl.ANY] * len(deps)],
        out_specs=[pl.BlockSpec(memory_space=p) for p in out_spaces],
        compiler_params=pltpu.CompilerParams(vmem_limit_bytes=moved + (4 << 20)),
        cost_estimate=pl.CostEstimate(flops=flops, bytes_accessed=moved, transcendentals=0),
        scratch_shapes=scratch,
    )(*args, *deps)


def after(token, *values):
    return lax.optimization_barrier((token,) + values)[1:]


def shape(rows, columns, dtype=F32):
    return jax.ShapeDtypeStruct((rows, columns), dtype)


def put_tail(s, tail_ref, base, factors, start, end):
    tail_ref[base : base + s.heads, :] = factors
    tail_ref[base + s.start : base + s.start + 1, :] = start
    tail_ref[base + s.end : base + s.end + 1, :] = end


def put_parts(first, size, h, whole, keep_ref, send_ref):
    low, high = whole[:size], whole[size:]
    rows = slice(h * size, (h + 1) * size)
    keep_ref[rows, :] = lax.select(first, low, high)
    send_ref[rows, :] = lax.select(first, high, low)


def state_kernel(s, keys, values, log_decay, doc_ids, keep, send, notes, first_update, *near):
    each, waits, first = s.heads, [], s.first
    if near:
        near_keys, near_values, near_logs, near_ids, arrived, small = near
        few = [
            pltpu.make_async_copy(doc_ids, near_ids, small.at[0]),
            pltpu.make_async_copy(log_decay, near_logs, small.at[1]),
        ]
        each = s.heads // arrived.shape[1]
        for g in range(arrived.shape[1]):
            far_part = pl.ds((s.first + g * each) * s.width, each * s.width)
            part = pl.ds(g * each * s.width, each * s.width)
            waits.append(
                [
                    pltpu.make_async_copy(keys.at[:, far_part], near_keys.at[:, part], arrived.at[0, g]),
                    pltpu.make_async_copy(
                        values.at[:, far_part], near_values.at[:, part], arrived.at[1, g]
                    ),
                ]
            )
        for copy in few + sum(waits, []):
            copy.start()
        for copy in few:
            copy.wait()
        keys, values, log_decay, doc_ids, first = near_keys, near_values, near_logs, near_ids, 0
    core, _, _ = place_bits(s.count, False)
    lower = core == 0
    docs = [jnp.full((1, s.width), doc_ids[j].astype(F32)) for j in range(s.blocks)]
    carries = [None] + [equal(docs[j - 1], docs[j]) for j in range(1, s.blocks)]
    logs = s.logs(log_decay)
    totals = [total_rows(a) for a in logs]
    factors = [jnp.exp(t) for t in totals]
    whole_factor = factors[0]
    for j in range(1, s.blocks):
        whole_factor = whole_factor * factors[j] * carries[j]
    base = s.heads * s.half
    send[base:, :] = jnp.zeros((s.tail, s.width), F32)
    put_tail(s, send, base, whole_factor, docs[0], docs[-1])
    notes[...] = jnp.zeros(notes.shape, F32)
    put_tail(s, notes, 0, whole_factor, docs[0], docs[-1])
    for j in range(1, s.blocks):
        notes[s.carry(j), :] = carries[j]
    columns = [decay_columns(a) for a in logs]
    ends = [jnp.exp(a[C - 1 : C, :] - a) for a in columns]
    for h in range(s.heads):
        if waits and h % each == 0:
            for copy in waits[h // each]:
                copy.wait()
        place = slice((first + h) * s.width, (first + h + 1) * s.width)
        state = None
        for j in range(s.blocks):
            scaled = keys[s.block(j), place].astype(F32) * ends[j][:, h : h + 1]
            update = dot(scaled.astype(BF16), values[s.block(j), place], 0, 0)
            if j < s.blocks - 1:
                first_update[s.rows(j * s.heads + h, s.width), :] = update
            if state is None:
                state = update
            else:
                state = (carries[j] * factors[j][h : h + 1, :]) * state + update
        put_parts(lower, s.half, h, state, keep, send)


def sides(first, own, other):
    return lax.select(first, own, other), lax.select(first, other, own)


def linked(s, far, near):
    return equal(far[s.end : s.end + 1, :], near[s.start : s.start + 1, :])


def join_tail(s, out, base, far, near, factor):
    out[base : base + s.tail, :] = jnp.zeros((s.tail, s.width), F32)
    put_tail(
        s,
        out,
        base,
        far[: s.heads, :] * factor,
        far[s.start : s.start + 1, :],
        near[s.end : s.end + 1, :],
    )


def chip_kernel(s, reverse, keep, received, own_tail, *rest):
    out_keep, out_send = rest[-3:-1] if reverse else rest
    core, chip, _ = place_bits(s.count, reverse)
    lower, left = core == 0, chip == 0
    base, top = s.heads * s.half, s.heads * s.quarter
    far, near = sides(lower, own_tail[: s.tail, :], received[base : base + s.tail, :])
    factor = near[: s.heads, :] * linked(s, far, near)
    join_tail(s, out_send, top, far, near, factor)
    if reverse:
        gain = rest[0][...] + received[base + s.tail :, :]
        every = rest[-1]
        if s.wave:
            every[: -s.gains, :] = rest[1][...]
        every[every.shape[0] - s.gains :, :] = gain
    for h in range(s.heads):
        rows = s.rows(h, s.half)
        far_state, near_state = sides(lower, keep[rows, :], received[rows, :])
        total = near_state + factor[h : h + 1, :] * far_state
        put_parts(left, s.quarter, h, total, out_keep, out_send)


def plane_kernel(s, reverse, keep, sent, received, *rest):
    columns, out = rest[:-1], rest[-1]
    _, chip, _ = place_bits(s.count, reverse)
    left = chip == 0
    top = s.heads * s.quarter
    far, near = sides(left, sent[top:, :], received[top:, :])
    factor = near[: s.heads, :] * linked(s, far, near)
    join_tail(s, out, top, far, near, factor)
    if columns:
        out[top + s.tail :, :] = sum([a[...] for a in columns[1:]], columns[0][...])
    for h in range(s.heads):
        rows = s.rows(h, s.quarter)
        far_state, near_state = sides(left, keep[rows, :], received[rows, :])
        out[rows, :] = near_state + factor[h : h + 1, :] * far_state


def spread_kernel(s, reverse, keep, sent, received, *rest):
    earlier, rest = rest[: s.window], rest[s.window :]
    out_keep, out_send = rest[1:3] if rest[2:] else rest
    _, chip, plane = place_bits(s.count, reverse)
    left = chip == 0
    top = s.heads * s.quarter
    far, near = sides(left, sent[top:, :], received[top:, :])
    tails = [ref[top : top + s.tail, :] for ref in earlier]
    reach = [(plane >= w + 1).astype(F32) for w in range(s.window)]
    entry = linked(s, tails[0], far) * reach[0]
    inner = [
        linked(s, tails[w + 1], tails[w]) * reach[w + 1] * tails[w][: s.heads, :]
        for w in range(s.window - 1)
    ]
    link = linked(s, far, near)
    far_factor = far[: s.heads, :]
    if rest[2:]:
        gain = rest[0][top + s.tail :, :]
        if s.planes > 1:
            gain = gain + earlier[0][top + s.tail :, :]
        rest[3][...] = gain
        out_send[top:, :] = gain
    for h in range(s.heads):
        rows, one = s.rows(h, s.quarter), slice(h, h + 1)
        state = earlier[-1][rows, :]
        for w in reversed(range(s.window - 1)):
            state = earlier[w][rows, :] + inner[w][one] * state
        into_far = entry * state
        far_state = lax.select(left, keep[rows, :], received[rows, :])
        into_near = link * (far_state + far_factor[one] * into_far)
        out_keep[rows, :] = lax.select(left, into_far, into_near)
        out_send[rows, :] = lax.select(left, into_near, into_far)


def entry_kernel(
    s, reverse, chip_keep, chip_received, keep, received, own_tail, out_keep, out_send
):
    core, chip, _ = place_bits(s.count, reverse)
    lower, left = core == 0, chip == 0
    base = s.heads * s.half
    far, near = sides(lower, own_tail[: s.tail, :], received[base : base + s.tail, :])
    link = linked(s, far, near)
    far_factor = far[: s.heads, :]
    for h in range(s.heads):
        rows, quarter = s.rows(h, s.half), s.rows(h, s.quarter)
        into_far = jnp.concatenate(
            sides(left, chip_keep[quarter, :], chip_received[quarter, :]), axis=0
        )
        far_state = lax.select(lower, keep[rows, :], received[rows, :])
        into_near = link * (far_state + far_factor[h : h + 1, :] * into_far)
        out_keep[rows, :] = lax.select(lower, into_far, into_near)
        out_send[rows, :] = lax.select(lower, into_near, into_far)


def joined(s, lower, keep, received, h):
    rows = s.rows(h, s.half)
    return jnp.concatenate(sides(lower, keep[rows, :], received[rows, :]), axis=0)


def decay_mask(column, row):
    at, other = triangle()
    gap = jnp.minimum(column - row, 0.0)
    return jnp.where(at >= other, jnp.exp(gap), 0.0)


def local_kernel(s, queries, keys, values, log_decay, gain, out, weights):
    for j, logs in enumerate(s.logs(log_decay)):
        columns, rows = decay_columns(logs), decay_rows(logs)
        for h in range(s.heads):
            mask = decay_mask(columns[:, h : h + 1], rows[h : h + 1, :])
            part = (s.block(j), s.head(h))
            scores = dot(queries[part], keys[part], 1, 1)
            weight = (scores * mask).astype(BF16)
            weights[s.rows(j * s.heads + h, C), :] = weight
            out[s.block(j), s.own(h)] = dot(weight, values[part], 1, 0)


def attention_kernel(
    s, queries, out_grad, gain, log_decay, notes, local, first_update, keep, received, *rest
):
    earlier_sums, (out, sums) = rest[:-2], rest[-2:]
    core, _, _ = place_bits(s.count, False)
    lower = core == 0
    logs = s.logs(log_decay)
    factors = [jnp.exp(total_rows(a)) for a in logs]
    decays = [jnp.exp(decay_columns(a)) for a in logs]
    squares = [jnp.zeros((C, s.width), F32) for _ in logs]
    inners = [jnp.zeros((C, s.width), F32) for _ in logs]
    for h in range(s.heads):
        state = joined(s, lower, keep, received, h)
        for j in range(s.blocks):
            part, own = (s.block(j), s.head(h)), (s.block(j), s.own(h))
            far = far_dot(queries[part], state, 0)
            attention = local[own] + decays[j][:, h : h + 1] * far
            out[own] = attention
            squares[j] = squares[j] + attention * attention
            inners[j] = inners[j] + out_grad[part].astype(F32) * gain[s.head(h)].reshape(1, s.width) * attention
            if j < s.blocks - 1:
                update = first_update[s.rows(j * s.heads + h, s.width), :]
                state = notes[s.carry(j + 1), :] * (factors[j][h : h + 1, :] * state + update)
    if earlier_sums:
        sums[...] = earlier_sums[0][...]
    else:
        sums[...] = jnp.zeros(sums.shape, F32)
    for j in range(s.blocks):
        for i, part in enumerate([squares[j], inners[j]]):
            row = (slice(i, i + 1), s.block(j))
            sums[row] = sums[row] + jnp.sum(part.T, axis=0, keepdims=True)


def grad_kernel(
    s, all_features, queries, out_grad, gain, log_decay, notes, attention, *rest
):
    sums, (attn_grad, keep, send, out_tail, out_gain, back_terms) = rest[:-6], rest[-6:]
    core, _, _ = place_bits(s.count, True)
    lower = core == 0
    logs = s.logs(log_decay)
    factors = [jnp.exp(total_rows(a)) for a in logs]
    decays = [jnp.exp(decay_columns(a)) for a in logs]
    totals = sum([a[...] for a in sums[1:]], sums[0][...]) / all_features
    spread = lambda row: jnp.broadcast_to(row, (C, C)).T
    inverses, slopes = [], []
    for j in range(s.blocks):
        inverse = lax.rsqrt(totals[0:1, s.block(j)] + EPSILON)
        inverses.append(spread(inverse))
        slopes.append(spread(totals[1:2, s.block(j)] * inverse * inverse))
    base = s.heads * s.half
    out_tail[...] = jnp.zeros(out_tail.shape, F32)
    own = notes[: s.tail, :]
    put_tail(
        s, out_tail, 0, own[: s.heads], own[s.end : s.end + 1], own[s.start : s.start + 1]
    )
    out_gain[...] = jnp.zeros(out_gain.shape, F32)
    for h in range(s.heads):
        gain_row = gain[s.head(h)].reshape(1, s.width)
        gain_part = jnp.zeros((1, s.width), F32)
        terms = []
        for j in range(s.blocks):
            part, own = (s.block(j), s.head(h)), (s.block(j), s.own(h))
            cot = out_grad[part].astype(F32)
            att = attention[own]
            grad = ((cot * gain_row - att * slopes[j]) * inverses[j]).astype(BF16)
            attn_grad[own] = grad
            gain_part = gain_part + jnp.sum(cot * att * inverses[j], axis=0, keepdims=True)
            weighted = (queries[part].astype(F32) * decays[j][:, h : h + 1]).astype(BF16)
            term = dot(weighted, grad, 0, 0)
            terms.append(term)
            if j > 0:
                back_terms[s.rows((j - 1) * s.heads + h, s.width), :] = term
        state = terms[-1]
        for j in reversed(range(s.blocks - 1)):
            state = terms[j] + (notes[s.carry(j + 1), :] * factors[j][h : h + 1, :]) * state
        put_parts(lower, s.half, h, state, keep, send)
        out_gain[h : h + 1, :] = gain_part
    send[base : base + s.tail, :] = out_tail[...]
    send[base + s.tail :, :] = out_gain[...]


def local_grad_kernel(s, queries, values, log_decay, weights, attn_grad, key_out, value_out):
    for j, logs in enumerate(s.logs(log_decay)):
        columns, rows = decay_columns(logs), decay_rows(logs)
        for h in range(s.heads):
            mask = decay_mask(columns[:, h : h + 1], rows[h : h + 1, :])
            part, own = (s.block(j), s.head(h)), (s.block(j), s.own(h))
            grad = attn_grad[own]
            grad_weight = (dot(grad, values[part], 1, 1) * mask).astype(BF16)
            key_out[own] = dot(grad_weight, queries[part], 0, 0)
            value_out[own] = dot(weights[s.rows(j * s.heads + h, C), :], grad, 0, 0)


def final_kernel(s, waves, keys, values, log_decay, notes, key_local, value_local, back_terms, *rest):
    keep, received = rest[:2]
    last = s.wave == waves - 1
    near_outs = rest[-2:]
    copies = []
    if last:
        *far_outs, far_gain, near_gain, sent = rest[-7:-2]
        groups = sent.shape[1] - s.wave
        own, other = rest[2 + 2 * s.wave : 4 + 2 * s.wave]
        base = s.heads * s.quarter
        for w in range(waves):
            for h in range(s.heads):
                row = w * s.gains + h
                total = own[row : row + 1, :] + other[base + row : base + row + 1, :]
                place = (w * s.heads + h) * s.width
                near_gain[place : place + s.width] = total.reshape(s.width)
        copies.append(pltpu.make_async_copy(near_gain, far_gain, sent.at[2, 0]))
        copies[-1].start()
        for w in range(s.wave):
            place = pl.ds(w * s.columns, s.columns)
            for i, far in enumerate(far_outs):
                near = rest[2 + 2 * w + i]
                copies.append(
                    pltpu.make_async_copy(near, far.at[:, place], sent.at[i, groups + w])
                )
                copies[-1].start()
    core, _, _ = place_bits(s.count, True)
    lower = core == 0
    logs = s.logs(log_decay)
    factors = [jnp.exp(total_rows(a)) for a in logs]
    columns = [decay_columns(a) for a in logs]
    ends = [jnp.exp(a[C - 1 : C, :] - a) for a in columns]
    for h in range(s.heads):
        state = joined(s, lower, keep, received, h)
        for j in reversed(range(s.blocks)):
            part, own = (s.block(j), s.head(h)), (s.block(j), s.own(h))
            end = ends[j][:, h : h + 1]
            key_far = end * far_dot(values[part], state, 1)
            value_far = end * far_dot(keys[part], state, 0)
            near_outs[0][own] = (key_local[own] + key_far).astype(BF16)
            near_outs[1][own] = (value_local[own] + value_far).astype(BF16)
            if j > 0:
                term = back_terms[s.rows((j - 1) * s.heads + h, s.width), :]
                state = notes[s.carry(j), :] * (term + factors[j][h : h + 1, :] * state)
        if last and (h + 1) * groups % s.heads == 0:
            each, g = s.heads // groups, h * groups // s.heads
            part = pl.ds(g * each * s.width, each * s.width)
            far_part = pl.ds((s.first + g * each) * s.width, each * s.width)
            for i, (near, far) in enumerate(zip(near_outs, far_outs)):
                copies.append(
                    pltpu.make_async_copy(near.at[:, part], far.at[:, far_part], sent.at[i, g])
                )
                copies[-1].start()
    for copy in copies:
        copy.wait()


def swap(value, axis, bit):
    count = lax.axis_size(axis)
    return lax.ppermute(value, axis, [(i, i ^ bit) for i in range(count)])


def next_plane(value, count, reverse):
    step = -PLANE if reverse else PLANE
    return lax.ppermute(value, "seq", [(i, (i + step) % count) for i in range(count)])


def pass_on(value, count, reverse, behind):
    planes = count // PLANE
    pairs = []
    for source in range(count):
        plane, place = divmod(source, PLANE)
        if plane < behind:
            target = source ^ 2
        else:
            target = (plane + 1 if plane < planes - 1 else behind) * PLANE + place
        pair = (source, target)
        pairs.append(tuple(count - 1 - a for a in pair) if reverse else pair)
    return lax.ppermute(value, "seq", pairs)


def scan_in(waves, parts, reverse, token, beside):
    bind = functools.partial
    gain_rows = lambda s: len(waves) * s.gains if reverse and s.wave == 0 else 0
    received, chips, chip_received, local, gains, others = [], [], [], [], [], []
    for s, (keep, send, tail, gain) in zip(waves, parts):
        received.append(swap(send, "seq", 1))
    for i, (s, (keep, send, tail, gain)) in enumerate(zip(waves, parts)):
        outs = [
            shape(s.heads * s.quarter, s.width),
            shape(s.heads * s.quarter + s.tail, s.width),
        ]
        (keep,) = after(token, keep)
        extra = []
        if reverse:
            extra = [gain, *gains]
            outs.append(shape((i + 1) * s.gains, s.width))
        *chip, = call(bind(chip_kernel, s, reverse), outs, keep, received[i], tail, *extra)
        gains = chip[2:]
        token = chip[0]
        chips.append(chip)
        chip_received.append(swap(chip[1], "seq", 2))
    if reverse:
        bit = waves[0].count // 2
        while bit > PLANE:
            if others:
                gains, others = [gains[0] + others[0]], []
            others = [swap(gains[0], "seq", bit + 1)]
            bit //= 2
    planes, passed = [], []
    for i in range(len(waves) - 1):
        token, one = beside(token, i)
        local.append(one)
    for i, s in enumerate(waves):
        (keep,) = after(token, chips[i][0])
        outs = [shape(s.heads * s.quarter + s.tail + gain_rows(s), s.width)]
        columns = gains + others if gain_rows(s) else []
        (plane,) = call(
            bind(plane_kernel, s, reverse),
            outs,
            keep,
            chips[i][1],
            chip_received[i],
            *columns,
            deps=planes[-1:],
        )
        token = plane
        planes.append(plane)
        passed.append([next_plane(plane, s.count, reverse)])
    for i in range(len(local), len(waves)):
        token, one = beside(token, i)
        local.append(one)
    passed = [list(after(token, one[0])) for one in passed]
    for w in range(1, waves[0].window):
        for i, s in enumerate(waves):
            passed[i].append(pass_on(passed[i][-1], s.count, reverse, w))
    spreads, spread_received = [], []
    for i, s in enumerate(waves):
        (keep,) = after(token, chips[i][0])
        outs = [
            shape(s.heads * s.quarter, s.width),
            shape(s.heads * s.quarter + gain_rows(s), s.width),
        ]
        extra = []
        if gain_rows(s):
            outs.append(shape(gain_rows(s), s.width))
            extra = [planes[i]]
        spread = call(
            bind(spread_kernel, s, reverse),
            outs,
            keep,
            chips[i][1],
            chip_received[i],
            *passed[i],
            *extra,
        )
        token = spread[0]
        spreads.append(spread)
        spread_received.append(swap(spread[1], "seq", 2))
    entries = []
    for i, s in enumerate(waves):
        (keep,) = after(token, spreads[i][0])
        entry = call(
            bind(entry_kernel, s, reverse),
            [shape(s.heads * s.half, s.width)] * 2,
            keep,
            spread_received[i],
            parts[i][0],
            received[i],
            parts[i][2],
        )
        token = entry[0]
        entries.append((entry[0], swap(entry[1], "seq", 1)))
    return entries, local, token, [spreads[0][-1], spread_received[0]]


def per_device(queries, keys, values, out_grad, log_decay, norm_gain, doc_ids):
    tokens, features = queries.shape
    heads = log_decay.shape[1]
    count, dp = lax.axis_size("seq"), lax.axis_size("dp")
    wave_count = max(w for w in WAVES if heads % w == 0)
    waves = [Sizes(tokens, features, heads, count, w, wave_count) for w in range(wave_count)]
    bind = functools.partial
    unit = 2 * C * C * C * waves[0].blocks * waves[0].heads
    gain = norm_gain
    log_decay = log_decay.T
    states = []
    far = [pltpu.with_memory_space_constraint(a, pltpu.HBM) for a in (keys, values, log_decay, doc_ids)]
    for s in waves:
        groups = max(g for g in (3, 2, 1) if s.heads % g == 0)
        given = (keys, values, log_decay, doc_ids)
        spaces = [pltpu.VMEM, pltpu.VMEM, pltpu.VMEM, pltpu.SMEM]
        scratch = []
        if not states:
            given, spaces = far, [pltpu.HBM] * 4
            scratch = [
                pltpu.VMEM((tokens, s.columns), BF16),
                pltpu.VMEM((tokens, s.columns), BF16),
                pltpu.VMEM(log_decay.shape, F32),
                pltpu.SMEM(doc_ids.shape, jnp.int32),
                pltpu.SemaphoreType.DMA((2, groups)),
                pltpu.SemaphoreType.DMA((2,)),
            ]
        else:
            given = given[:2] + after(token, log_decay) + given[3:]
        state = call(
            bind(state_kernel, s),
            [
                shape(s.heads * s.half, s.width),
                shape(s.heads * s.half + s.tail, s.width),
                shape(s.notes, s.width),
                shape(max(1, s.blocks - 1) * s.heads * s.width, s.width),
            ],
            *given,
            flops=unit,
            spaces=spaces,
            scratch=scratch,
        )
        token = state[0]
        states.append(state)
    queries, keys, values, out_grad, gain, log_decay = after(
        token, queries, keys, values, out_grad, gain, log_decay
    )

    def beside_forward(token, i):
        s = waves[i]
        (held,) = after(token, log_decay)
        local = call(
            bind(local_kernel, s),
            [shape(tokens, s.columns), shape(s.blocks * s.heads * C, C, BF16)],
            queries,
            keys,
            values,
            held,
            gain,
            flops=2 * unit,
        )
        return local[0], local

    parts = [(state[0], state[1], state[2], None) for state in states]
    entries, local, token, _ = scan_in(waves, parts, False, token, beside_forward)
    attentions, sums = [], []
    for i, s in enumerate(waves):
        (held,) = after(token, log_decay)
        attention, total = call(
            bind(attention_kernel, s),
            [shape(tokens, s.columns), shape(8, tokens)],
            queries,
            out_grad,
            gain,
            held,
            states[i][2],
            local[i][0],
            states[i][3],
            *entries[i],
            *sums,
            flops=2 * unit,
        )
        token = attention
        attentions.append(attention)
        sums = [total]
    if dp & (dp - 1):
        sums = [lax.psum(sums[0], "dp")]
    else:
        bit = 1
        while bit < dp:
            total = sum(sums[1:], sums[0])
            sums = [total, swap(total, "dp", bit)]
            bit *= 2
    grads = []
    for i, s in enumerate(waves):
        (held,) = after(token, log_decay)
        grad = call(
            bind(grad_kernel, s, features * dp),
            [
                shape(tokens, s.columns, BF16),
                shape(s.heads * s.half, s.width),
                shape(s.heads * s.half + s.tail + s.gains, s.width),
                shape(s.tail, s.width),
                shape(s.gains, s.width),
                shape(max(1, s.blocks - 1) * s.heads * s.width, s.width),
            ],
            queries,
            out_grad,
            gain,
            held,
            states[i][2],
            attentions[i],
            *sums,
            flops=unit,
        )
        token = grad[0]
        grads.append(grad)

    def beside_backward(token, i):
        s = waves[i]
        (held,) = after(token, log_decay)
        local_grad = call(
            bind(local_grad_kernel, s),
            [shape(tokens, s.columns), shape(tokens, s.columns)],
            queries,
            values,
            held,
            local[i][1],
            grads[i][0],
            flops=3 * unit,
        )
        return local_grad[0], local_grad

    parts = [(grad[1], grad[2], grad[3], grad[4]) for grad in grads]
    entries, local_grads, token, gains = scan_in(waves, parts, True, token, beside_backward)
    done = []
    for i, s in enumerate(waves):
        last = i == wave_count - 1
        (held,) = after(token, log_decay)
        groups = max(g for g in (3, 2, 1) if s.heads % g == 0)
        given = [
            keys, values, held, states[i][2], *local_grads[i], grads[i][5], *entries[i], *done,
        ]
        scratch = []
        if last:
            given += gains
            outs = [pltpu.HBM((tokens, features), BF16)] * 2 + [pltpu.HBM((features,), F32)]
            out_spaces = [pltpu.HBM] * 3
            scratch = [
                pltpu.VMEM((features,), F32),
                pltpu.SemaphoreType.DMA((3, groups + i)),
                pltpu.VMEM((tokens, s.columns), BF16),
                pltpu.VMEM((tokens, s.columns), BF16),
            ]
        else:
            outs = [shape(tokens, s.columns, BF16)] * 2
            out_spaces = [pltpu.VMEM] * 2
        made = call(
            bind(final_kernel, s, wave_count),
            outs,
            *given,
            flops=4 * unit,
            out_spaces=out_spaces,
            scratch=scratch,
        )
        token = made[0]
        done += made
    return tuple(done[-3:])


def solution(mesh):
    placed = (
        P("seq", "dp"),
        P("seq", "dp"),
        P("seq", "dp"),
        P("seq", "dp"),
        P("seq", "dp"),
        P("dp"),
        P("seq"),
    )
    return jax.shard_map(
        per_device,
        mesh=mesh,
        in_specs=placed,
        out_specs=(P("seq", "dp"), P("seq", "dp"), P("dp")),
        check_vma=False,
    )
```

```python
import functools
import math

import jax
import jax.numpy as jnp
from jax import lax
from jax.experimental import pallas as pl
from jax.experimental.pallas import tpu as pltpu
from jax.sharding import PartitionSpec as P

C = 128
EPSILON = 1e-06
PLANE = 4
WAVES = (2, 1)
F32 = jnp.float32
BF16 = jnp.bfloat16


def dot(a, b, contract_a, contract_b):
    return lax.dot_general(
        a,
        b,
        (((contract_a,), (contract_b,)), ((), ())),
        preferred_element_type=F32,
    )


def two_parts(a):
    high = a.astype(BF16)
    return high, (a - high.astype(F32)).astype(BF16)


def far_dot(a, state, contract_state):
    parts = jnp.concatenate(two_parts(state), axis=contract_state)
    return dot(jnp.concatenate([a, a], axis=1), parts, 1, contract_state)


def equal(a, b):
    return (a == b).astype(F32)


def place_bits(count, reverse):
    place = lax.axis_index("seq")
    place = count - 1 - place if reverse else place
    return lax.rem(place, 2), lax.rem(place // 2, 2), place // PLANE


def triangle():
    row = lax.broadcasted_iota(jnp.int32, (C, C), 0)
    column = lax.broadcasted_iota(jnp.int32, (C, C), 1)
    return row, column


def sums_of(log_block, chosen, contract, log_first):
    parts, left = [], log_block
    for _ in range(3):
        parts.append(left.astype(BF16))
        left = left - parts[-1].astype(F32)
    chosen = chosen.astype(BF16)
    total = None
    for some in (parts[2:], parts[:2]):
        logs = jnp.concatenate(some, axis=1)
        which = jnp.concatenate([chosen] * len(some), axis=contract)
        if log_first:
            one = dot(logs, which, 1, contract)
        else:
            one = dot(which, logs, contract, 1)
        total = one if total is None else total + one
    return total


def decay_columns(log_block):
    row, column = triangle()
    return sums_of(log_block, (row >= column).astype(F32), 1, False)


def decay_rows(log_block):
    row, column = triangle()
    return sums_of(log_block, (row <= column).astype(F32), 0, True)


def total_rows(log_block):
    return sums_of(log_block, jnp.ones((C, C), F32), 0, True)


class Sizes:
    def __init__(self, tokens, features, all_heads, count, wave, waves):
        self.tokens, self.features, self.count = tokens, features, count
        self.heads = all_heads // waves
        self.first = wave * self.heads
        self.wave = wave
        self.blocks = tokens // C
        self.width = features // all_heads
        self.half = self.width // 2
        self.quarter = self.width // 4
        self.columns = self.heads * self.width
        self.planes = count // PLANE
        longest = self.blocks * count // 2
        per_plane = self.blocks * PLANE
        self.window = max(1, min(self.planes - 1, 1 + (longest - 2) // per_plane))
        self.gains = -(-self.heads // 8) * 8
        self.tail = -(-(self.heads + 2) // 8) * 8
        self.start, self.end = self.heads, self.heads + 1
        self.factors = self.heads + 2 + self.blocks
        self.notes = -(-(self.factors + self.blocks * self.heads) // 8) * 8

    def own(self, h):
        return slice(h * self.width, (h + 1) * self.width)

    def head(self, h):
        return self.own(self.first + h)

    def block(self, j):
        return slice(j * C, (j + 1) * C)

    def rows(self, h, size):
        return slice(h * size, (h + 1) * size)

    def carry(self, j):
        return slice(self.heads + 2 + j, self.heads + 3 + j)

    def factor(self, j, h):
        row = self.factors + j * self.heads + h
        return slice(row, row + 1)

    def logs(self, log_decay):
        return [
            log_decay[self.first : self.first + self.heads, self.block(j)]
            for j in range(self.blocks)
        ]


def call(kernel, outs, *args, flops=0, spaces=None, out_spaces=None, scratch=(), deps=()):
    moved = sum(math.prod(a.shape) * a.dtype.itemsize for a in (*args, *outs))
    spaces = spaces or [pltpu.VMEM] * len(args)
    out_spaces = out_spaces or [pltpu.VMEM] * len(outs)
    given = len(args)
    return pl.pallas_call(
        lambda *refs: kernel(*refs[:given], *refs[given + len(deps) :]),
        out_shape=outs,
        in_specs=[pl.BlockSpec(memory_space=p) for p in spaces + [pl.ANY] * len(deps)],
        out_specs=[pl.BlockSpec(memory_space=p) for p in out_spaces],
        compiler_params=pltpu.CompilerParams(vmem_limit_bytes=moved + (4 << 20)),
        cost_estimate=pl.CostEstimate(flops=flops, bytes_accessed=moved, transcendentals=0),
        scratch_shapes=scratch,
    )(*args, *deps)


def after(token, *values):
    return lax.optimization_barrier((token,) + values)[1:]


def shape(rows, columns, dtype=F32):
    return jax.ShapeDtypeStruct((rows, columns), dtype)


def put_tail(s, tail_ref, base, factors, start, end):
    tail_ref[base : base + s.heads, :] = factors
    tail_ref[base + s.start : base + s.start + 1, :] = start
    tail_ref[base + s.end : base + s.end + 1, :] = end


def put_parts(first, size, h, whole, keep_ref, send_ref):
    low, high = whole[:size], whole[size:]
    rows = slice(h * size, (h + 1) * size)
    keep_ref[rows, :] = lax.select(first, low, high)
    send_ref[rows, :] = lax.select(first, high, low)


def state_kernel(
    s, keys, values, log_decay, doc_ids, keep, send, notes, cums, first_update, *near
):
    each, waits, first = s.heads, [], s.first
    if near:
        near_keys, near_values, near_logs, near_ids, arrived, small = near
        few = [
            pltpu.make_async_copy(doc_ids, near_ids, small.at[0]),
            pltpu.make_async_copy(log_decay, near_logs, small.at[1]),
        ]
        each = s.heads // arrived.shape[1]
        for g in range(arrived.shape[1]):
            far_part = pl.ds((s.first + g * each) * s.width, each * s.width)
            part = pl.ds(g * each * s.width, each * s.width)
            waits.append(
                [
                    pltpu.make_async_copy(keys.at[:, far_part], near_keys.at[:, part], arrived.at[0, g]),
                    pltpu.make_async_copy(
                        values.at[:, far_part], near_values.at[:, part], arrived.at[1, g]
                    ),
                ]
            )
        for copy in few + sum(waits, []):
            copy.start()
        for copy in few:
            copy.wait()
        keys, values, log_decay, doc_ids, first = near_keys, near_values, near_logs, near_ids, 0
    core, _, _ = place_bits(s.count, False)
    lower = core == 0
    if near:
        docs = [jnp.full((1, s.width), doc_ids[j].astype(F32)) for j in range(s.blocks)]
        carries = [None] + [equal(docs[j - 1], docs[j]) for j in range(1, s.blocks)]
    else:
        docs = [doc_ids[s.start : s.start + 1, :], doc_ids[s.end : s.end + 1, :]]
        carries = [doc_ids[s.carry(j), :] for j in range(s.blocks)]
    logs = s.logs(log_decay)
    totals = [total_rows(a) for a in logs]
    factors = [jnp.exp(t) for t in totals]
    whole_factor = factors[0]
    for j in range(1, s.blocks):
        whole_factor = whole_factor * factors[j] * carries[j]
    base = s.heads * s.half
    send[base:, :] = jnp.zeros((s.tail, s.width), F32)
    put_tail(s, send, base, whole_factor, docs[0], docs[-1])
    notes[...] = jnp.zeros(notes.shape, F32)
    put_tail(s, notes, 0, whole_factor, docs[0], docs[-1])
    for j in range(1, s.blocks):
        notes[s.carry(j), :] = carries[j]
    for j, rows in enumerate(factors):
        notes[s.factor(j, 0).start : s.factor(j, 0).start + s.heads, :] = rows
    columns = [decay_columns(a) for a in logs]
    ends = [jnp.exp(a[C - 1 : C, :] - a) for a in columns]
    for j, column in enumerate(columns):
        cums[s.block(j), :] = column
    for h in range(s.heads):
        if waits and h % each == 0:
            for copy in waits[h // each]:
                copy.wait()
        place = slice((first + h) * s.width, (first + h + 1) * s.width)
        state = None
        for j in range(s.blocks):
            scaled = keys[s.block(j), place].astype(F32) * ends[j][:, h : h + 1]
            update = dot(scaled.astype(BF16), values[s.block(j), place], 0, 0)
            if j < s.blocks - 1:
                first_update[s.rows(j * s.heads + h, s.width), :] = update
            if state is None:
                state = update
            else:
                state = (carries[j] * factors[j][h : h + 1, :]) * state + update
        put_parts(lower, s.half, h, state, keep, send)


def sides(first, own, other):
    return lax.select(first, own, other), lax.select(first, other, own)


def linked(s, far, near):
    return equal(far[s.end : s.end + 1, :], near[s.start : s.start + 1, :])


def join_tail(s, out, base, far, near, factor):
    out[base : base + s.tail, :] = jnp.zeros((s.tail, s.width), F32)
    put_tail(
        s,
        out,
        base,
        far[: s.heads, :] * factor,
        far[s.start : s.start + 1, :],
        near[s.end : s.end + 1, :],
    )


def chip_kernel(s, reverse, keep, received, own_tail, *rest):
    out_keep, out_send = rest[-3:-1] if reverse else rest
    core, chip, _ = place_bits(s.count, reverse)
    lower, left = core == 0, chip == 0
    base, top = s.heads * s.half, s.heads * s.quarter
    far, near = sides(lower, own_tail[: s.tail, :], received[base : base + s.tail, :])
    factor = near[: s.heads, :] * linked(s, far, near)
    join_tail(s, out_send, top, far, near, factor)
    if reverse:
        gain = rest[0][...] + received[base + s.tail :, :]
        every = rest[-1]
        if s.wave:
            every[: -s.gains, :] = rest[1][...]
        every[every.shape[0] - s.gains :, :] = gain
    for h in range(s.heads):
        rows = s.rows(h, s.half)
        far_state, near_state = sides(lower, keep[rows, :], received[rows, :])
        total = near_state + factor[h : h + 1, :] * far_state
        put_parts(left, s.quarter, h, total, out_keep, out_send)


def plane_kernel(s, reverse, keep, sent, received, *rest):
    columns, out = rest[:-1], rest[-1]
    _, chip, _ = place_bits(s.count, reverse)
    left = chip == 0
    top = s.heads * s.quarter
    far, near = sides(left, sent[top:, :], received[top:, :])
    factor = near[: s.heads, :] * linked(s, far, near)
    join_tail(s, out, top, far, near, factor)
    if columns:
        out[top + s.tail :, :] = sum([a[...] for a in columns[1:]], columns[0][...])
    for h in range(s.heads):
        rows = s.rows(h, s.quarter)
        far_state, near_state = sides(left, keep[rows, :], received[rows, :])
        out[rows, :] = near_state + factor[h : h + 1, :] * far_state


def spread_kernel(s, reverse, keep, sent, received, *rest):
    earlier, rest = rest[: s.window], rest[s.window :]
    out_keep, out_send = rest[1:3] if rest[2:] else rest
    _, chip, plane = place_bits(s.count, reverse)
    left = chip == 0
    top = s.heads * s.quarter
    far, near = sides(left, sent[top:, :], received[top:, :])
    tails = [ref[top : top + s.tail, :] for ref in earlier]
    reach = [(plane >= w + 1).astype(F32) for w in range(s.window)]
    entry = linked(s, tails[0], far) * reach[0]
    inner = [
        linked(s, tails[w + 1], tails[w]) * reach[w + 1] * tails[w][: s.heads, :]
        for w in range(s.window - 1)
    ]
    link = linked(s, far, near)
    far_factor = far[: s.heads, :]
    if rest[2:]:
        gain = rest[0][top + s.tail :, :]
        if s.planes > 1:
            gain = gain + earlier[0][top + s.tail :, :]
        rest[3][...] = gain
        out_send[top:, :] = gain
    for h in range(s.heads):
        rows, one = s.rows(h, s.quarter), slice(h, h + 1)
        state = earlier[-1][rows, :]
        for w in reversed(range(s.window - 1)):
            state = earlier[w][rows, :] + inner[w][one] * state
        into_far = entry * state
        far_state = lax.select(left, keep[rows, :], received[rows, :])
        into_near = link * (far_state + far_factor[one] * into_far)
        out_keep[rows, :] = lax.select(left, into_far, into_near)
        out_send[rows, :] = lax.select(left, into_near, into_far)


def entry_kernel(
    s, reverse, chip_keep, chip_received, keep, received, own_tail, out_keep, out_send
):
    core, chip, _ = place_bits(s.count, reverse)
    lower, left = core == 0, chip == 0
    base = s.heads * s.half
    far, near = sides(lower, own_tail[: s.tail, :], received[base : base + s.tail, :])
    link = linked(s, far, near)
    far_factor = far[: s.heads, :]
    for h in range(s.heads):
        rows, quarter = s.rows(h, s.half), s.rows(h, s.quarter)
        into_far = jnp.concatenate(
            sides(left, chip_keep[quarter, :], chip_received[quarter, :]), axis=0
        )
        far_state = lax.select(lower, keep[rows, :], received[rows, :])
        into_near = link * (far_state + far_factor[h : h + 1, :] * into_far)
        out_keep[rows, :] = lax.select(lower, into_far, into_near)
        out_send[rows, :] = lax.select(lower, into_near, into_far)


def joined(s, lower, keep, received, h):
    rows = s.rows(h, s.half)
    return jnp.concatenate(sides(lower, keep[rows, :], received[rows, :]), axis=0)


def decay_mask(column, row):
    at, other = triangle()
    gap = jnp.minimum(column - row, 0.0)
    return jnp.where(at >= other, jnp.exp(gap), 0.0)


def local_kernel(s, queries, keys, values, log_decay, cums, gain, out, weights):
    for j, logs in enumerate(s.logs(log_decay)):
        columns, rows = cums[s.block(j), :], decay_rows(logs)
        for h in range(s.heads):
            mask = decay_mask(columns[:, h : h + 1], rows[h : h + 1, :])
            part = (s.block(j), s.head(h))
            scores = dot(queries[part], keys[part], 1, 1)
            weight = (scores * mask).astype(BF16)
            weights[s.rows(j * s.heads + h, C), :] = weight
            out[s.block(j), s.own(h)] = dot(weight, values[part], 1, 0)


def attention_kernel(
    s, queries, out_grad, gain, cums, notes, local, first_update, keep, received, *rest
):
    earlier_sums, (out, sums) = rest[:-2], rest[-2:]
    core, _, _ = place_bits(s.count, False)
    lower = core == 0
    decays = [jnp.exp(cums[s.block(j), :]) for j in range(s.blocks)]
    squares = [jnp.zeros((C, s.width), F32) for _ in decays]
    inners = [jnp.zeros((C, s.width), F32) for _ in decays]
    for h in range(s.heads):
        state = joined(s, lower, keep, received, h)
        for j in range(s.blocks):
            part, own = (s.block(j), s.head(h)), (s.block(j), s.own(h))
            far = far_dot(queries[part], state, 0)
            attention = local[own] + decays[j][:, h : h + 1] * far
            out[own] = attention
            squares[j] = squares[j] + attention * attention
            inners[j] = inners[j] + out_grad[part].astype(F32) * gain[s.head(h)].reshape(1, s.width) * attention
            if j < s.blocks - 1:
                update = first_update[s.rows(j * s.heads + h, s.width), :]
                state = notes[s.carry(j + 1), :] * (notes[s.factor(j, h), :] * state + update)
    if earlier_sums:
        sums[...] = earlier_sums[0][...]
    else:
        sums[...] = jnp.zeros(sums.shape, F32)
    for j in range(s.blocks):
        for i, part in enumerate([squares[j], inners[j]]):
            row = (slice(i, i + 1), s.block(j))
            sums[row] = sums[row] + jnp.sum(part.T, axis=0, keepdims=True)


def grad_kernel(
    s, all_features, queries, out_grad, gain, cums, notes, attention, *rest
):
    sums, (attn_grad, keep, send, out_tail, out_gain, back_terms) = rest[:-6], rest[-6:]
    core, _, _ = place_bits(s.count, True)
    lower = core == 0
    decays = [jnp.exp(cums[s.block(j), :]) for j in range(s.blocks)]
    totals = sum([a[...] for a in sums[1:]], sums[0][...]) / all_features
    spread = lambda row: jnp.broadcast_to(row, (C, C)).T
    inverses, slopes = [], []
    for j in range(s.blocks):
        inverse = lax.rsqrt(totals[0:1, s.block(j)] + EPSILON)
        inverses.append(spread(inverse))
        slopes.append(spread(totals[1:2, s.block(j)] * inverse * inverse))
    base = s.heads * s.half
    out_tail[...] = jnp.zeros(out_tail.shape, F32)
    own = notes[: s.tail, :]
    put_tail(
        s, out_tail, 0, own[: s.heads], own[s.end : s.end + 1], own[s.start : s.start + 1]
    )
    out_gain[...] = jnp.zeros(out_gain.shape, F32)
    for h in range(s.heads):
        gain_row = gain[s.head(h)].reshape(1, s.width)
        gain_part = jnp.zeros((1, s.width), F32)
        terms = []
        for j in range(s.blocks):
            part, own = (s.block(j), s.head(h)), (s.block(j), s.own(h))
            cot = out_grad[part].astype(F32)
            att = attention[own]
            grad = ((cot * gain_row - att * slopes[j]) * inverses[j]).astype(BF16)
            attn_grad[own] = grad
            gain_part = gain_part + jnp.sum(cot * att * inverses[j], axis=0, keepdims=True)
            weighted = (queries[part].astype(F32) * decays[j][:, h : h + 1]).astype(BF16)
            term = dot(weighted, grad, 0, 0)
            terms.append(term)
            if j > 0:
                back_terms[s.rows((j - 1) * s.heads + h, s.width), :] = term
        state = terms[-1]
        for j in reversed(range(s.blocks - 1)):
            state = terms[j] + (notes[s.carry(j + 1), :] * notes[s.factor(j, h), :]) * state
        put_parts(lower, s.half, h, state, keep, send)
        out_gain[h : h + 1, :] = gain_part
    send[base : base + s.tail, :] = out_tail[...]
    send[base + s.tail :, :] = out_gain[...]


def local_grad_kernel(
    s, queries, values, log_decay, cums, weights, attn_grad, key_out, value_out
):
    for j, logs in enumerate(s.logs(log_decay)):
        columns, rows = cums[s.block(j), :], decay_rows(logs)
        for h in range(s.heads):
            mask = decay_mask(columns[:, h : h + 1], rows[h : h + 1, :])
            part, own = (s.block(j), s.head(h)), (s.block(j), s.own(h))
            grad = attn_grad[own]
            grad_weight = (dot(grad, values[part], 1, 1) * mask).astype(BF16)
            key_out[own] = dot(grad_weight, queries[part], 0, 0)
            value_out[own] = dot(weights[s.rows(j * s.heads + h, C), :], grad, 0, 0)


def final_kernel(s, waves, keys, values, cums, notes, key_local, value_local, back_terms, *rest):
    keep, received = rest[:2]
    last = s.wave == waves - 1
    near_outs = rest[-2:]
    copies = []
    if last:
        *far_outs, far_gain, near_gain, sent = rest[-7:-2]
        groups = sent.shape[1] - s.wave
        own, other = rest[2 + 2 * s.wave : 4 + 2 * s.wave]
        base = s.heads * s.quarter
        for w in range(waves):
            for h in range(s.heads):
                row = w * s.gains + h
                total = own[row : row + 1, :] + other[base + row : base + row + 1, :]
                place = (w * s.heads + h) * s.width
                near_gain[place : place + s.width] = total.reshape(s.width)
        copies.append(pltpu.make_async_copy(near_gain, far_gain, sent.at[2, 0]))
        copies[-1].start()
        for w in range(s.wave):
            place = pl.ds(w * s.columns, s.columns)
            for i, far in enumerate(far_outs):
                near = rest[2 + 2 * w + i]
                copies.append(
                    pltpu.make_async_copy(near, far.at[:, place], sent.at[i, groups + w])
                )
                copies[-1].start()
    core, _, _ = place_bits(s.count, True)
    lower = core == 0
    columns = [cums[s.block(j), :] for j in range(s.blocks)]
    ends = [jnp.exp(a[C - 1 : C, :] - a) for a in columns]
    for h in range(s.heads):
        state = joined(s, lower, keep, received, h)
        for j in reversed(range(s.blocks)):
            part, own = (s.block(j), s.head(h)), (s.block(j), s.own(h))
            end = ends[j][:, h : h + 1]
            key_far = end * far_dot(values[part], state, 1)
            value_far = end * far_dot(keys[part], state, 0)
            near_outs[0][own] = (key_local[own] + key_far).astype(BF16)
            near_outs[1][own] = (value_local[own] + value_far).astype(BF16)
            if j > 0:
                term = back_terms[s.rows((j - 1) * s.heads + h, s.width), :]
                state = notes[s.carry(j), :] * (term + notes[s.factor(j, h), :] * state)
        if last and (h + 1) * groups % s.heads == 0:
            each, g = s.heads // groups, h * groups // s.heads
            part = pl.ds(g * each * s.width, each * s.width)
            far_part = pl.ds((s.first + g * each) * s.width, each * s.width)
            for i, (near, far) in enumerate(zip(near_outs, far_outs)):
                copies.append(
                    pltpu.make_async_copy(near.at[:, part], far.at[:, far_part], sent.at[i, g])
                )
                copies[-1].start()
    for copy in copies:
        copy.wait()


def swap(value, axis, bit):
    count = lax.axis_size(axis)
    return lax.ppermute(value, axis, [(i, i ^ bit) for i in range(count)])


def next_plane(value, count, reverse):
    step = -PLANE if reverse else PLANE
    return lax.ppermute(value, "seq", [(i, (i + step) % count) for i in range(count)])


def pass_on(value, count, reverse, behind):
    planes = count // PLANE
    pairs = []
    for source in range(count):
        plane, place = divmod(source, PLANE)
        if plane < behind:
            target = source ^ 2
        else:
            target = (plane + 1 if plane < planes - 1 else behind) * PLANE + place
        pair = (source, target)
        pairs.append(tuple(count - 1 - a for a in pair) if reverse else pair)
    return lax.ppermute(value, "seq", pairs)


def scan_in(waves, parts, reverse, token, beside):
    bind = functools.partial
    gain_rows = lambda s: len(waves) * s.gains if reverse and s.wave == 0 else 0
    received, chips, chip_received, local, gains, others = [], [], [], [], [], []
    for s, (keep, send, tail, gain) in zip(waves, parts):
        received.append(swap(send, "seq", 1))
    for i, (s, (keep, send, tail, gain)) in enumerate(zip(waves, parts)):
        outs = [
            shape(s.heads * s.quarter, s.width),
            shape(s.heads * s.quarter + s.tail, s.width),
        ]
        (keep,) = after(token, keep)
        extra = []
        if reverse:
            extra = [gain, *gains]
            outs.append(shape((i + 1) * s.gains, s.width))
        *chip, = call(bind(chip_kernel, s, reverse), outs, keep, received[i], tail, *extra)
        gains = chip[2:]
        token = chip[0]
        chips.append(chip)
        chip_received.append(swap(chip[1], "seq", 2))
    if reverse:
        bit = waves[0].count // 2
        while bit > PLANE:
            if others:
                gains, others = [gains[0] + others[0]], []
            others = [swap(gains[0], "seq", bit + 1)]
            bit //= 2
    planes, passed = [], []
    for i in range(len(waves) - 1):
        token, one = beside(token, i)
        local.append(one)
    for i, s in enumerate(waves):
        (keep,) = after(token, chips[i][0])
        outs = [shape(s.heads * s.quarter + s.tail + gain_rows(s), s.width)]
        columns = gains + others if gain_rows(s) else []
        (plane,) = call(
            bind(plane_kernel, s, reverse),
            outs,
            keep,
            chips[i][1],
            chip_received[i],
            *columns,
            deps=planes[-1:],
        )
        token = plane
        planes.append(plane)
        passed.append([next_plane(plane, s.count, reverse)])
    for i in range(len(local), len(waves)):
        token, one = beside(token, i)
        local.append(one)
    passed = [list(after(token, one[0])) for one in passed]
    for w in range(1, waves[0].window):
        for i, s in enumerate(waves):
            passed[i].append(pass_on(passed[i][-1], s.count, reverse, w))
    spreads, spread_received = [], []
    for i, s in enumerate(waves):
        (keep,) = after(token, chips[i][0])
        outs = [
            shape(s.heads * s.quarter, s.width),
            shape(s.heads * s.quarter + gain_rows(s), s.width),
        ]
        extra = []
        if gain_rows(s):
            outs.append(shape(gain_rows(s), s.width))
            extra = [planes[i]]
        spread = call(
            bind(spread_kernel, s, reverse),
            outs,
            keep,
            chips[i][1],
            chip_received[i],
            *passed[i],
            *extra,
        )
        token = spread[0]
        spreads.append(spread)
        spread_received.append(swap(spread[1], "seq", 2))
    entries = []
    for i, s in enumerate(waves):
        (keep,) = after(token, spreads[i][0])
        entry = call(
            bind(entry_kernel, s, reverse),
            [shape(s.heads * s.half, s.width)] * 2,
            keep,
            spread_received[i],
            parts[i][0],
            received[i],
            parts[i][2],
        )
        token = entry[0]
        entries.append((entry[0], swap(entry[1], "seq", 1)))
    return entries, local, token, [spreads[0][-1], spread_received[0]]


def per_device(queries, keys, values, out_grad, log_decay, norm_gain, doc_ids):
    tokens, features = queries.shape
    heads = log_decay.shape[1]
    count, dp = lax.axis_size("seq"), lax.axis_size("dp")
    wave_count = max(w for w in WAVES if heads % w == 0)
    waves = [Sizes(tokens, features, heads, count, w, wave_count) for w in range(wave_count)]
    bind = functools.partial
    unit = 2 * C * C * C * waves[0].blocks * waves[0].heads
    gain = norm_gain
    log_decay = log_decay.T
    states = []
    far = [pltpu.with_memory_space_constraint(a, pltpu.HBM) for a in (keys, values, log_decay, doc_ids)]
    for s in waves:
        groups = max(g for g in (3, 2, 1) if s.heads % g == 0)
        given = (keys, values, log_decay, doc_ids)
        spaces = [pltpu.VMEM] * 4
        scratch = []
        if not states:
            given, spaces = far, [pltpu.HBM] * 4
            scratch = [
                pltpu.VMEM((tokens, s.columns), BF16),
                pltpu.VMEM((tokens, s.columns), BF16),
                pltpu.VMEM(log_decay.shape, F32),
                pltpu.SMEM(doc_ids.shape, jnp.int32),
                pltpu.SemaphoreType.DMA((2, groups)),
                pltpu.SemaphoreType.DMA((2,)),
            ]
        else:
            given = (keys, values, log_decay, states[0][2])
        state = call(
            bind(state_kernel, s),
            [
                shape(s.heads * s.half, s.width),
                shape(s.heads * s.half + s.tail, s.width),
                shape(s.notes, s.width),
                shape(tokens, s.heads),
                shape(max(1, s.blocks - 1) * s.heads * s.width, s.width),
            ],
            *given,
            flops=unit,
            spaces=spaces,
            scratch=scratch,
        )
        token = state[0]
        states.append(state)
    queries, keys, values, out_grad, gain, log_decay = after(
        token, queries, keys, values, out_grad, gain, log_decay
    )

    def beside_forward(token, i):
        s = waves[i]
        (held,) = after(token, log_decay)
        local = call(
            bind(local_kernel, s),
            [shape(tokens, s.columns), shape(s.blocks * s.heads * C, C, BF16)],
            queries,
            keys,
            values,
            held,
            states[i][3],
            gain,
            flops=2 * unit,
        )
        return local[0], local

    parts = [(state[0], state[1], state[2], None) for state in states]
    entries, local, token, _ = scan_in(waves, parts, False, token, beside_forward)
    attentions, sums = [], []
    for i, s in enumerate(waves):
        attention, total = call(
            bind(attention_kernel, s),
            [shape(tokens, s.columns), shape(8, tokens)],
            queries,
            out_grad,
            gain,
            states[i][3],
            states[i][2],
            local[i][0],
            states[i][4],
            *entries[i],
            *sums,
            flops=2 * unit,
        )
        token = attention
        attentions.append(attention)
        sums = [total]
    if dp & (dp - 1):
        sums = [lax.psum(sums[0], "dp")]
    else:
        bit = 1
        while bit < dp:
            total = sum(sums[1:], sums[0])
            sums = [total, swap(total, "dp", bit)]
            bit *= 2
    grads = []
    for i, s in enumerate(waves):
        grad = call(
            bind(grad_kernel, s, features * dp),
            [
                shape(tokens, s.columns, BF16),
                shape(s.heads * s.half, s.width),
                shape(s.heads * s.half + s.tail + s.gains, s.width),
                shape(s.tail, s.width),
                shape(s.gains, s.width),
                shape(max(1, s.blocks - 1) * s.heads * s.width, s.width),
            ],
            queries,
            out_grad,
            gain,
            states[i][3],
            states[i][2],
            attentions[i],
            *sums,
            flops=unit,
        )
        token = grad[0]
        grads.append(grad)

    def beside_backward(token, i):
        s = waves[i]
        (held,) = after(token, log_decay)
        local_grad = call(
            bind(local_grad_kernel, s),
            [shape(tokens, s.columns), shape(tokens, s.columns)],
            queries,
            values,
            held,
            states[i][3],
            local[i][1],
            grads[i][0],
            flops=3 * unit,
        )
        return local_grad[0], local_grad

    parts = [(grad[1], grad[2], grad[3], grad[4]) for grad in grads]
    entries, local_grads, token, gains = scan_in(waves, parts, True, token, beside_backward)
    done = []
    for i, s in enumerate(waves):
        last = i == wave_count - 1
        (held,) = after(token, log_decay)
        groups = max(g for g in (3, 2, 1) if s.heads % g == 0)
        given = [
            keys, values, states[i][3], states[i][2], *local_grads[i], grads[i][5], *entries[i], *done,
        ]
        scratch = []
        if last:
            given += gains
            outs = [pltpu.HBM((tokens, features), BF16)] * 2 + [pltpu.HBM((features,), F32)]
            out_spaces = [pltpu.HBM] * 3
            scratch = [
                pltpu.VMEM((features,), F32),
                pltpu.SemaphoreType.DMA((3, groups + i)),
                pltpu.VMEM((tokens, s.columns), BF16),
                pltpu.VMEM((tokens, s.columns), BF16),
            ]
        else:
            outs = [shape(tokens, s.columns, BF16)] * 2
            out_spaces = [pltpu.VMEM] * 2
        made = call(
            bind(final_kernel, s, wave_count),
            outs,
            *given,
            flops=4 * unit,
            out_spaces=out_spaces,
            scratch=scratch,
        )
        token = made[0]
        done += made
    return tuple(done[-3:])


def solution(mesh):
    placed = (
        P("seq", "dp"),
        P("seq", "dp"),
        P("seq", "dp"),
        P("seq", "dp"),
        P("seq", "dp"),
        P("dp"),
        P("seq"),
    )
    return jax.shard_map(
        per_device,
        mesh=mesh,
        in_specs=placed,
        out_specs=(P("seq", "dp"), P("seq", "dp"), P("dp")),
        check_vma=False,
    )
```

```python
import functools
import math

import jax
import jax.numpy as jnp
from jax import lax
from jax.experimental import pallas as pl
from jax.experimental.pallas import tpu as pltpu
from jax.sharding import PartitionSpec as P

C = 128
EPSILON = 1e-06
PLANE = 4
SECOND_WAVE = 0.5
LOADED, STORED = 6, 3
F32 = jnp.float32
BF16 = jnp.bfloat16


def dot(a, b, contract_a, contract_b):
    return lax.dot_general(
        a,
        b,
        (((contract_a,), (contract_b,)), ((), ())),
        preferred_element_type=F32,
    )


def two_parts(a):
    high = a.astype(BF16)
    return high, (a - high.astype(F32)).astype(BF16)


def far_dot(a, state, contract_state):
    parts = jnp.concatenate(two_parts(state), axis=contract_state)
    return dot(jnp.concatenate([a, a], axis=1), parts, 1, contract_state)


def equal(a, b):
    return (a == b).astype(F32)


def place_bits(count, reverse):
    place = lax.axis_index("seq")
    place = count - 1 - place if reverse else place
    return lax.rem(place, 2), lax.rem(place // 2, 2), place // PLANE


def triangle():
    row = lax.broadcasted_iota(jnp.int32, (C, C), 0)
    column = lax.broadcasted_iota(jnp.int32, (C, C), 1)
    return row, column


def sums_of(log_block, chosen, contract, log_first):
    parts, left = [], log_block
    for _ in range(3):
        parts.append(left.astype(BF16))
        left = left - parts[-1].astype(F32)
    chosen = chosen.astype(BF16)
    total = None
    for some in (parts[2:], parts[:2]):
        logs = jnp.concatenate(some, axis=1)
        which = jnp.concatenate([chosen] * len(some), axis=contract)
        if log_first:
            one = dot(logs, which, 1, contract)
        else:
            one = dot(which, logs, contract, 1)
        total = one if total is None else total + one
    return total


def decay_columns(log_block):
    row, column = triangle()
    return sums_of(log_block, (row >= column).astype(F32), 1, False)


def decay_rows(log_block):
    row, column = triangle()
    return sums_of(log_block, (row <= column).astype(F32), 0, True)


def total_rows(log_block):
    return sums_of(log_block, jnp.ones((C, C), F32), 0, True)


class Sizes:
    def __init__(self, tokens, features, all_heads, count, wave, first, heads):
        self.tokens, self.features, self.count = tokens, features, count
        self.heads, self.first, self.wave = heads, first, wave
        self.blocks = tokens // C
        self.width = features // all_heads
        self.half = self.width // 2
        self.quarter = self.width // 4
        self.columns = self.heads * self.width
        self.planes = count // PLANE
        longest = self.blocks * count // 2
        per_plane = self.blocks * PLANE
        self.window = max(1, min(self.planes - 1, 1 + (longest - 2) // per_plane))
        self.gains = -(-self.heads // 8) * 8
        self.tail = -(-(self.heads + 2) // 8) * 8
        self.start, self.end = self.heads, self.heads + 1
        self.factors = self.heads + 2 + self.blocks
        self.notes = -(-(self.factors + self.blocks * self.heads) // 8) * 8

    def own(self, h):
        return slice(h * self.width, (h + 1) * self.width)

    def head(self, h):
        return self.own(self.first + h)

    def block(self, j):
        return slice(j * C, (j + 1) * C)

    def rows(self, h, size):
        return slice(h * size, (h + 1) * size)

    def groups(self, most):
        edges = [*range(0, self.heads, most), self.heads]
        return [(a, b, pl.ds(a * self.width, (b - a) * self.width),
                 pl.ds((self.first + a) * self.width, (b - a) * self.width))
                for a, b in zip(edges[:-1], edges[1:])]

    def carry(self, j):
        return slice(self.heads + 2 + j, self.heads + 3 + j)

    def factor(self, j, h):
        row = self.factors + j * self.heads + h
        return slice(row, row + 1)

    def logs(self, log_decay):
        return [
            log_decay[self.first : self.first + self.heads, self.block(j)]
            for j in range(self.blocks)
        ]


def call(kernel, outs, *args, flops=0, spaces=None, out_spaces=None, scratch=(), deps=()):
    moved = sum(math.prod(a.shape) * a.dtype.itemsize for a in (*args, *outs))
    spaces = spaces or [pltpu.VMEM] * len(args)
    out_spaces = out_spaces or [pltpu.VMEM] * len(outs)
    given = len(args)
    return pl.pallas_call(
        lambda *refs: kernel(*refs[:given], *refs[given + len(deps) :]),
        out_shape=outs,
        in_specs=[pl.BlockSpec(memory_space=p) for p in spaces + [pl.ANY] * len(deps)],
        out_specs=[pl.BlockSpec(memory_space=p) for p in out_spaces],
        compiler_params=pltpu.CompilerParams(vmem_limit_bytes=moved + (4 << 20)),
        cost_estimate=pl.CostEstimate(flops=flops, bytes_accessed=moved, transcendentals=0),
        scratch_shapes=scratch,
    )(*args, *deps)


def after(token, *values):
    return lax.optimization_barrier((token,) + values)[1:]


def shape(rows, columns, dtype=F32):
    return jax.ShapeDtypeStruct((rows, columns), dtype)


def put_tail(s, tail_ref, base, factors, start, end):
    tail_ref[base : base + s.heads, :] = factors
    tail_ref[base + s.start : base + s.start + 1, :] = start
    tail_ref[base + s.end : base + s.end + 1, :] = end


def put_parts(first, size, h, whole, keep_ref, send_ref):
    low, high = whole[:size], whole[size:]
    rows = slice(h * size, (h + 1) * size)
    keep_ref[rows, :] = lax.select(first, low, high)
    send_ref[rows, :] = lax.select(first, high, low)


def state_kernel(
    s, told, keys, values, log_decay, doc_ids, keep, send, notes, cums, first_update, *near
):
    waits, first = {}, s.first
    if near:
        near_keys, near_values, near_logs, near_ids, arrived, small = near
        ids_copy = pltpu.make_async_copy(doc_ids, near_ids, small.at[0])
        logs_copy = pltpu.make_async_copy(log_decay, near_logs, small.at[1])
        for g, (a, _, part, far_part) in enumerate(s.groups(LOADED)):
            waits[a] = [
                pltpu.make_async_copy(far.at[:, far_part], close.at[:, part], arrived.at[i, g])
                for i, (far, close) in enumerate([(keys, near_keys), (values, near_values)])
            ]
        for copy in [logs_copy, ids_copy] + sum(waits.values(), []):
            copy.start()
        logs_copy.wait()
        keys, values, log_decay, doc_ids, first = near_keys, near_values, near_logs, near_ids, 0
    core, _, _ = place_bits(s.count, False)
    lower = core == 0
    logs = s.logs(log_decay)
    totals = [total_rows(a) for a in logs]
    factors = [jnp.exp(t) for t in totals]
    columns = [decay_columns(a) for a in logs]
    ends = [jnp.exp(a[C - 1 : C, :] - a) for a in columns]
    for j, column in enumerate(columns):
        cums[s.block(j), :] = column
    if near:
        ids_copy.wait()
        docs = [jnp.full((1, s.width), doc_ids[j].astype(F32)) for j in range(s.blocks)]
        carries = [None] + [equal(docs[j - 1], docs[j]) for j in range(1, s.blocks)]
    else:
        docs = [doc_ids[told.start : told.start + 1, :], doc_ids[told.end : told.end + 1, :]]
        carries = [doc_ids[told.carry(j), :] for j in range(s.blocks)]
    whole_factor = factors[0]
    for j in range(1, s.blocks):
        whole_factor = whole_factor * factors[j] * carries[j]
    base = s.heads * s.half
    send[base:, :] = jnp.zeros((s.tail, s.width), F32)
    put_tail(s, send, base, whole_factor, docs[0], docs[-1])
    notes[...] = jnp.zeros(notes.shape, F32)
    put_tail(s, notes, 0, whole_factor, docs[0], docs[-1])
    for j in range(1, s.blocks):
        notes[s.carry(j), :] = carries[j]
    for j, rows in enumerate(factors):
        notes[s.factor(j, 0).start : s.factor(j, 0).start + s.heads, :] = rows
    for h in range(s.heads):
        for copy in waits.get(h, ()):
            copy.wait()
        place = slice((first + h) * s.width, (first + h + 1) * s.width)
        state = None
        for j in range(s.blocks):
            scaled = keys[s.block(j), place].astype(F32) * ends[j][:, h : h + 1]
            update = dot(scaled.astype(BF16), values[s.block(j), place], 0, 0)
            if j < s.blocks - 1:
                first_update[s.rows(j * s.heads + h, s.width), :] = update
            if state is None:
                state = update
            else:
                state = (carries[j] * factors[j][h : h + 1, :]) * state + update
        put_parts(lower, s.half, h, state, keep, send)


def sides(first, own, other):
    return lax.select(first, own, other), lax.select(first, other, own)


def linked(s, far, near):
    return equal(far[s.end : s.end + 1, :], near[s.start : s.start + 1, :])


def join_tail(s, out, base, far, near, factor):
    out[base : base + s.tail, :] = jnp.zeros((s.tail, s.width), F32)
    put_tail(
        s,
        out,
        base,
        far[: s.heads, :] * factor,
        far[s.start : s.start + 1, :],
        near[s.end : s.end + 1, :],
    )


def chip_kernel(s, reverse, keep, received, own_tail, *rest):
    out_keep, out_send = rest[-3:-1] if reverse else rest
    core, chip, _ = place_bits(s.count, reverse)
    lower, left = core == 0, chip == 0
    base, top = s.heads * s.half, s.heads * s.quarter
    far, near = sides(lower, own_tail[: s.tail, :], received[base : base + s.tail, :])
    factor = near[: s.heads, :] * linked(s, far, near)
    join_tail(s, out_send, top, far, near, factor)
    if reverse:
        gain = rest[0][...] + received[base + s.tail :, :]
        every = rest[-1]
        if s.wave:
            every[: -s.gains, :] = rest[1][...]
        every[every.shape[0] - s.gains :, :] = gain
    for h in range(s.heads):
        rows = s.rows(h, s.half)
        far_state, near_state = sides(lower, keep[rows, :], received[rows, :])
        total = near_state + factor[h : h + 1, :] * far_state
        put_parts(left, s.quarter, h, total, out_keep, out_send)


def plane_kernel(s, reverse, keep, sent, received, *rest):
    columns, out = rest[:-1], rest[-1]
    _, chip, _ = place_bits(s.count, reverse)
    left = chip == 0
    top = s.heads * s.quarter
    far, near = sides(left, sent[top:, :], received[top:, :])
    factor = near[: s.heads, :] * linked(s, far, near)
    join_tail(s, out, top, far, near, factor)
    if columns:
        out[top + s.tail :, :] = sum([a[...] for a in columns[1:]], columns[0][...])
    for h in range(s.heads):
        rows = s.rows(h, s.quarter)
        far_state, near_state = sides(left, keep[rows, :], received[rows, :])
        out[rows, :] = near_state + factor[h : h + 1, :] * far_state


def spread_kernel(s, reverse, keep, sent, received, *rest):
    earlier, rest = rest[: s.window], rest[s.window :]
    out_keep, out_send = rest[1:3] if rest[2:] else rest
    _, chip, plane = place_bits(s.count, reverse)
    left = chip == 0
    top = s.heads * s.quarter
    far, near = sides(left, sent[top:, :], received[top:, :])
    tails = [ref[top : top + s.tail, :] for ref in earlier]
    reach = [(plane >= w + 1).astype(F32) for w in range(s.window)]
    entry = linked(s, tails[0], far) * reach[0]
    inner = [
        linked(s, tails[w + 1], tails[w]) * reach[w + 1] * tails[w][: s.heads, :]
        for w in range(s.window - 1)
    ]
    link = linked(s, far, near)
    far_factor = far[: s.heads, :]
    if rest[2:]:
        gain = rest[0][top + s.tail :, :]
        if s.planes > 1:
            gain = gain + earlier[0][top + s.tail :, :]
        rest[3][...] = gain
        out_send[top:, :] = gain
    for h in range(s.heads):
        rows, one = s.rows(h, s.quarter), slice(h, h + 1)
        state = earlier[-1][rows, :]
        for w in reversed(range(s.window - 1)):
            state = earlier[w][rows, :] + inner[w][one] * state
        into_far = entry * state
        far_state = lax.select(left, keep[rows, :], received[rows, :])
        into_near = link * (far_state + far_factor[one] * into_far)
        out_keep[rows, :] = lax.select(left, into_far, into_near)
        out_send[rows, :] = lax.select(left, into_near, into_far)


def entry_kernel(
    s, reverse, chip_keep, chip_received, keep, received, own_tail, out_keep, out_send
):
    core, chip, _ = place_bits(s.count, reverse)
    lower, left = core == 0, chip == 0
    base = s.heads * s.half
    far, near = sides(lower, own_tail[: s.tail, :], received[base : base + s.tail, :])
    link = linked(s, far, near)
    far_factor = far[: s.heads, :]
    for h in range(s.heads):
        rows, quarter = s.rows(h, s.half), s.rows(h, s.quarter)
        into_far = jnp.concatenate(
            sides(left, chip_keep[quarter, :], chip_received[quarter, :]), axis=0
        )
        far_state = lax.select(lower, keep[rows, :], received[rows, :])
        into_near = link * (far_state + far_factor[h : h + 1, :] * into_far)
        out_keep[rows, :] = lax.select(lower, into_far, into_near)
        out_send[rows, :] = lax.select(lower, into_near, into_far)


def joined(s, lower, keep, received, h):
    rows = s.rows(h, s.half)
    return jnp.concatenate(sides(lower, keep[rows, :], received[rows, :]), axis=0)


def decay_mask(column, row):
    at, other = triangle()
    gap = jnp.minimum(column - row, 0.0)
    return jnp.where(at >= other, jnp.exp(gap), 0.0)


def local_kernel(s, queries, keys, values, log_decay, cums, gain, out, weights):
    for j, logs in enumerate(s.logs(log_decay)):
        columns, rows = cums[s.block(j), :], decay_rows(logs)
        for h in range(s.heads):
            mask = decay_mask(columns[:, h : h + 1], rows[h : h + 1, :])
            part = (s.block(j), s.head(h))
            scores = dot(queries[part], keys[part], 1, 1)
            weight = (scores * mask).astype(BF16)
            weights[s.rows(j * s.heads + h, C), :] = weight
            out[s.block(j), s.own(h)] = dot(weight, values[part], 1, 0)


def attention_kernel(
    s, queries, out_grad, gain, cums, notes, local, first_update, keep, received, *rest
):
    earlier_sums, (out, sums) = rest[:-2], rest[-2:]
    core, _, _ = place_bits(s.count, False)
    lower = core == 0
    decays = [jnp.exp(cums[s.block(j), :]) for j in range(s.blocks)]
    squares = [jnp.zeros((C, s.width), F32) for _ in decays]
    inners = [jnp.zeros((C, s.width), F32) for _ in decays]
    for h in range(s.heads):
        state = joined(s, lower, keep, received, h)
        for j in range(s.blocks):
            part, own = (s.block(j), s.head(h)), (s.block(j), s.own(h))
            far = far_dot(queries[part], state, 0)
            attention = local[own] + decays[j][:, h : h + 1] * far
            out[own] = attention
            squares[j] = squares[j] + attention * attention
            inners[j] = inners[j] + out_grad[part].astype(F32) * gain[s.head(h)].reshape(1, s.width) * attention
            if j < s.blocks - 1:
                update = first_update[s.rows(j * s.heads + h, s.width), :]
                state = notes[s.carry(j + 1), :] * (notes[s.factor(j, h), :] * state + update)
    if earlier_sums:
        sums[...] = earlier_sums[0][...]
    else:
        sums[...] = jnp.zeros(sums.shape, F32)
    for j in range(s.blocks):
        for i, part in enumerate([squares[j], inners[j]]):
            row = (slice(i, i + 1), s.block(j))
            sums[row] = sums[row] + jnp.sum(part.T, axis=0, keepdims=True)


def grad_kernel(
    s, all_features, queries, out_grad, gain, cums, notes, attention, *rest
):
    sums, (attn_grad, keep, send, out_tail, out_gain, back_terms) = rest[:-6], rest[-6:]
    core, _, _ = place_bits(s.count, True)
    lower = core == 0
    decays = [jnp.exp(cums[s.block(j), :]) for j in range(s.blocks)]
    totals = sum([a[...] for a in sums[1:]], sums[0][...]) / all_features
    spread = lambda row: jnp.broadcast_to(row, (C, C)).T
    inverses, slopes = [], []
    for j in range(s.blocks):
        inverse = lax.rsqrt(totals[0:1, s.block(j)] + EPSILON)
        inverses.append(spread(inverse))
        slopes.append(spread(totals[1:2, s.block(j)] * inverse * inverse))
    base = s.heads * s.half
    out_tail[...] = jnp.zeros(out_tail.shape, F32)
    own = notes[: s.tail, :]
    put_tail(
        s, out_tail, 0, own[: s.heads], own[s.end : s.end + 1], own[s.start : s.start + 1]
    )
    out_gain[...] = jnp.zeros(out_gain.shape, F32)
    for h in range(s.heads):
        gain_row = gain[s.head(h)].reshape(1, s.width)
        gain_part = jnp.zeros((1, s.width), F32)
        terms = []
        for j in range(s.blocks):
            part, own = (s.block(j), s.head(h)), (s.block(j), s.own(h))
            cot = out_grad[part].astype(F32)
            att = attention[own]
            grad = ((cot * gain_row - att * slopes[j]) * inverses[j]).astype(BF16)
            attn_grad[own] = grad
            gain_part = gain_part + jnp.sum(cot * att * inverses[j], axis=0, keepdims=True)
            weighted = (queries[part].astype(F32) * decays[j][:, h : h + 1]).astype(BF16)
            term = dot(weighted, grad, 0, 0)
            terms.append(term)
            if j > 0:
                back_terms[s.rows((j - 1) * s.heads + h, s.width), :] = term
        state = terms[-1]
        for j in reversed(range(s.blocks - 1)):
            state = terms[j] + (notes[s.carry(j + 1), :] * notes[s.factor(j, h), :]) * state
        put_parts(lower, s.half, h, state, keep, send)
        out_gain[h : h + 1, :] = gain_part
    send[base : base + s.tail, :] = out_tail[...]
    send[base + s.tail :, :] = out_gain[...]


def local_grad_kernel(
    s, queries, values, log_decay, cums, weights, attn_grad, key_out, value_out
):
    for j, logs in enumerate(s.logs(log_decay)):
        columns, rows = cums[s.block(j), :], decay_rows(logs)
        for h in range(s.heads):
            mask = decay_mask(columns[:, h : h + 1], rows[h : h + 1, :])
            part, own = (s.block(j), s.head(h)), (s.block(j), s.own(h))
            grad = attn_grad[own]
            grad_weight = (dot(grad, values[part], 1, 1) * mask).astype(BF16)
            key_out[own] = dot(grad_weight, queries[part], 0, 0)
            value_out[own] = dot(weights[s.rows(j * s.heads + h, C), :], grad, 0, 0)


def final_kernel(s, waves, keys, values, cums, notes, key_local, value_local, back_terms, *rest):
    keep, received = rest[:2]
    last = s is waves[-1]
    near_outs = rest[-2:]
    copies, groups = [], []
    if last:
        *far_outs, far_gain, near_gain, sent = rest[-7:-2]
        groups = s.groups(STORED)
        own, other = rest[2 + 2 * s.wave : 4 + 2 * s.wave]
        base = waves[0].heads * s.quarter
        for wave in waves:
            for h in range(wave.heads):
                row = wave.wave * s.gains + h
                total = own[row : row + 1, :] + other[base + row : base + row + 1, :]
                near_gain[wave.head(h)] = total.reshape(s.width)
        copies.append(pltpu.make_async_copy(near_gain, far_gain, sent.at[2, 0]))
        copies[-1].start()
        for w, wave in enumerate(waves[:-1]):
            place = pl.ds(wave.first * s.width, wave.columns)
            for i, far in enumerate(far_outs):
                near = rest[2 + 2 * w + i]
                copies.append(
                    pltpu.make_async_copy(near, far.at[:, place], sent.at[i, len(groups) + w])
                )
                copies[-1].start()
    core, _, _ = place_bits(s.count, True)
    lower = core == 0
    columns = [cums[s.block(j), :] for j in range(s.blocks)]
    ends = [jnp.exp(a[C - 1 : C, :] - a) for a in columns]
    for h in range(s.heads):
        state = joined(s, lower, keep, received, h)
        for j in reversed(range(s.blocks)):
            part, own = (s.block(j), s.head(h)), (s.block(j), s.own(h))
            end = ends[j][:, h : h + 1]
            key_far = end * far_dot(values[part], state, 1)
            value_far = end * far_dot(keys[part], state, 0)
            near_outs[0][own] = (key_local[own] + key_far).astype(BF16)
            near_outs[1][own] = (value_local[own] + value_far).astype(BF16)
            if j > 0:
                term = back_terms[s.rows((j - 1) * s.heads + h, s.width), :]
                state = notes[s.carry(j), :] * (term + notes[s.factor(j, h), :] * state)
        for g, (_, stop, part, far_part) in enumerate(groups):
            if h + 1 != stop:
                continue
            for i, (near, far) in enumerate(zip(near_outs, far_outs)):
                copies.append(
                    pltpu.make_async_copy(near.at[:, part], far.at[:, far_part], sent.at[i, g])
                )
                copies[-1].start()
    for copy in copies:
        copy.wait()


def swap(value, axis, bit):
    count = lax.axis_size(axis)
    return lax.ppermute(value, axis, [(i, i ^ bit) for i in range(count)])


def next_plane(value, count, reverse):
    step = -PLANE if reverse else PLANE
    return lax.ppermute(value, "seq", [(i, (i + step) % count) for i in range(count)])


def pass_on(value, count, reverse, behind):
    planes = count // PLANE
    pairs = []
    for source in range(count):
        plane, place = divmod(source, PLANE)
        if plane < behind:
            target = source ^ 2
        else:
            target = (plane + 1 if plane < planes - 1 else behind) * PLANE + place
        pair = (source, target)
        pairs.append(tuple(count - 1 - a for a in pair) if reverse else pair)
    return lax.ppermute(value, "seq", pairs)


def scan_in(waves, parts, reverse, token, beside):
    bind = functools.partial
    gain_rows = lambda s: len(waves) * s.gains if reverse and s.wave == 0 else 0
    received, chips, chip_received, local, gains, others = [], [], [], [], [], []
    for s, (keep, send, tail, gain) in zip(waves, parts):
        received.append(swap(send, "seq", 1))
    for i, (s, (keep, send, tail, gain)) in enumerate(zip(waves, parts)):
        outs = [
            shape(s.heads * s.quarter, s.width),
            shape(s.heads * s.quarter + s.tail, s.width),
        ]
        (keep,) = after(token, keep)
        extra = []
        if reverse:
            extra = [gain, *gains]
            outs.append(shape((i + 1) * s.gains, s.width))
        *chip, = call(bind(chip_kernel, s, reverse), outs, keep, received[i], tail, *extra)
        gains = chip[2:]
        token = chip[0]
        chips.append(chip)
        chip_received.append(swap(chip[1], "seq", 2))
    if reverse:
        bit = waves[0].count // 2
        while bit > PLANE:
            if others:
                gains, others = [gains[0] + others[0]], []
            others = [swap(gains[0], "seq", bit + 1)]
            bit //= 2
    planes, passed = [], []
    for i in range(len(waves) - 1):
        token, one = beside(token, i)
        local.append(one)
    for i, s in enumerate(waves):
        (keep,) = after(token, chips[i][0])
        outs = [shape(s.heads * s.quarter + s.tail + gain_rows(s), s.width)]
        columns = gains + others if gain_rows(s) else []
        (plane,) = call(
            bind(plane_kernel, s, reverse),
            outs,
            keep,
            chips[i][1],
            chip_received[i],
            *columns,
            deps=planes[-1:],
        )
        token = plane
        planes.append(plane)
        passed.append([next_plane(plane, s.count, reverse)])
    for i in range(len(local), len(waves)):
        token, one = beside(token, i)
        local.append(one)
    passed = [list(after(token, one[0])) for one in passed]
    for w in range(1, waves[0].window):
        for i, s in enumerate(waves):
            passed[i].append(pass_on(passed[i][-1], s.count, reverse, w))
    spreads, spread_received = [], []
    for i, s in enumerate(waves):
        (keep,) = after(token, chips[i][0])
        outs = [
            shape(s.heads * s.quarter, s.width),
            shape(s.heads * s.quarter + gain_rows(s), s.width),
        ]
        extra = []
        if gain_rows(s):
            outs.append(shape(gain_rows(s), s.width))
            extra = [planes[i]]
        spread = call(
            bind(spread_kernel, s, reverse),
            outs,
            keep,
            chips[i][1],
            chip_received[i],
            *passed[i],
            *extra,
        )
        token = spread[0]
        spreads.append(spread)
        spread_received.append(swap(spread[1], "seq", 2))
    entries = []
    for i, s in enumerate(waves):
        (keep,) = after(token, spreads[i][0])
        entry = call(
            bind(entry_kernel, s, reverse),
            [shape(s.heads * s.half, s.width)] * 2,
            keep,
            spread_received[i],
            parts[i][0],
            received[i],
            parts[i][2],
        )
        token = entry[0]
        entries.append((entry[0], swap(entry[1], "seq", 1)))
    return entries, local, token, [spreads[0][-1], spread_received[0]]


def per_device(queries, keys, values, out_grad, log_decay, norm_gain, doc_ids):
    tokens, features = queries.shape
    heads = log_decay.shape[1]
    count, dp = lax.axis_size("seq"), lax.axis_size("dp")
    second = round(heads * SECOND_WAVE) if heads > 4 else 0
    split = [(0, heads - second), (heads - second, second)][: 2 if second else 1]
    waves = [Sizes(tokens, features, heads, count, w, *part) for w, part in enumerate(split)]
    bind = functools.partial
    unit = 2 * C * C * C * waves[0].blocks * waves[0].heads
    gain = norm_gain
    log_decay = log_decay.T
    states = []
    far = [pltpu.with_memory_space_constraint(a, pltpu.HBM) for a in (keys, values, log_decay, doc_ids)]
    for s in waves:
        given = (keys, values, log_decay, doc_ids)
        spaces = [pltpu.VMEM] * 4
        scratch = []
        if not states:
            given, spaces = far, [pltpu.HBM] * 4
            scratch = [
                pltpu.VMEM((tokens, s.columns), BF16),
                pltpu.VMEM((tokens, s.columns), BF16),
                pltpu.VMEM(log_decay.shape, F32),
                pltpu.SMEM(doc_ids.shape, jnp.int32),
                pltpu.SemaphoreType.DMA((2, len(s.groups(LOADED)))),
                pltpu.SemaphoreType.DMA((2,)),
            ]
        else:
            given = (keys, values, log_decay, states[0][2])
        state = call(
            bind(state_kernel, s, waves[0]),
            [
                shape(s.heads * s.half, s.width),
                shape(s.heads * s.half + s.tail, s.width),
                shape(s.notes, s.width),
                shape(tokens, s.heads),
                shape(max(1, s.blocks - 1) * s.heads * s.width, s.width),
            ],
            *given,
            flops=unit,
            spaces=spaces,
            scratch=scratch,
        )
        token = state[0]
        states.append(state)
    queries, keys, values, out_grad, gain, log_decay = after(
        token, queries, keys, values, out_grad, gain, log_decay
    )

    def beside_forward(token, i):
        s = waves[i]
        (held,) = after(token, log_decay)
        local = call(
            bind(local_kernel, s),
            [shape(tokens, s.columns), shape(s.blocks * s.heads * C, C, BF16)],
            queries,
            keys,
            values,
            held,
            states[i][3],
            gain,
            flops=2 * unit,
        )
        return local[0], local

    parts = [(state[0], state[1], state[2], None) for state in states]
    entries, local, token, _ = scan_in(waves, parts, False, token, beside_forward)
    attentions, sums = [], []
    for i, s in enumerate(waves):
        attention, total = call(
            bind(attention_kernel, s),
            [shape(tokens, s.columns), shape(8, tokens)],
            queries,
            out_grad,
            gain,
            states[i][3],
            states[i][2],
            local[i][0],
            states[i][4],
            *entries[i],
            *sums,
            flops=2 * unit,
        )
        token = attention
        attentions.append(attention)
        sums = [total]
    if dp & (dp - 1):
        sums = [lax.psum(sums[0], "dp")]
    else:
        bit = 1
        while bit < dp:
            total = sum(sums[1:], sums[0])
            sums = [total, swap(total, "dp", bit)]
            bit *= 2
    grads = []
    for i, s in enumerate(waves):
        grad = call(
            bind(grad_kernel, s, features * dp),
            [
                shape(tokens, s.columns, BF16),
                shape(s.heads * s.half, s.width),
                shape(s.heads * s.half + s.tail + s.gains, s.width),
                shape(s.tail, s.width),
                shape(s.gains, s.width),
                shape(max(1, s.blocks - 1) * s.heads * s.width, s.width),
            ],
            queries,
            out_grad,
            gain,
            states[i][3],
            states[i][2],
            attentions[i],
            *sums,
            flops=unit,
            deps=[token] if grads else [],
        )
        token = grad[0]
        grads.append(grad)

    def beside_backward(token, i):
        s = waves[i]
        (held,) = after(token, log_decay)
        local_grad = call(
            bind(local_grad_kernel, s),
            [shape(tokens, s.columns), shape(tokens, s.columns)],
            queries,
            values,
            held,
            states[i][3],
            local[i][1],
            grads[i][0],
            flops=3 * unit,
        )
        return local_grad[0], local_grad

    parts = [(grad[1], grad[2], grad[3], grad[4]) for grad in grads]
    entries, local_grads, token, gains = scan_in(waves, parts, True, token, beside_backward)
    done = []
    for i, s in enumerate(waves):
        last = s is waves[-1]
        (held,) = after(token, log_decay)
        given = [
            keys, values, states[i][3], states[i][2], *local_grads[i], grads[i][5], *entries[i], *done,
        ]
        scratch = []
        if last:
            given += gains
            outs = [pltpu.HBM((tokens, features), BF16)] * 2 + [pltpu.HBM((features,), F32)]
            out_spaces = [pltpu.HBM] * 3
            scratch = [
                pltpu.VMEM((features,), F32),
                pltpu.SemaphoreType.DMA((3, len(s.groups(STORED)) + i)),
                pltpu.VMEM((tokens, s.columns), BF16),
                pltpu.VMEM((tokens, s.columns), BF16),
            ]
        else:
            outs = [shape(tokens, s.columns, BF16)] * 2
            out_spaces = [pltpu.VMEM] * 2
        made = call(
            bind(final_kernel, s, waves),
            outs,
            *given,
            flops=4 * unit,
            out_spaces=out_spaces,
            scratch=scratch,
        )
        token = made[0]
        done += made
    return tuple(done[-3:])


def solution(mesh):
    placed = (
        P("seq", "dp"),
        P("seq", "dp"),
        P("seq", "dp"),
        P("seq", "dp"),
        P("seq", "dp"),
        P("dp"),
        P("seq"),
    )
    return jax.shard_map(
        per_device,
        mesh=mesh,
        in_specs=placed,
        out_specs=(P("seq", "dp"), P("seq", "dp"), P("dp")),
        check_vma=False,
    )
```

```python
import functools
import math

import jax
import jax.numpy as jnp
from jax import lax
from jax.experimental import pallas as pl
from jax.experimental.pallas import tpu as pltpu
from jax.sharding import PartitionSpec as P

C = 128
EPSILON = 1e-06
PLANE = 4
SECOND_WAVE = 0.5
LOADED, STORED = 6, 3
F32 = jnp.float32
BF16 = jnp.bfloat16


def dot(a, b, contract_a, contract_b):
    return lax.dot_general(
        a,
        b,
        (((contract_a,), (contract_b,)), ((), ())),
        preferred_element_type=F32,
    )


def two_parts(a):
    high = a.astype(BF16)
    return high, (a - high.astype(F32)).astype(BF16)


def far_dot(a, state, contract_state):
    parts = jnp.concatenate(two_parts(state), axis=contract_state)
    return dot(jnp.concatenate([a, a], axis=1), parts, 1, contract_state)


def equal(a, b):
    return (a == b).astype(F32)


def place_bits(count, reverse):
    place = lax.axis_index("seq")
    place = count - 1 - place if reverse else place
    return lax.rem(place, 2), lax.rem(place // 2, 2), place // PLANE


def triangle():
    row = lax.broadcasted_iota(jnp.int32, (C, C), 0)
    column = lax.broadcasted_iota(jnp.int32, (C, C), 1)
    return row, column


def sums_of(log_block, chosen, contract, log_first):
    parts, left = [], log_block
    for _ in range(3):
        parts.append(left.astype(BF16))
        left = left - parts[-1].astype(F32)
    chosen = chosen.astype(BF16)
    total = None
    for some in (parts[2:], parts[:2]):
        logs = jnp.concatenate(some, axis=1)
        which = jnp.concatenate([chosen] * len(some), axis=contract)
        if log_first:
            one = dot(logs, which, 1, contract)
        else:
            one = dot(which, logs, contract, 1)
        total = one if total is None else total + one
    return total


def decay_columns(log_block):
    row, column = triangle()
    return sums_of(log_block, (row >= column).astype(F32), 1, False)


def decay_rows(log_block):
    row, column = triangle()
    return sums_of(log_block, (row <= column).astype(F32), 0, True)


def total_rows(log_block):
    return sums_of(log_block, jnp.ones((C, C), F32), 0, True)


class Sizes:
    def __init__(self, tokens, features, all_heads, count, wave, first, heads):
        self.tokens, self.features, self.count = tokens, features, count
        self.heads, self.first, self.wave = heads, first, wave
        self.blocks = tokens // C
        self.width = features // all_heads
        self.half = self.width // 2
        self.quarter = self.width // 4
        self.columns = self.heads * self.width
        self.planes = count // PLANE
        longest = self.blocks * count // 2
        per_plane = self.blocks * PLANE
        self.window = max(1, min(self.planes - 1, 1 + (longest - 2) // per_plane))
        self.gains = -(-self.heads // 8) * 8
        self.tail = -(-(self.heads + 2) // 8) * 8
        self.start, self.end = self.heads, self.heads + 1
        self.factors = self.heads + 2 + self.blocks
        self.notes = -(-(self.factors + self.blocks * self.heads) // 8) * 8

    def own(self, h):
        return slice(h * self.width, (h + 1) * self.width)

    def head(self, h):
        return self.own(self.first + h)

    def block(self, j):
        return slice(j * C, (j + 1) * C)

    def rows(self, h, size):
        return slice(h * size, (h + 1) * size)

    def groups(self, most):
        edges = [*range(0, self.heads, most), self.heads]
        return [(a, b, pl.ds(a * self.width, (b - a) * self.width),
                 pl.ds((self.first + a) * self.width, (b - a) * self.width))
                for a, b in zip(edges[:-1], edges[1:])]

    def carry(self, j):
        return slice(self.heads + 2 + j, self.heads + 3 + j)

    def factor(self, j, h):
        row = self.factors + j * self.heads + h
        return slice(row, row + 1)

    def logs(self, log_decay):
        return [
            log_decay[self.first : self.first + self.heads, self.block(j)]
            for j in range(self.blocks)
        ]


def call(kernel, outs, *args, flops=0, spaces=None, out_spaces=None, scratch=(), deps=()):
    moved = sum(math.prod(a.shape) * a.dtype.itemsize for a in (*args, *outs))
    spaces = spaces or [pltpu.VMEM] * len(args)
    out_spaces = out_spaces or [pltpu.VMEM] * len(outs)
    given = len(args)
    return pl.pallas_call(
        lambda *refs: kernel(*refs[:given], *refs[given + len(deps) :]),
        out_shape=outs,
        in_specs=[pl.BlockSpec(memory_space=p) for p in spaces + [pl.ANY] * len(deps)],
        out_specs=[pl.BlockSpec(memory_space=p) for p in out_spaces],
        compiler_params=pltpu.CompilerParams(vmem_limit_bytes=moved + (4 << 20)),
        cost_estimate=pl.CostEstimate(flops=flops, bytes_accessed=moved, transcendentals=0),
        scratch_shapes=scratch,
    )(*args, *deps)


def after(token, *values):
    return lax.optimization_barrier((token,) + values)[1:]


def shape(rows, columns, dtype=F32):
    return jax.ShapeDtypeStruct((rows, columns), dtype)


def put_tail(s, tail_ref, base, factors, start, end):
    tail_ref[base : base + s.heads, :] = factors
    tail_ref[base + s.start : base + s.start + 1, :] = start
    tail_ref[base + s.end : base + s.end + 1, :] = end


def put_parts(first, size, h, whole, keep_ref, send_ref):
    low, high = whole[:size], whole[size:]
    rows = slice(h * size, (h + 1) * size)
    keep_ref[rows, :] = lax.select(first, low, high)
    send_ref[rows, :] = lax.select(first, high, low)


def state_kernel(
    s, told, keys, values, log_decay, doc_ids, keep, send, notes, cums, first_update, *near
):
    waits, first = {}, s.first
    if near:
        near_keys, near_values, near_logs, near_ids, arrived, small = near
        ids_copy = pltpu.make_async_copy(doc_ids, near_ids, small.at[0])
        logs_copy = pltpu.make_async_copy(log_decay, near_logs, small.at[1])
        for g, (a, _, part, far_part) in enumerate(s.groups(LOADED)):
            waits[a] = [
                pltpu.make_async_copy(far.at[:, far_part], close.at[:, part], arrived.at[i, g])
                for i, (far, close) in enumerate([(keys, near_keys), (values, near_values)])
            ]
        for copy in [logs_copy, ids_copy] + sum(waits.values(), []):
            copy.start()
        logs_copy.wait()
        keys, values, log_decay, doc_ids, first = near_keys, near_values, near_logs, near_ids, 0
    core, _, _ = place_bits(s.count, False)
    lower = core == 0
    logs = s.logs(log_decay)
    totals = [total_rows(a) for a in logs]
    factors = [jnp.exp(t) for t in totals]
    columns = [decay_columns(a) for a in logs]
    ends = [jnp.exp(a[C - 1 : C, :] - a) for a in columns]
    for j, column in enumerate(columns):
        cums[s.block(j), :] = column
    if near:
        ids_copy.wait()
        docs = [jnp.full((1, s.width), doc_ids[j].astype(F32)) for j in range(s.blocks)]
        carries = [None] + [equal(docs[j - 1], docs[j]) for j in range(1, s.blocks)]
    else:
        docs = [doc_ids[told.start : told.start + 1, :], doc_ids[told.end : told.end + 1, :]]
        carries = [doc_ids[told.carry(j), :] for j in range(s.blocks)]
    whole_factor = factors[0]
    for j in range(1, s.blocks):
        whole_factor = whole_factor * factors[j] * carries[j]
    base = s.heads * s.half
    send[base:, :] = jnp.zeros((s.tail, s.width), F32)
    put_tail(s, send, base, whole_factor, docs[0], docs[-1])
    notes[...] = jnp.zeros(notes.shape, F32)
    put_tail(s, notes, 0, whole_factor, docs[0], docs[-1])
    for j in range(1, s.blocks):
        notes[s.carry(j), :] = carries[j]
    for j, rows in enumerate(factors):
        notes[s.factor(j, 0).start : s.factor(j, 0).start + s.heads, :] = rows
    for h in range(s.heads):
        for copy in waits.get(h, ()):
            copy.wait()
        place = slice((first + h) * s.width, (first + h + 1) * s.width)
        state = None
        for j in range(s.blocks):
            scaled = keys[s.block(j), place].astype(F32) * ends[j][:, h : h + 1]
            update = dot(scaled.astype(BF16), values[s.block(j), place], 0, 0)
            if j < s.blocks - 1:
                first_update[s.rows(j * s.heads + h, s.width), :] = update
            if state is None:
                state = update
            else:
                state = (carries[j] * factors[j][h : h + 1, :]) * state + update
        put_parts(lower, s.half, h, state, keep, send)


def sides(first, own, other):
    return lax.select(first, own, other), lax.select(first, other, own)


def linked(s, far, near):
    return equal(far[s.end : s.end + 1, :], near[s.start : s.start + 1, :])


def join_tail(s, out, base, far, near, factor):
    out[base : base + s.tail, :] = jnp.zeros((s.tail, s.width), F32)
    put_tail(
        s,
        out,
        base,
        far[: s.heads, :] * factor,
        far[s.start : s.start + 1, :],
        near[s.end : s.end + 1, :],
    )


def chip_kernel(s, reverse, keep, received, own_tail, *rest):
    out_keep, out_send = rest[-3:-1] if reverse else rest
    core, chip, _ = place_bits(s.count, reverse)
    lower, left = core == 0, chip == 0
    base, top = s.heads * s.half, s.heads * s.quarter
    far, near = sides(lower, own_tail[: s.tail, :], received[base : base + s.tail, :])
    factor = near[: s.heads, :] * linked(s, far, near)
    join_tail(s, out_send, top, far, near, factor)
    if reverse:
        gain = rest[0][...] + received[base + s.tail :, :]
        every = rest[-1]
        if s.wave:
            every[: -s.gains, :] = rest[1][...]
        every[every.shape[0] - s.gains :, :] = gain
    for h in range(s.heads):
        rows = s.rows(h, s.half)
        far_state, near_state = sides(lower, keep[rows, :], received[rows, :])
        total = near_state + factor[h : h + 1, :] * far_state
        put_parts(left, s.quarter, h, total, out_keep, out_send)


def plane_kernel(s, reverse, keep, sent, received, *rest):
    columns, out = rest[:-1], rest[-1]
    _, chip, _ = place_bits(s.count, reverse)
    left = chip == 0
    top = s.heads * s.quarter
    far, near = sides(left, sent[top:, :], received[top:, :])
    factor = near[: s.heads, :] * linked(s, far, near)
    join_tail(s, out, top, far, near, factor)
    if columns:
        out[top + s.tail :, :] = sum([a[...] for a in columns[1:]], columns[0][...])
    for h in range(s.heads):
        rows = s.rows(h, s.quarter)
        far_state, near_state = sides(left, keep[rows, :], received[rows, :])
        out[rows, :] = near_state + factor[h : h + 1, :] * far_state


def spread_kernel(s, reverse, keep, sent, received, *rest):
    earlier, rest = rest[: s.window], rest[s.window :]
    out_keep, out_send = rest[1:3] if rest[2:] else rest
    _, chip, plane = place_bits(s.count, reverse)
    left = chip == 0
    top = s.heads * s.quarter
    far, near = sides(left, sent[top:, :], received[top:, :])
    tails = [ref[top : top + s.tail, :] for ref in earlier]
    reach = [(plane >= w + 1).astype(F32) for w in range(s.window)]
    entry = linked(s, tails[0], far) * reach[0]
    inner = [
        linked(s, tails[w + 1], tails[w]) * reach[w + 1] * tails[w][: s.heads, :]
        for w in range(s.window - 1)
    ]
    link = linked(s, far, near)
    far_factor = far[: s.heads, :]
    if rest[2:]:
        gain = rest[0][top + s.tail :, :]
        if s.planes > 1:
            gain = gain + earlier[0][top + s.tail :, :]
        rest[3][...] = gain
        out_send[top:, :] = gain
    for h in range(s.heads):
        rows, one = s.rows(h, s.quarter), slice(h, h + 1)
        state = earlier[-1][rows, :]
        for w in reversed(range(s.window - 1)):
            state = earlier[w][rows, :] + inner[w][one] * state
        into_far = entry * state
        far_state = lax.select(left, keep[rows, :], received[rows, :])
        into_near = link * (far_state + far_factor[one] * into_far)
        out_keep[rows, :] = lax.select(left, into_far, into_near)
        out_send[rows, :] = lax.select(left, into_near, into_far)


def entry_kernel(
    s, reverse, chip_keep, chip_received, keep, received, own_tail, out_keep, out_send
):
    core, chip, _ = place_bits(s.count, reverse)
    lower, left = core == 0, chip == 0
    base = s.heads * s.half
    far, near = sides(lower, own_tail[: s.tail, :], received[base : base + s.tail, :])
    link = linked(s, far, near)
    far_factor = far[: s.heads, :]
    for h in range(s.heads):
        rows, quarter = s.rows(h, s.half), s.rows(h, s.quarter)
        into_far = jnp.concatenate(
            sides(left, chip_keep[quarter, :], chip_received[quarter, :]), axis=0
        )
        far_state = lax.select(lower, keep[rows, :], received[rows, :])
        into_near = link * (far_state + far_factor[h : h + 1, :] * into_far)
        out_keep[rows, :] = lax.select(lower, into_far, into_near)
        out_send[rows, :] = lax.select(lower, into_near, into_far)


def joined(s, lower, keep, received, h):
    rows = s.rows(h, s.half)
    return jnp.concatenate(sides(lower, keep[rows, :], received[rows, :]), axis=0)


def decay_mask(column, row):
    at, other = triangle()
    gap = jnp.minimum(column - row, 0.0)
    return jnp.where(at >= other, jnp.exp(gap), 0.0)


def local_kernel(s, queries, keys, values, log_decay, cums, gain, out, weights):
    for j, logs in enumerate(s.logs(log_decay)):
        columns, rows = cums[s.block(j), :], decay_rows(logs)
        for h in range(s.heads):
            mask = decay_mask(columns[:, h : h + 1], rows[h : h + 1, :])
            part = (s.block(j), s.head(h))
            scores = dot(queries[part], keys[part], 1, 1)
            weight = (scores * mask).astype(BF16)
            weights[s.rows(j * s.heads + h, C), :] = weight
            out[s.block(j), s.own(h)] = dot(weight, values[part], 1, 0)


def attention_kernel(
    s, queries, out_grad, gain, cums, notes, local, first_update, keep, received, *rest
):
    earlier_sums, (out, sums) = rest[:-2], rest[-2:]
    core, _, _ = place_bits(s.count, False)
    lower = core == 0
    decays = [jnp.exp(cums[s.block(j), :]) for j in range(s.blocks)]
    squares = [jnp.zeros((C, s.width), F32) for _ in decays]
    inners = [jnp.zeros((C, s.width), F32) for _ in decays]
    for h in range(s.heads):
        state = joined(s, lower, keep, received, h)
        for j in range(s.blocks):
            part, own = (s.block(j), s.head(h)), (s.block(j), s.own(h))
            far = far_dot(queries[part], state, 0)
            attention = local[own] + decays[j][:, h : h + 1] * far
            out[own] = attention
            squares[j] = squares[j] + attention * attention
            inners[j] = inners[j] + out_grad[part].astype(F32) * gain[s.head(h)].reshape(1, s.width) * attention
            if j < s.blocks - 1:
                update = first_update[s.rows(j * s.heads + h, s.width), :]
                state = notes[s.carry(j + 1), :] * (notes[s.factor(j, h), :] * state + update)
    if earlier_sums:
        sums[...] = earlier_sums[0][...]
    else:
        sums[...] = jnp.zeros(sums.shape, F32)
    for j in range(s.blocks):
        for i, part in enumerate([squares[j], inners[j]]):
            row = (slice(i, i + 1), s.block(j))
            sums[row] = sums[row] + jnp.sum(part.T, axis=0, keepdims=True)


def grad_kernel(
    s, all_features, queries, out_grad, gain, cums, notes, attention, *rest
):
    sums, (attn_grad, keep, send, out_tail, out_gain, back_terms) = rest[:-6], rest[-6:]
    core, _, _ = place_bits(s.count, True)
    lower = core == 0
    decays = [jnp.exp(cums[s.block(j), :]) for j in range(s.blocks)]
    totals = sum([a[...] for a in sums[1:]], sums[0][...]) / all_features
    spread = lambda row: jnp.broadcast_to(row, (C, C)).T
    inverses, slopes = [], []
    for j in range(s.blocks):
        inverse = lax.rsqrt(totals[0:1, s.block(j)] + EPSILON)
        inverses.append(spread(inverse))
        slopes.append(spread(totals[1:2, s.block(j)] * inverse * inverse))
    base = s.heads * s.half
    out_tail[...] = jnp.zeros(out_tail.shape, F32)
    own = notes[: s.tail, :]
    put_tail(
        s, out_tail, 0, own[: s.heads], own[s.end : s.end + 1], own[s.start : s.start + 1]
    )
    out_gain[...] = jnp.zeros(out_gain.shape, F32)
    for h in range(s.heads):
        gain_row = gain[s.head(h)].reshape(1, s.width)
        gain_part = jnp.zeros((1, s.width), F32)
        terms = []
        for j in range(s.blocks):
            part, own = (s.block(j), s.head(h)), (s.block(j), s.own(h))
            cot = out_grad[part].astype(F32)
            att = attention[own]
            grad = ((cot * gain_row - att * slopes[j]) * inverses[j]).astype(BF16)
            attn_grad[own] = grad
            gain_part = gain_part + jnp.sum(cot * att * inverses[j], axis=0, keepdims=True)
            weighted = (queries[part].astype(F32) * decays[j][:, h : h + 1]).astype(BF16)
            term = dot(weighted, grad, 0, 0)
            terms.append(term)
            if j > 0:
                back_terms[s.rows((j - 1) * s.heads + h, s.width), :] = term
        state = terms[-1]
        for j in reversed(range(s.blocks - 1)):
            state = terms[j] + (notes[s.carry(j + 1), :] * notes[s.factor(j, h), :]) * state
        put_parts(lower, s.half, h, state, keep, send)
        out_gain[h : h + 1, :] = gain_part
    send[base : base + s.tail, :] = out_tail[...]
    send[base + s.tail :, :] = out_gain[...]


def local_grad_kernel(
    s, queries, values, log_decay, cums, weights, attn_grad, key_out, value_out
):
    for j, logs in enumerate(s.logs(log_decay)):
        columns, rows = cums[s.block(j), :], decay_rows(logs)
        for h in range(s.heads):
            mask = decay_mask(columns[:, h : h + 1], rows[h : h + 1, :])
            part, own = (s.block(j), s.head(h)), (s.block(j), s.own(h))
            grad = attn_grad[own]
            grad_weight = (dot(grad, values[part], 1, 1) * mask).astype(BF16)
            key_out[own] = dot(grad_weight, queries[part], 0, 0)
            value_out[own] = dot(weights[s.rows(j * s.heads + h, C), :], grad, 0, 0)


def final_kernel(s, waves, keys, values, cums, notes, key_local, value_local, back_terms, *rest):
    keep, received = rest[:2]
    last = s is waves[-1]
    near_outs = rest[-2:]
    copies, groups = [], []
    if last:
        *far_outs, far_gain, near_gain, sent = rest[-7:-2]
        groups = s.groups(STORED)
        own, other = rest[2 + 2 * s.wave : 4 + 2 * s.wave]
        base = waves[0].heads * s.quarter
        for wave in waves:
            for h in range(wave.heads):
                row = wave.wave * s.gains + h
                total = own[row : row + 1, :] + other[base + row : base + row + 1, :]
                near_gain[wave.head(h)] = total.reshape(s.width)
        copies.append(pltpu.make_async_copy(near_gain, far_gain, sent.at[2, 0]))
        copies[-1].start()
        for w, wave in enumerate(waves[:-1]):
            place = pl.ds(wave.first * s.width, wave.columns)
            for i, far in enumerate(far_outs):
                near = rest[2 + 2 * w + i]
                copies.append(
                    pltpu.make_async_copy(near, far.at[:, place], sent.at[i, len(groups) + w])
                )
                copies[-1].start()
    core, _, _ = place_bits(s.count, True)
    lower = core == 0
    columns = [cums[s.block(j), :] for j in range(s.blocks)]
    ends = [jnp.exp(a[C - 1 : C, :] - a) for a in columns]
    for h in range(s.heads):
        state = joined(s, lower, keep, received, h)
        for j in reversed(range(s.blocks)):
            part, own = (s.block(j), s.head(h)), (s.block(j), s.own(h))
            end = ends[j][:, h : h + 1]
            key_far = end * far_dot(values[part], state, 1)
            value_far = end * far_dot(keys[part], state, 0)
            near_outs[0][own] = (key_local[own] + key_far).astype(BF16)
            near_outs[1][own] = (value_local[own] + value_far).astype(BF16)
            if j > 0:
                term = back_terms[s.rows((j - 1) * s.heads + h, s.width), :]
                state = notes[s.carry(j), :] * (term + notes[s.factor(j, h), :] * state)
        for g, (_, stop, part, far_part) in enumerate(groups):
            if h + 1 != stop:
                continue
            for i, (near, far) in enumerate(zip(near_outs, far_outs)):
                copies.append(
                    pltpu.make_async_copy(near.at[:, part], far.at[:, far_part], sent.at[i, g])
                )
                copies[-1].start()
    for copy in copies:
        copy.wait()


def swap(value, axis, bit):
    count = lax.axis_size(axis)
    return lax.ppermute(value, axis, [(i, i ^ bit) for i in range(count)])


def next_plane(value, count, reverse):
    step = -PLANE if reverse else PLANE
    return lax.ppermute(value, "seq", [(i, (i + step) % count) for i in range(count)])


def pass_on(value, count, reverse, behind):
    planes = count // PLANE
    pairs = []
    for source in range(count):
        plane, place = divmod(source, PLANE)
        if plane < behind:
            target = source ^ 1
        else:
            target = (plane + 1 if plane < planes - 1 else behind) * PLANE + place
        pair = (source, target)
        pairs.append(tuple(count - 1 - a for a in pair) if reverse else pair)
    return lax.ppermute(value, "seq", pairs)


def scan_in(waves, parts, reverse, token, beside):
    bind = functools.partial
    gain_rows = lambda s: len(waves) * s.gains if reverse and s.wave == 0 else 0
    received, chips, chip_received, local, gains, others = [], [], [], [], [], []
    for s, (keep, send, tail, gain) in zip(waves, parts):
        received.append(swap(send, "seq", 1))
    for i, (s, (keep, send, tail, gain)) in enumerate(zip(waves, parts)):
        outs = [
            shape(s.heads * s.quarter, s.width),
            shape(s.heads * s.quarter + s.tail, s.width),
        ]
        (keep,) = after(token, keep)
        extra = []
        if reverse:
            extra = [gain, *gains]
            outs.append(shape((i + 1) * s.gains, s.width))
        *chip, = call(bind(chip_kernel, s, reverse), outs, keep, received[i], tail, *extra)
        gains = chip[2:]
        token = chip[0]
        chips.append(chip)
        chip_received.append(swap(chip[1], "seq", 2))
    if reverse:
        bit = waves[0].count // 2
        while bit > PLANE:
            if others:
                gains, others = [gains[0] + others[0]], []
            others = [swap(gains[0], "seq", bit + 1)]
            bit //= 2
    planes, passed = [], []
    for i in range(len(waves) - 1):
        token, one = beside(token, i)
        local.append(one)
    for i, s in enumerate(waves):
        (keep,) = after(token, chips[i][0])
        outs = [shape(s.heads * s.quarter + s.tail + gain_rows(s), s.width)]
        columns = gains + others if gain_rows(s) else []
        (plane,) = call(
            bind(plane_kernel, s, reverse),
            outs,
            keep,
            chips[i][1],
            chip_received[i],
            *columns,
            deps=planes[-1:],
        )
        token = plane
        planes.append(plane)
        passed.append([next_plane(plane, s.count, reverse)])
    for i in range(len(local), len(waves)):
        token, one = beside(token, i)
        local.append(one)
    passed = [list(after(token, one[0])) for one in passed]
    for w in range(1, waves[0].window):
        for i, s in enumerate(waves):
            passed[i].append(pass_on(passed[i][-1], s.count, reverse, w))
    spreads, spread_received = [], []
    for i, s in enumerate(waves):
        (keep,) = after(token, chips[i][0])
        outs = [
            shape(s.heads * s.quarter, s.width),
            shape(s.heads * s.quarter + gain_rows(s), s.width),
        ]
        extra = []
        if gain_rows(s):
            outs.append(shape(gain_rows(s), s.width))
            extra = [planes[i]]
        spread = call(
            bind(spread_kernel, s, reverse),
            outs,
            keep,
            chips[i][1],
            chip_received[i],
            *passed[i],
            *extra,
        )
        token = spread[0]
        spreads.append(spread)
        spread_received.append(swap(spread[1], "seq", 2))
    entries = []
    for i, s in enumerate(waves):
        (keep,) = after(token, spreads[i][0])
        entry = call(
            bind(entry_kernel, s, reverse),
            [shape(s.heads * s.half, s.width)] * 2,
            keep,
            spread_received[i],
            parts[i][0],
            received[i],
            parts[i][2],
        )
        token = entry[0]
        entries.append((entry[0], swap(entry[1], "seq", 1)))
    return entries, local, token, [spreads[0][-1], spread_received[0]]


def per_device(queries, keys, values, out_grad, log_decay, norm_gain, doc_ids):
    tokens, features = queries.shape
    heads = log_decay.shape[1]
    count, dp = lax.axis_size("seq"), lax.axis_size("dp")
    second = round(heads * SECOND_WAVE) if heads > 4 else 0
    split = [(0, heads - second), (heads - second, second)][: 2 if second else 1]
    waves = [Sizes(tokens, features, heads, count, w, *part) for w, part in enumerate(split)]
    bind = functools.partial
    unit = 2 * C * C * C * waves[0].blocks * waves[0].heads
    gain = norm_gain
    log_decay = log_decay.T
    states = []
    far = [pltpu.with_memory_space_constraint(a, pltpu.HBM) for a in (keys, values, log_decay, doc_ids)]
    for s in waves:
        given = (keys, values, log_decay, doc_ids)
        spaces = [pltpu.VMEM] * 4
        scratch = []
        if not states:
            given, spaces = far, [pltpu.HBM] * 4
            scratch = [
                pltpu.VMEM((tokens, s.columns), BF16),
                pltpu.VMEM((tokens, s.columns), BF16),
                pltpu.VMEM(log_decay.shape, F32),
                pltpu.SMEM(doc_ids.shape, jnp.int32),
                pltpu.SemaphoreType.DMA((2, len(s.groups(LOADED)))),
                pltpu.SemaphoreType.DMA((2,)),
            ]
        else:
            given = (keys, values, log_decay, states[0][2])
        state = call(
            bind(state_kernel, s, waves[0]),
            [
                shape(s.heads * s.half, s.width),
                shape(s.heads * s.half + s.tail, s.width),
                shape(s.notes, s.width),
                shape(tokens, s.heads),
                shape(max(1, s.blocks - 1) * s.heads * s.width, s.width),
            ],
            *given,
            flops=unit,
            spaces=spaces,
            scratch=scratch,
        )
        token = state[0]
        states.append(state)
    queries, keys, values, out_grad, gain, log_decay = after(
        token, queries, keys, values, out_grad, gain, log_decay
    )

    def beside_forward(token, i):
        s = waves[i]
        (held,) = after(token, log_decay)
        local = call(
            bind(local_kernel, s),
            [shape(tokens, s.columns), shape(s.blocks * s.heads * C, C, BF16)],
            queries,
            keys,
            values,
            held,
            states[i][3],
            gain,
            flops=2 * unit,
        )
        return local[0], local

    parts = [(state[0], state[1], state[2], None) for state in states]
    entries, local, token, _ = scan_in(waves, parts, False, token, beside_forward)
    attentions, sums = [], []
    for i, s in enumerate(waves):
        attention, total = call(
            bind(attention_kernel, s),
            [shape(tokens, s.columns), shape(8, tokens)],
            queries,
            out_grad,
            gain,
            states[i][3],
            states[i][2],
            local[i][0],
            states[i][4],
            *entries[i],
            *sums,
            flops=2 * unit,
        )
        token = attention
        attentions.append(attention)
        sums = [total]
    if dp & (dp - 1):
        sums = [lax.psum(sums[0], "dp")]
    else:
        bit = 1
        while bit < dp:
            total = sum(sums[1:], sums[0])
            sums = [total, swap(total, "dp", bit)]
            bit *= 2
    grads = []
    for i, s in enumerate(waves):
        grad = call(
            bind(grad_kernel, s, features * dp),
            [
                shape(tokens, s.columns, BF16),
                shape(s.heads * s.half, s.width),
                shape(s.heads * s.half + s.tail + s.gains, s.width),
                shape(s.tail, s.width),
                shape(s.gains, s.width),
                shape(max(1, s.blocks - 1) * s.heads * s.width, s.width),
            ],
            queries,
            out_grad,
            gain,
            states[i][3],
            states[i][2],
            attentions[i],
            *sums,
            flops=unit,
            deps=[token] if grads else [],
        )
        token = grad[0]
        grads.append(grad)

    def beside_backward(token, i):
        s = waves[i]
        (held,) = after(token, log_decay)
        local_grad = call(
            bind(local_grad_kernel, s),
            [shape(tokens, s.columns), shape(tokens, s.columns)],
            queries,
            values,
            held,
            states[i][3],
            local[i][1],
            grads[i][0],
            flops=3 * unit,
        )
        return local_grad[0], local_grad

    parts = [(grad[1], grad[2], grad[3], grad[4]) for grad in grads]
    entries, local_grads, token, gains = scan_in(waves, parts, True, token, beside_backward)
    done = []
    for i, s in enumerate(waves):
        last = s is waves[-1]
        (held,) = after(token, log_decay)
        given = [
            keys, values, states[i][3], states[i][2], *local_grads[i], grads[i][5], *entries[i], *done,
        ]
        scratch = []
        if last:
            given += gains
            outs = [pltpu.HBM((tokens, features), BF16)] * 2 + [pltpu.HBM((features,), F32)]
            out_spaces = [pltpu.HBM] * 3
            scratch = [
                pltpu.VMEM((features,), F32),
                pltpu.SemaphoreType.DMA((3, len(s.groups(STORED)) + i)),
                pltpu.VMEM((tokens, s.columns), BF16),
                pltpu.VMEM((tokens, s.columns), BF16),
            ]
        else:
            outs = [shape(tokens, s.columns, BF16)] * 2
            out_spaces = [pltpu.VMEM] * 2
        made = call(
            bind(final_kernel, s, waves),
            outs,
            *given,
            flops=4 * unit,
            out_spaces=out_spaces,
            scratch=scratch,
        )
        token = made[0]
        done += made
    return tuple(done[-3:])


def solution(mesh):
    placed = (
        P("seq", "dp"),
        P("seq", "dp"),
        P("seq", "dp"),
        P("seq", "dp"),
        P("seq", "dp"),
        P("dp"),
        P("seq"),
    )
    return jax.shard_map(
        per_device,
        mesh=mesh,
        in_specs=placed,
        out_specs=(P("seq", "dp"), P("seq", "dp"), P("dp")),
        check_vma=False,
    )
```

```python
import functools
import math

import jax
import jax.numpy as jnp
from jax import lax
from jax.experimental import pallas as pl
from jax.experimental.pallas import tpu as pltpu
from jax.sharding import PartitionSpec as P

C = 128
EPSILON = 1e-06
PLANE = 4
SECOND_WAVE = 0.5
LOADED, STORED = 6, 3
F32 = jnp.float32
BF16 = jnp.bfloat16


def dot(a, b, contract_a, contract_b):
    return lax.dot_general(
        a,
        b,
        (((contract_a,), (contract_b,)), ((), ())),
        preferred_element_type=F32,
    )


def two_parts(a):
    high = a.astype(BF16)
    return high, (a - high.astype(F32)).astype(BF16)


def far_dot(a, state, contract_state):
    parts = jnp.concatenate(two_parts(state), axis=contract_state)
    return dot(jnp.concatenate([a, a], axis=1), parts, 1, contract_state)


def equal(a, b):
    return (a == b).astype(F32)


def place_bits(count, reverse):
    place = lax.axis_index("seq")
    place = count - 1 - place if reverse else place
    return lax.rem(place, 2), lax.rem(place // 2, 2), place // PLANE


def triangle():
    row = lax.broadcasted_iota(jnp.int32, (C, C), 0)
    column = lax.broadcasted_iota(jnp.int32, (C, C), 1)
    return row, column


def sums_of(log_block, chosen, contract, log_first):
    parts, left = [], log_block
    for _ in range(3):
        parts.append(left.astype(BF16))
        left = left - parts[-1].astype(F32)
    chosen = chosen.astype(BF16)
    total = None
    for some in (parts[2:], parts[:2]):
        logs = jnp.concatenate(some, axis=1)
        which = jnp.concatenate([chosen] * len(some), axis=contract)
        if log_first:
            one = dot(logs, which, 1, contract)
        else:
            one = dot(which, logs, contract, 1)
        total = one if total is None else total + one
    return total


def decay_columns(log_block):
    row, column = triangle()
    return sums_of(log_block, (row >= column).astype(F32), 1, False)


def decay_rows(log_block):
    row, column = triangle()
    return sums_of(log_block, (row <= column).astype(F32), 0, True)


def total_rows(log_block):
    return sums_of(log_block, jnp.ones((C, C), F32), 0, True)


class Sizes:
    def __init__(self, tokens, features, all_heads, count, wave, first, heads):
        self.tokens, self.features, self.count = tokens, features, count
        self.heads, self.first, self.wave = heads, first, wave
        self.blocks = tokens // C
        self.width = features // all_heads
        self.half = self.width // 2
        self.quarter = self.width // 4
        self.columns = self.heads * self.width
        self.planes = count // PLANE
        longest = self.blocks * count // 2
        per_plane = self.blocks * PLANE
        self.window = max(1, min(self.planes - 1, 1 + (longest - 2) // per_plane))
        self.gains = -(-self.heads // 8) * 8
        self.tail = -(-(self.heads + 2) // 8) * 8
        self.start, self.end = self.heads, self.heads + 1
        self.factors = self.heads + 2 + self.blocks
        self.notes = -(-(self.factors + self.blocks * self.heads) // 8) * 8

    def own(self, h):
        return slice(h * self.width, (h + 1) * self.width)

    def head(self, h):
        return self.own(self.first + h)

    def block(self, j):
        return slice(j * C, (j + 1) * C)

    def rows(self, h, size):
        return slice(h * size, (h + 1) * size)

    def groups(self, most):
        edges = [*range(0, self.heads, most), self.heads]
        return [(a, b, pl.ds(a * self.width, (b - a) * self.width),
                 pl.ds((self.first + a) * self.width, (b - a) * self.width))
                for a, b in zip(edges[:-1], edges[1:])]

    def carry(self, j):
        return slice(self.heads + 2 + j, self.heads + 3 + j)

    def factor(self, j, h):
        row = self.factors + j * self.heads + h
        return slice(row, row + 1)

    def logs(self, log_decay):
        return [
            log_decay[self.first : self.first + self.heads, self.block(j)]
            for j in range(self.blocks)
        ]


def call(kernel, outs, *args, flops=0, spaces=None, out_spaces=None, scratch=(), deps=()):
    moved = sum(math.prod(a.shape) * a.dtype.itemsize for a in (*args, *outs))
    spaces = spaces or [pltpu.VMEM] * len(args)
    out_spaces = out_spaces or [pltpu.VMEM] * len(outs)
    given = len(args)
    return pl.pallas_call(
        lambda *refs: kernel(*refs[:given], *refs[given + len(deps) :]),
        out_shape=outs,
        in_specs=[pl.BlockSpec(memory_space=p) for p in spaces + [pl.ANY] * len(deps)],
        out_specs=[pl.BlockSpec(memory_space=p) for p in out_spaces],
        compiler_params=pltpu.CompilerParams(vmem_limit_bytes=moved + (4 << 20)),
        cost_estimate=pl.CostEstimate(flops=flops, bytes_accessed=moved, transcendentals=0),
        scratch_shapes=scratch,
    )(*args, *deps)


def after(token, *values):
    return lax.optimization_barrier((token,) + values)[1:]


def shape(rows, columns, dtype=F32):
    return jax.ShapeDtypeStruct((rows, columns), dtype)


def put_tail(s, tail_ref, base, factors, start, end):
    tail_ref[base : base + s.heads, :] = factors
    tail_ref[base + s.start : base + s.start + 1, :] = start
    tail_ref[base + s.end : base + s.end + 1, :] = end


def put_parts(first, size, h, whole, keep_ref, send_ref):
    low, high = whole[:size], whole[size:]
    rows = slice(h * size, (h + 1) * size)
    keep_ref[rows, :] = lax.select(first, low, high)
    send_ref[rows, :] = lax.select(first, high, low)


def state_kernel(
    s, told, keys, values, log_decay, doc_ids, keep, send, notes, cums, first_update, *near
):
    waits, first = {}, s.first
    if near:
        near_keys, near_values, near_logs, near_ids, arrived, small = near
        ids_copy = pltpu.make_async_copy(doc_ids, near_ids, small.at[0])
        logs_copy = pltpu.make_async_copy(log_decay, near_logs, small.at[1])
        for g, (a, _, part, far_part) in enumerate(s.groups(LOADED)):
            waits[a] = [
                pltpu.make_async_copy(far.at[:, far_part], close.at[:, part], arrived.at[i, g])
                for i, (far, close) in enumerate([(keys, near_keys), (values, near_values)])
            ]
        for copy in [logs_copy, ids_copy] + sum(waits.values(), []):
            copy.start()
        logs_copy.wait()
        keys, values, log_decay, doc_ids, first = near_keys, near_values, near_logs, near_ids, 0
    core, _, _ = place_bits(s.count, False)
    lower = core == 0
    logs = s.logs(log_decay)
    totals = [total_rows(a) for a in logs]
    factors = [jnp.exp(t) for t in totals]
    columns = [decay_columns(a) for a in logs]
    ends = [jnp.exp(a[C - 1 : C, :] - a) for a in columns]
    for j, column in enumerate(columns):
        cums[s.block(j), :] = column
    if near:
        ids_copy.wait()
        docs = [jnp.full((1, s.width), doc_ids[j].astype(F32)) for j in range(s.blocks)]
        carries = [None] + [equal(docs[j - 1], docs[j]) for j in range(1, s.blocks)]
    else:
        docs = [doc_ids[told.start : told.start + 1, :], doc_ids[told.end : told.end + 1, :]]
        carries = [doc_ids[told.carry(j), :] for j in range(s.blocks)]
    whole_factor = factors[0]
    for j in range(1, s.blocks):
        whole_factor = whole_factor * factors[j] * carries[j]
    base = s.heads * s.half
    send[base:, :] = jnp.zeros((s.tail, s.width), F32)
    put_tail(s, send, base, whole_factor, docs[0], docs[-1])
    notes[...] = jnp.zeros(notes.shape, F32)
    put_tail(s, notes, 0, whole_factor, docs[0], docs[-1])
    for j in range(1, s.blocks):
        notes[s.carry(j), :] = carries[j]
    for j, rows in enumerate(factors):
        notes[s.factor(j, 0).start : s.factor(j, 0).start + s.heads, :] = rows
    for h in range(s.heads):
        for copy in waits.get(h, ()):
            copy.wait()
        place = slice((first + h) * s.width, (first + h + 1) * s.width)
        state = None
        for j in range(s.blocks):
            scaled = keys[s.block(j), place].astype(F32) * ends[j][:, h : h + 1]
            update = dot(scaled.astype(BF16), values[s.block(j), place], 0, 0)
            if j < s.blocks - 1:
                first_update[s.rows(j * s.heads + h, s.width), :] = update
            if state is None:
                state = update
            else:
                state = (carries[j] * factors[j][h : h + 1, :]) * state + update
        put_parts(lower, s.half, h, state, keep, send)


def sides(first, own, other):
    return lax.select(first, own, other), lax.select(first, other, own)


def linked(s, far, near):
    return equal(far[s.end : s.end + 1, :], near[s.start : s.start + 1, :])


def join_tail(s, out, base, far, near, factor):
    out[base : base + s.tail, :] = jnp.zeros((s.tail, s.width), F32)
    put_tail(
        s,
        out,
        base,
        far[: s.heads, :] * factor,
        far[s.start : s.start + 1, :],
        near[s.end : s.end + 1, :],
    )


def chip_kernel(s, reverse, keep, received, own_tail, *rest):
    out_keep, out_send = rest[-3:-1] if reverse else rest
    core, chip, _ = place_bits(s.count, reverse)
    lower, left = core == 0, chip == 0
    base, top = s.heads * s.half, s.heads * s.quarter
    far, near = sides(lower, own_tail[: s.tail, :], received[base : base + s.tail, :])
    factor = near[: s.heads, :] * linked(s, far, near)
    join_tail(s, out_send, top, far, near, factor)
    if reverse:
        gain = rest[0][...] + received[base + s.tail :, :]
        every = rest[-1]
        if s.wave:
            every[: -s.gains, :] = rest[1][...]
        every[every.shape[0] - s.gains :, :] = gain
    for h in range(s.heads):
        rows = s.rows(h, s.half)
        far_state, near_state = sides(lower, keep[rows, :], received[rows, :])
        total = near_state + factor[h : h + 1, :] * far_state
        put_parts(left, s.quarter, h, total, out_keep, out_send)


def plane_kernel(s, reverse, keep, sent, received, *rest):
    columns, out = rest[:-1], rest[-1]
    _, chip, _ = place_bits(s.count, reverse)
    left = chip == 0
    top = s.heads * s.quarter
    far, near = sides(left, sent[top:, :], received[top:, :])
    factor = near[: s.heads, :] * linked(s, far, near)
    join_tail(s, out, top, far, near, factor)
    if columns:
        out[top + s.tail :, :] = sum([a[...] for a in columns[1:]], columns[0][...])
    for h in range(s.heads):
        rows = s.rows(h, s.quarter)
        far_state, near_state = sides(left, keep[rows, :], received[rows, :])
        out[rows, :] = near_state + factor[h : h + 1, :] * far_state


def spread_kernel(s, reverse, keep, sent, received, *rest):
    earlier, rest = rest[: s.window], rest[s.window :]
    out_keep, out_send = rest[1:3] if rest[2:] else rest
    _, chip, plane = place_bits(s.count, reverse)
    left = chip == 0
    top = s.heads * s.quarter
    far, near = sides(left, sent[top:, :], received[top:, :])
    tails = [ref[top : top + s.tail, :] for ref in earlier]
    reach = [(plane >= w + 1).astype(F32) for w in range(s.window)]
    entry = linked(s, tails[0], far) * reach[0]
    inner = [
        linked(s, tails[w + 1], tails[w]) * reach[w + 1] * tails[w][: s.heads, :]
        for w in range(s.window - 1)
    ]
    link = linked(s, far, near)
    far_factor = far[: s.heads, :]
    if rest[2:]:
        gain = rest[0][top + s.tail :, :]
        if s.planes > 1:
            gain = gain + earlier[0][top + s.tail :, :]
        rest[3][...] = gain
        out_send[top:, :] = gain
    for h in range(s.heads):
        rows, one = s.rows(h, s.quarter), slice(h, h + 1)
        state = earlier[-1][rows, :]
        for w in reversed(range(s.window - 1)):
            state = earlier[w][rows, :] + inner[w][one] * state
        into_far = entry * state
        far_state = lax.select(left, keep[rows, :], received[rows, :])
        into_near = link * (far_state + far_factor[one] * into_far)
        out_keep[rows, :] = lax.select(left, into_far, into_near)
        out_send[rows, :] = lax.select(left, into_near, into_far)


def entry_kernel(
    s, reverse, chip_keep, chip_received, keep, received, own_tail, out_keep, out_send
):
    core, chip, _ = place_bits(s.count, reverse)
    lower, left = core == 0, chip == 0
    base = s.heads * s.half
    far, near = sides(lower, own_tail[: s.tail, :], received[base : base + s.tail, :])
    link = linked(s, far, near)
    far_factor = far[: s.heads, :]
    for h in range(s.heads):
        rows, quarter = s.rows(h, s.half), s.rows(h, s.quarter)
        into_far = jnp.concatenate(
            sides(left, chip_keep[quarter, :], chip_received[quarter, :]), axis=0
        )
        far_state = lax.select(lower, keep[rows, :], received[rows, :])
        into_near = link * (far_state + far_factor[h : h + 1, :] * into_far)
        out_keep[rows, :] = lax.select(lower, into_far, into_near)
        out_send[rows, :] = lax.select(lower, into_near, into_far)


def joined(s, lower, keep, received, h):
    rows = s.rows(h, s.half)
    return jnp.concatenate(sides(lower, keep[rows, :], received[rows, :]), axis=0)


def decay_mask(column, row):
    at, other = triangle()
    gap = jnp.minimum(column - row, 0.0)
    return jnp.where(at >= other, jnp.exp(gap), 0.0)


def local_kernel(s, queries, keys, values, log_decay, cums, gain, out, weights):
    for j, logs in enumerate(s.logs(log_decay)):
        columns, rows = cums[s.block(j), :], decay_rows(logs)
        for h in range(s.heads):
            mask = decay_mask(columns[:, h : h + 1], rows[h : h + 1, :])
            part = (s.block(j), s.head(h))
            scores = dot(queries[part], keys[part], 1, 1)
            weight = (scores * mask).astype(BF16)
            weights[s.rows(j * s.heads + h, C), :] = weight
            out[s.block(j), s.own(h)] = dot(weight, values[part], 1, 0)


def attention_kernel(
    s, queries, out_grad, gain, cums, notes, local, first_update, keep, received, *rest
):
    earlier_sums, (out, sums) = rest[:-2], rest[-2:]
    core, _, _ = place_bits(s.count, False)
    lower = core == 0
    decays = [jnp.exp(cums[s.block(j), :]) for j in range(s.blocks)]
    squares = [jnp.zeros((C, s.width), F32) for _ in decays]
    inners = [jnp.zeros((C, s.width), F32) for _ in decays]
    for h in range(s.heads):
        state = joined(s, lower, keep, received, h)
        for j in range(s.blocks):
            part, own = (s.block(j), s.head(h)), (s.block(j), s.own(h))
            far = far_dot(queries[part], state, 0)
            attention = local[own] + decays[j][:, h : h + 1] * far
            out[own] = attention
            squares[j] = squares[j] + attention * attention
            inners[j] = inners[j] + out_grad[part].astype(F32) * gain[s.head(h)].reshape(1, s.width) * attention
            if j < s.blocks - 1:
                update = first_update[s.rows(j * s.heads + h, s.width), :]
                state = notes[s.carry(j + 1), :] * (notes[s.factor(j, h), :] * state + update)
    if earlier_sums:
        sums[...] = earlier_sums[0][...]
    else:
        sums[...] = jnp.zeros(sums.shape, F32)
    for j in range(s.blocks):
        for i, part in enumerate([squares[j], inners[j]]):
            row = (slice(i, i + 1), s.block(j))
            sums[row] = sums[row] + jnp.sum(part.T, axis=0, keepdims=True)


def grad_kernel(
    s, all_features, queries, out_grad, gain, cums, notes, attention, *rest
):
    sums, (attn_grad, keep, send, out_tail, out_gain, back_terms) = rest[:-6], rest[-6:]
    core, _, _ = place_bits(s.count, True)
    lower = core == 0
    decays = [jnp.exp(cums[s.block(j), :]) for j in range(s.blocks)]
    totals = sum([a[...] for a in sums[1:]], sums[0][...]) / all_features
    spread = lambda row: jnp.broadcast_to(row, (C, C)).T
    inverses, slopes = [], []
    for j in range(s.blocks):
        inverse = lax.rsqrt(totals[0:1, s.block(j)] + EPSILON)
        inverses.append(spread(inverse))
        slopes.append(spread(totals[1:2, s.block(j)] * inverse * inverse))
    base = s.heads * s.half
    out_tail[...] = jnp.zeros(out_tail.shape, F32)
    own = notes[: s.tail, :]
    put_tail(
        s, out_tail, 0, own[: s.heads], own[s.end : s.end + 1], own[s.start : s.start + 1]
    )
    out_gain[...] = jnp.zeros(out_gain.shape, F32)
    for h in range(s.heads):
        gain_row = gain[s.head(h)].reshape(1, s.width)
        gain_part = jnp.zeros((1, s.width), F32)
        terms = []
        for j in range(s.blocks):
            part, own = (s.block(j), s.head(h)), (s.block(j), s.own(h))
            cot = out_grad[part].astype(F32)
            att = attention[own]
            grad = ((cot * gain_row - att * slopes[j]) * inverses[j]).astype(BF16)
            attn_grad[own] = grad
            gain_part = gain_part + jnp.sum(cot * att * inverses[j], axis=0, keepdims=True)
            weighted = (queries[part].astype(F32) * decays[j][:, h : h + 1]).astype(BF16)
            term = dot(weighted, grad, 0, 0)
            terms.append(term)
            if j > 0:
                back_terms[s.rows((j - 1) * s.heads + h, s.width), :] = term
        state = terms[-1]
        for j in reversed(range(s.blocks - 1)):
            state = terms[j] + (notes[s.carry(j + 1), :] * notes[s.factor(j, h), :]) * state
        put_parts(lower, s.half, h, state, keep, send)
        out_gain[h : h + 1, :] = gain_part
    send[base : base + s.tail, :] = out_tail[...]
    send[base + s.tail :, :] = out_gain[...]


def local_grad_kernel(
    s, queries, values, log_decay, cums, weights, attn_grad, key_out, value_out
):
    for j, logs in enumerate(s.logs(log_decay)):
        columns, rows = cums[s.block(j), :], decay_rows(logs)
        for h in range(s.heads):
            mask = decay_mask(columns[:, h : h + 1], rows[h : h + 1, :])
            part, own = (s.block(j), s.head(h)), (s.block(j), s.own(h))
            grad = attn_grad[own]
            grad_weight = (dot(grad, values[part], 1, 1) * mask).astype(BF16)
            key_out[own] = dot(grad_weight, queries[part], 0, 0)
            value_out[own] = dot(weights[s.rows(j * s.heads + h, C), :], grad, 0, 0)


def final_kernel(s, waves, keys, values, cums, notes, key_local, value_local, back_terms, *rest):
    keep, received = rest[:2]
    last = s is waves[-1]
    near_outs = rest[-2:]
    copies, groups = [], []
    if last:
        *far_outs, far_gain, near_gain, sent = rest[-7:-2]
        groups = s.groups(STORED)
        own, other = rest[2 + 2 * s.wave : 4 + 2 * s.wave]
        base = waves[0].heads * s.quarter
        for wave in waves:
            for h in range(wave.heads):
                row = wave.wave * s.gains + h
                total = own[row : row + 1, :] + other[base + row : base + row + 1, :]
                near_gain[wave.head(h)] = total.reshape(s.width)
        copies.append(pltpu.make_async_copy(near_gain, far_gain, sent.at[2, 0]))
        copies[-1].start()
        for w, wave in enumerate(waves[:-1]):
            place = pl.ds(wave.first * s.width, wave.columns)
            for i, far in enumerate(far_outs):
                near = rest[2 + 2 * w + i]
                copies.append(
                    pltpu.make_async_copy(near, far.at[:, place], sent.at[i, len(groups) + w])
                )
                copies[-1].start()
    core, _, _ = place_bits(s.count, True)
    lower = core == 0
    columns = [cums[s.block(j), :] for j in range(s.blocks)]
    ends = [jnp.exp(a[C - 1 : C, :] - a) for a in columns]
    for h in range(s.heads):
        state = joined(s, lower, keep, received, h)
        for j in reversed(range(s.blocks)):
            part, own = (s.block(j), s.head(h)), (s.block(j), s.own(h))
            end = ends[j][:, h : h + 1]
            key_far = end * far_dot(values[part], state, 1)
            value_far = end * far_dot(keys[part], state, 0)
            near_outs[0][own] = (key_local[own] + key_far).astype(BF16)
            near_outs[1][own] = (value_local[own] + value_far).astype(BF16)
            if j > 0:
                term = back_terms[s.rows((j - 1) * s.heads + h, s.width), :]
                state = notes[s.carry(j), :] * (term + notes[s.factor(j, h), :] * state)
        for g, (_, stop, part, far_part) in enumerate(groups):
            if h + 1 != stop:
                continue
            for i, (near, far) in enumerate(zip(near_outs, far_outs)):
                copies.append(
                    pltpu.make_async_copy(near.at[:, part], far.at[:, far_part], sent.at[i, g])
                )
                copies[-1].start()
    for copy in copies:
        copy.wait()


def swap(value, axis, bit):
    count = lax.axis_size(axis)
    return lax.ppermute(value, axis, [(i, i ^ bit) for i in range(count)])


def next_plane(value, count, reverse):
    step = -PLANE if reverse else PLANE
    pairs = [(i, i + step) if 0 <= i + step < count else (i, (i + step) % count ^ 1) for i in range(count)]
    return lax.ppermute(value, "seq", pairs)


def pass_on(value, count, reverse, behind):
    planes = count // PLANE
    pairs = []
    for source in range(count):
        plane, place = divmod(source, PLANE)
        if plane < behind:
            target = source ^ 1
        else:
            target = (plane + 1 if plane < planes - 1 else behind) * PLANE + place
        pair = (source, target)
        pairs.append(tuple(count - 1 - a for a in pair) if reverse else pair)
    return lax.ppermute(value, "seq", pairs)


def scan_in(waves, parts, reverse, token, beside):
    bind = functools.partial
    gain_rows = lambda s: len(waves) * s.gains if reverse and s.wave == 0 else 0
    received, chips, chip_received, local, gains, others = [], [], [], [], [], []
    for s, (keep, send, tail, gain) in zip(waves, parts):
        received.append(swap(send, "seq", 1))
    for i, (s, (keep, send, tail, gain)) in enumerate(zip(waves, parts)):
        outs = [
            shape(s.heads * s.quarter, s.width),
            shape(s.heads * s.quarter + s.tail, s.width),
        ]
        (keep,) = after(token, keep)
        extra = []
        if reverse:
            extra = [gain, *gains]
            outs.append(shape((i + 1) * s.gains, s.width))
        *chip, = call(bind(chip_kernel, s, reverse), outs, keep, received[i], tail, *extra)
        gains = chip[2:]
        token = chip[0]
        chips.append(chip)
        chip_received.append(swap(chip[1], "seq", 2))
    if reverse:
        bit = waves[0].count // 2
        while bit > PLANE:
            if others:
                gains, others = [gains[0] + others[0]], []
            others = [swap(gains[0], "seq", bit + 1)]
            bit //= 2
    planes, passed = [], []
    for i in range(len(waves) - 1):
        token, one = beside(token, i)
        local.append(one)
    for i, s in enumerate(waves):
        (keep,) = after(token, chips[i][0])
        outs = [shape(s.heads * s.quarter + s.tail + gain_rows(s), s.width)]
        columns = gains + others if gain_rows(s) else []
        (plane,) = call(
            bind(plane_kernel, s, reverse),
            outs,
            keep,
            chips[i][1],
            chip_received[i],
            *columns,
            deps=planes[-1:],
        )
        token = plane
        planes.append(plane)
        passed.append([next_plane(plane, s.count, reverse)])
    for i in range(len(local), len(waves)):
        token, one = beside(token, i)
        local.append(one)
    passed = [list(after(token, one[0])) for one in passed]
    for w in range(1, waves[0].window):
        for i, s in enumerate(waves):
            passed[i].append(pass_on(passed[i][-1], s.count, reverse, w))
    spreads, spread_received = [], []
    for i, s in enumerate(waves):
        (keep,) = after(token, chips[i][0])
        outs = [
            shape(s.heads * s.quarter, s.width),
            shape(s.heads * s.quarter + gain_rows(s), s.width),
        ]
        extra = []
        if gain_rows(s):
            outs.append(shape(gain_rows(s), s.width))
            extra = [planes[i]]
        spread = call(
            bind(spread_kernel, s, reverse),
            outs,
            keep,
            chips[i][1],
            chip_received[i],
            *passed[i],
            *extra,
        )
        token = spread[0]
        spreads.append(spread)
        spread_received.append(swap(spread[1], "seq", 2))
    entries = []
    for i, s in enumerate(waves):
        (keep,) = after(token, spreads[i][0])
        entry = call(
            bind(entry_kernel, s, reverse),
            [shape(s.heads * s.half, s.width)] * 2,
            keep,
            spread_received[i],
            parts[i][0],
            received[i],
            parts[i][2],
        )
        token = entry[0]
        entries.append((entry[0], swap(entry[1], "seq", 1)))
    return entries, local, token, [spreads[0][-1], spread_received[0]]


def per_device(queries, keys, values, out_grad, log_decay, norm_gain, doc_ids):
    tokens, features = queries.shape
    heads = log_decay.shape[1]
    count, dp = lax.axis_size("seq"), lax.axis_size("dp")
    second = round(heads * SECOND_WAVE) if heads > 4 else 0
    split = [(0, heads - second), (heads - second, second)][: 2 if second else 1]
    waves = [Sizes(tokens, features, heads, count, w, *part) for w, part in enumerate(split)]
    bind = functools.partial
    unit = 2 * C * C * C * waves[0].blocks * waves[0].heads
    gain = norm_gain
    log_decay = log_decay.T
    states = []
    far = [pltpu.with_memory_space_constraint(a, pltpu.HBM) for a in (keys, values, log_decay, doc_ids)]
    for s in waves:
        given = (keys, values, log_decay, doc_ids)
        spaces = [pltpu.VMEM] * 4
        scratch = []
        if not states:
            given, spaces = far, [pltpu.HBM] * 4
            scratch = [
                pltpu.VMEM((tokens, s.columns), BF16),
                pltpu.VMEM((tokens, s.columns), BF16),
                pltpu.VMEM(log_decay.shape, F32),
                pltpu.SMEM(doc_ids.shape, jnp.int32),
                pltpu.SemaphoreType.DMA((2, len(s.groups(LOADED)))),
                pltpu.SemaphoreType.DMA((2,)),
            ]
        else:
            given = (keys, values, log_decay, states[0][2])
        state = call(
            bind(state_kernel, s, waves[0]),
            [
                shape(s.heads * s.half, s.width),
                shape(s.heads * s.half + s.tail, s.width),
                shape(s.notes, s.width),
                shape(tokens, s.heads),
                shape(max(1, s.blocks - 1) * s.heads * s.width, s.width),
            ],
            *given,
            flops=unit,
            spaces=spaces,
            scratch=scratch,
        )
        token = state[0]
        states.append(state)
    queries, keys, values, out_grad, gain, log_decay = after(
        token, queries, keys, values, out_grad, gain, log_decay
    )

    def beside_forward(token, i):
        s = waves[i]
        (held,) = after(token, log_decay)
        local = call(
            bind(local_kernel, s),
            [shape(tokens, s.columns), shape(s.blocks * s.heads * C, C, BF16)],
            queries,
            keys,
            values,
            held,
            states[i][3],
            gain,
            flops=2 * unit,
        )
        return local[0], local

    parts = [(state[0], state[1], state[2], None) for state in states]
    entries, local, token, _ = scan_in(waves, parts, False, token, beside_forward)
    attentions, sums = [], []
    for i, s in enumerate(waves):
        attention, total = call(
            bind(attention_kernel, s),
            [shape(tokens, s.columns), shape(8, tokens)],
            queries,
            out_grad,
            gain,
            states[i][3],
            states[i][2],
            local[i][0],
            states[i][4],
            *entries[i],
            *sums,
            flops=2 * unit,
        )
        token = attention
        attentions.append(attention)
        sums = [total]
    if dp & (dp - 1):
        sums = [lax.psum(sums[0], "dp")]
    else:
        bit = 1
        while bit < dp:
            total = sum(sums[1:], sums[0])
            sums = [total, swap(total, "dp", bit)]
            bit *= 2
    grads = []
    for i, s in enumerate(waves):
        grad = call(
            bind(grad_kernel, s, features * dp),
            [
                shape(tokens, s.columns, BF16),
                shape(s.heads * s.half, s.width),
                shape(s.heads * s.half + s.tail + s.gains, s.width),
                shape(s.tail, s.width),
                shape(s.gains, s.width),
                shape(max(1, s.blocks - 1) * s.heads * s.width, s.width),
            ],
            queries,
            out_grad,
            gain,
            states[i][3],
            states[i][2],
            attentions[i],
            *sums,
            flops=unit,
            deps=[token] if grads else [],
        )
        token = grad[0]
        grads.append(grad)

    def beside_backward(token, i):
        s = waves[i]
        (held,) = after(token, log_decay)
        local_grad = call(
            bind(local_grad_kernel, s),
            [shape(tokens, s.columns), shape(tokens, s.columns)],
            queries,
            values,
            held,
            states[i][3],
            local[i][1],
            grads[i][0],
            flops=3 * unit,
        )
        return local_grad[0], local_grad

    parts = [(grad[1], grad[2], grad[3], grad[4]) for grad in grads]
    entries, local_grads, token, gains = scan_in(waves, parts, True, token, beside_backward)
    done = []
    for i, s in enumerate(waves):
        last = s is waves[-1]
        (held,) = after(token, log_decay)
        given = [
            keys, values, states[i][3], states[i][2], *local_grads[i], grads[i][5], *entries[i], *done,
        ]
        scratch = []
        if last:
            given += gains
            outs = [pltpu.HBM((tokens, features), BF16)] * 2 + [pltpu.HBM((features,), F32)]
            out_spaces = [pltpu.HBM] * 3
            scratch = [
                pltpu.VMEM((features,), F32),
                pltpu.SemaphoreType.DMA((3, len(s.groups(STORED)) + i)),
                pltpu.VMEM((tokens, s.columns), BF16),
                pltpu.VMEM((tokens, s.columns), BF16),
            ]
        else:
            outs = [shape(tokens, s.columns, BF16)] * 2
            out_spaces = [pltpu.VMEM] * 2
        made = call(
            bind(final_kernel, s, waves),
            outs,
            *given,
            flops=4 * unit,
            out_spaces=out_spaces,
            scratch=scratch,
        )
        token = made[0]
        done += made
    return tuple(done[-3:])


def solution(mesh):
    placed = (
        P("seq", "dp"),
        P("seq", "dp"),
        P("seq", "dp"),
        P("seq", "dp"),
        P("seq", "dp"),
        P("dp"),
        P("seq"),
    )
    return jax.shard_map(
        per_device,
        mesh=mesh,
        in_specs=placed,
        out_specs=(P("seq", "dp"), P("seq", "dp"), P("dp")),
        check_vma=False,
    )
```
